32 devices in a mesh: pipe: 4 (over y, core), expert: 8 (over z, x).
Axes of the slice: x: 2, y: 2, z: 4, core: 2. Of those that a mesh axis runs over, the one named last changes fastest.
Arguments:
- grad_sent: bfloat16 [4, 1024, 2048], P('pipe', 'expert'), may hold values from -6 to 6
- routes: int32 [4, 1024, 2], P('pipe', 'expert'), may hold values from 0 to 7, all different within a row; in each aligned block of 64 rows (0 to 63, 64 to 127, ..., all dimensions but the last counted through in order) at most 24 rows name the same one
- router_probs: float32 [4, 1024, 8], P('pipe', 'expert'), may hold values from 0.025 to 0.625
- saved_hidden: bfloat16 [4, 3072, 768], P('pipe', 'expert'), may hold values from -6 to 6
- w_down: bfloat16 [8, 768, 2048], P('expert'), may hold values from -0.21875 to 0.21875
- w_router: bfloat16 [2048, 8], replicated, may hold values from -0.125 to 0.125
Outputs:
- d_hidden: bfloat16 [4, 3072, 768], P('pipe', 'expert')
- grad_router_in: bfloat16 [4, 1024, 2048], P('pipe', 'expert')
The draws below stay inside these ranges and needn't reach their ends.
Inputs may be any that keep to these rules, and one draw needn't show every extreme that they name: `routes`: each token names 2 different experts. In each micro-batch of one device (an aligned block of 64 rows) no expert is named by more than 24 tokens, a bound that some block reaches.
All inputs are finite; a program needn't handle non-finite values.
Results may differ from the reference program's by a relative error of at most 0.0046.
Values may be sent and summed in bfloat16 or wider, within the bound.
No kernel may reach another device: no remote copies, remote signals or barrier semaphores. Data moves between devices by JAX's collectives and lax.ppermute only.
A program may use at most 64 MiB of HBM per device.

```python
import math
import jax
import jax.numpy as jnp
import numpy as np
from jax import lax

D = 2048
FF = 768
TOP = 2
MICRO = 2
MB_TOK = 64
SECTIONS = 4
EXPERTS = 8
TOKENS = 1024
CAP = 24
SLOTS = 384


def shard_levels(stream_key, dims, shards, low, largest):
    gain, own = 1.0, jax.random.fold_in(stream_key, 6)
    for axis_at, blocks in shards:
        heights = jnp.exp(jax.random.uniform(jax.random.fold_in(own, axis_at), (blocks,), jnp.float32, low / len(shards), largest / len(shards)))
        gain = gain * jnp.repeat(heights, dims[axis_at] // blocks).reshape([-1 if axis == axis_at else 1 for axis in range(len(dims))])
    return gain


def shared_out(key, own, number, rows, amount, top, reach, lean):
    ranking = jax.random.permutation(key, amount)
    packed, usual = load_shares(amount, rows * top, reach, lean, True), load_shares(amount, rows * top, reach, lean, False)
    places = jnp.arange(amount)

    def named(sizes, turn):
        used = int((sizes > 0).sum())
        fixed = max(1, used // 4)
        shifted = fixed + (places - fixed + turn * (used - fixed)) % max(1, amount - fixed)
        return jnp.zeros((amount,), jnp.int32).at[ranking[jnp.where(places < fixed, places, shifted)]].set(jnp.asarray(sizes, jnp.int32))

    sizes = jnp.where(number % 4 == 0, named(packed, number // 4), named(usual, number - number // 4 - 1))
    mixed = jax.random.permutation(jax.random.fold_in(own, 3), amount)
    source_of, sink = mixed[0:amount // 2 * 2:2], mixed[1:amount // 2 * 2:2]
    slack = jnp.minimum(sizes[source_of] - 1, reach - sizes[sink]) // 2
    slack = jnp.where((source_of == ranking[0]) | (sink == ranking[0]) | (sizes[sink] == 0), 0, jnp.maximum(slack, 0))
    shifted = jax.random.randint(jax.random.fold_in(own, 4), (amount // 2,), 0, 1 << 20) % (slack + 1)
    sizes = sizes.at[source_of].add(-shifted).at[sink].add(shifted)
    items = jnp.searchsorted(jnp.cumsum(sizes), jnp.arange(rows * top), side="right").astype(jnp.int32)
    grid = items.reshape(top, rows).T
    grid = grid[jax.random.permutation(jax.random.fold_in(own, 1), rows)]
    turn = jax.random.randint(jax.random.fold_in(own, 2), (rows, 1), 0, top)
    return jnp.take_along_axis(grid, (jnp.arange(top)[None, :] + turn) % top, axis=1)


def load_shares(amount, total, limit, lean, full):
    loads = [(1 << 20) // math.isqrt(rank ** lean) + 1 for rank in range(1, amount + 1)]
    largest = limit if full else min(limit, max(-(-total // amount), total * loads[0] // sum(loads)))
    least = 1 if total - largest >= amount - 1 else 0
    counts, spare = [largest] + [least] * (amount - 1), total - largest - least * (amount - 1)
    while spare > 0:
        free = [i for i in range(1, amount) if counts[i] < largest] or [i for i in range(1, amount) if counts[i] < limit]
        whole, left = sum([loads[i] for i in free]), spare
        for i in free:
            addition = min(limit - counts[i], max(1, left * loads[i] // whole), spare)
            counts[i] = counts[i] + addition
            spare = spare - addition
    return np.array(counts)


def bell_draw(stream_key, extent, deviation, limit, cuts=(), held_as=jnp.bfloat16):
    loudness = shard_levels(stream_key, extent, cuts, -0.22, 0.18) if cuts else 1.0
    array = jax.random.normal(stream_key, extent, jnp.float32) * deviation * loudness
    return jnp.minimum(jnp.maximum(array, -limit), limit).astype(held_as)


def setup_inputs(seed: int = 0) -> dict:
    key_list = jax.random.split(jax.random.key(seed), 7)
    grad_sent = bell_draw(key_list[0], (SECTIONS, TOKENS, D), 1.0, 6.0, ((0, 4), (1, 8)))
    routes_keys = jax.random.split(jax.random.fold_in(key_list[1], 1), SECTIONS * TOKENS // MB_TOK)
    routes_turns = jax.random.permutation(jax.random.fold_in(key_list[1], 3), SECTIONS * TOKENS // MB_TOK)
    routes = jax.vmap(lambda own, number: shared_out(jax.random.fold_in(key_list[1], 2), own, number, MB_TOK, EXPERTS, TOP, CAP, 2))(routes_keys, routes_turns).reshape((SECTIONS, TOKENS, TOP))
    router_probs = jnp.clip(jnp.exp(math.log(0.625) - 3.218876 * jax.random.uniform(key_list[2], (SECTIONS, TOKENS, EXPERTS), jnp.float32) ** shard_levels(key_list[2], (SECTIONS, TOKENS, EXPERTS), ((0, 4), (1, 8)), -0.2, 0.2)), 0.025, 0.625)
    saved_hidden = bell_draw(key_list[3], (SECTIONS, EXPERTS * SLOTS, FF), 1.0, 6.0, ((0, 4), (1, 8)))
    w_down = bell_draw(key_list[4], (EXPERTS, FF, D), FF ** -0.5, 0.21875, ((0, 8),))
    w_router = bell_draw(key_list[5], (D, EXPERTS), D ** -0.5, 0.125)
    return {"grad_sent": grad_sent, "routes": routes, "router_probs": router_probs, "saved_hidden": saved_hidden, "w_down": w_down, "w_router": w_router}


def reference(grad_sent, routes, router_probs, saved_hidden, w_down, w_router):
    incoming = jnp.roll(grad_sent, -1, axis=0)
    chosen = jnp.take_along_axis(router_probs, routes, axis=2)
    weights = chosen / jnp.sum(chosen, axis=2, keepdims=True)
    rounded = lax.optimization_barrier(weights.astype(jnp.bfloat16)).astype(jnp.float32)
    route_rows = routes.reshape(SECTIONS, EXPERTS, MICRO, MB_TOK * TOP)
    onehot = (route_rows[..., None] == jnp.arange(EXPERTS, dtype=jnp.int32)).astype(jnp.int32)
    rank_of = jnp.sum((jnp.cumsum(onehot, axis=3) - onehot) * onehot, axis=4).astype(jnp.int32)
    source = jnp.arange(EXPERTS, dtype=jnp.int32)[None, :, None, None]
    micro_step = jnp.arange(MICRO, dtype=jnp.int32)[None, None, :, None]
    position = route_rows * SLOTS + (micro_step * EXPERTS + source) * CAP + rank_of
    position = position.reshape(SECTIONS, TOKENS * TOP).astype(jnp.int32)
    weight_slots = rounded.reshape(SECTIONS, TOKENS * TOP)

    def one_section(pack):
        section_grad, slot_rows, slot_scales, held = pack
        spread = jnp.repeat(section_grad, TOP, axis=0)
        buffer = jnp.zeros((EXPERTS * SLOTS, D), jnp.bfloat16).at[slot_rows].set(spread)
        scale_buf = jnp.zeros((EXPERTS * SLOTS,), jnp.float32).at[slot_rows].set(slot_scales)

        def one_expert(inner):
            dy_rows, saved_rows, weight = inner
            grad_hidden = jnp.dot(dy_rows, weight.T, preferred_element_type=jnp.float32)
            route_grad = jnp.sum(grad_hidden * saved_rows.astype(jnp.float32), axis=1)
            return grad_hidden, route_grad

        grad_hidden, route_grad = lax.map(one_expert, (buffer.reshape(EXPERTS, SLOTS, D), held.reshape(EXPERTS, SLOTS, FF), w_down))
        section_hidden = (scale_buf[:, None] * grad_hidden.reshape(EXPERTS * SLOTS, FF)).astype(jnp.bfloat16)
        return section_hidden, route_grad.reshape(EXPERTS * SLOTS)[slot_rows]

    d_hidden, slot_grad = lax.map(one_section, (incoming, position, weight_slots, saved_hidden))
    slot_grad = slot_grad.reshape(SECTIONS, TOKENS, TOP)
    centred = slot_grad - jnp.sum(weights * slot_grad, axis=2, keepdims=True)
    logit_part = weights * centred
    onehot_tok = (routes[..., None] == jnp.arange(EXPERTS, dtype=jnp.int32)).astype(jnp.float32)
    logit_grad = jnp.sum(logit_part[..., None] * onehot_tok, axis=2)
    grad_in = jnp.einsum("ste,de->std", logit_grad, w_router.astype(jnp.float32), precision=lax.Precision.HIGHEST)
    return d_hidden, grad_in.astype(jnp.bfloat16)
```

```python
import functools

import jax
import jax.numpy as jnp
from jax import lax
from jax.experimental import pallas as pl
from jax.experimental.pallas import tpu as pltpu
from jax.sharding import PartitionSpec as P

TOP = 2
MICRO = 2
MB_TOK = 64
LANES = 128
F32, BF16 = jnp.float32, jnp.bfloat16
VMEM_LIMIT = 40 * 1024 * 1024


def iota(shape, axis):
    return lax.broadcasted_iota(jnp.int32, shape, axis)


def info_kernel(routes_ref, probs_ref, info_ref):
    routes = routes_ref[...]
    probs = probs_ref[...]
    expert = iota(probs.shape, 1)
    first, second = routes[:, 0:1], routes[:, 1:2]
    p_first = jnp.sum(jnp.where(expert == first, probs, 0.0), axis=1, keepdims=True)
    p_second = jnp.sum(jnp.where(expert == second, probs, 0.0), axis=1, keepdims=True)
    total = p_first + p_second
    lane = iota((routes.shape[0], LANES), 1)
    table = jnp.where(lane == 0, first.astype(F32), 0.0)
    table = jnp.where(lane == 1, second.astype(F32), table)
    table = jnp.where(lane == 2, p_first / total, table)
    table = jnp.where(lane == 3, p_second / total, table)
    info_ref[...] = table.T[0:8, :]


def ranks(info, expert_rows):
    first, second = info[0:1, :].astype(jnp.int32), info[1:2, :].astype(jnp.int32)
    on_first, on_second = expert_rows == first, expert_rows == second
    named = on_first | on_second
    before = iota((LANES, LANES), 0)
    after = iota((LANES, LANES), 1)
    earlier = ((before < after) & (before // MB_TOK == after // MB_TOK)).astype(F32).astype(BF16)
    rank = jnp.dot(named.astype(F32).astype(BF16), earlier, preferred_element_type=F32)
    rank = jnp.where(named, rank.astype(jnp.int32), -1)
    weight = jnp.where(on_first, info[2:3, :], 0.0) + jnp.where(on_second, info[3:4, :], 0.0)
    return rank, weight.astype(BF16).astype(F32)


def pick(rank_row, weight_row, micro, capacity):
    slot = iota((capacity, LANES), 0)
    token = iota((capacity, LANES), 1)
    hit = (slot == rank_row) & (token // MB_TOK == micro)
    onehot = jnp.where(hit, 1.0, 0.0)
    scale = jnp.sum(jnp.where(hit, weight_row, 0.0), axis=1, keepdims=True)
    return onehot, jnp.broadcast_to(scale, (capacity, LANES))


def pack_kernel(half, capacity, plan, me_ref, *refs):
    n_info = 1 + max(which for which, _ in plan)
    infos, tokens, outs = refs[:n_info], refs[n_info : n_info + len(plan)], refs[n_info + len(plan) :]
    me = me_ref[0]
    rows = jnp.bitwise_xor(me, iota((8, LANES), 0))
    tables = [ranks(info[...], rows) for info in infos]
    at = 0
    for (which, micros), token in zip(plan, tokens):
        rank, weight = tables[which]
        pieces, scales = [], []
        for j in range(half):
            for micro in micros:
                onehot, scale = pick(rank[j : j + 1, :], weight[j : j + 1, :], micro, capacity)
                pieces.append(onehot)
                scales.append(scale)
        width = token.shape[0]
        lead = micros[0] * MB_TOK
        chosen = jnp.concatenate(pieces, axis=0)[:, lead : lead + width].astype(BF16)
        packed = jnp.dot(chosen, token[...], preferred_element_type=F32).astype(BF16)
        size = capacity * len(micros)
        for j in range(half):
            outs[j][at : at + size, 0 : token.shape[1]] = packed[j * size : (j + 1) * size]
            for i in range(len(micros)):
                outs[j][at + i * capacity : at + (i + 1) * capacity, token.shape[1] :] = scales[
                    j * len(micros) + i
                ].astype(BF16)
        at += size


def pack(me, infos, tokens, plan, half, capacity):
    rows = capacity * sum(len(micros) for _, micros in plan)
    width = tokens[0].shape[1]
    block = jax.ShapeDtypeStruct((rows, width + LANES), BF16)
    vmem = pl.BlockSpec(memory_space=pltpu.VMEM)
    return pl.pallas_call(
        functools.partial(pack_kernel, half, capacity, plan),
        out_shape=[block] * half,
        in_specs=[pl.BlockSpec(memory_space=pltpu.SMEM)] + [vmem] * (len(infos) + len(tokens)),
        out_specs=[vmem] * half,
        compiler_params=pltpu.CompilerParams(vmem_limit_bytes=VMEM_LIMIT),
    )(me, *infos, *tokens)


def expert_kernel(half, capacity, plans, me_ref, *refs):
    n_blocks = len(plans) * half
    blocks, (w_ref, saved_ref, d_ref, grad_ref) = refs[:n_blocks], refs[n_blocks : n_blocks + 4]
    lhs, product, scale, partial = refs[n_blocks + 4 :]
    me = me_ref[0]
    peers = 2 * half
    width = w_ref.shape[1]
    step = pl.program_id(0)

    places = []
    at = 0
    for group, plan in enumerate(plans):
        for j in range(half):
            for i, (far, micro) in enumerate(plan):
                source = jnp.bitwise_xor(me, j + (half if far else 0))
                places.append((at, group * half + j, i * capacity, source, micro))
                at += capacity

    @pl.when(step == 0)
    def _():
        partial[...] = jnp.zeros_like(partial)
        start = 0
        for block in blocks:
            lhs[start : start + block.shape[0], :] = block[:, 0:width]
            start += block.shape[0]
        for _, which, row, source, micro in places:
            slot = pl.multiple_of((micro * peers + source) * capacity, 8)
            scale[pl.ds(slot, capacity), :] = blocks[which][row : row + capacity, width:].astype(F32)

    got = lax.dot_general(lhs[...], w_ref[...], (((1,), (1,)), ((), ())), preferred_element_type=F32)
    for begin, _, _, source, micro in places:
        slot = pl.multiple_of((micro * peers + source) * capacity, 8)
        product[pl.ds(slot, capacity), :] = got[begin : begin + capacity, :]
    total = jnp.zeros((product.shape[0], LANES), F32)
    for lane in range(0, product.shape[1], LANES):
        part = product[:, lane : lane + LANES]
        total = total + part * saved_ref[:, lane : lane + LANES].astype(F32)
        d_ref[:, lane : lane + LANES] = (scale[...] * part).astype(BF16)
    for micro in range(MICRO):
        for source in range(peers):
            slot, row = (micro * peers + source) * capacity, source * MB_TOK + micro * (MB_TOK // 2)
            partial[row : row + capacity, :] += total[slot : slot + capacity, :]

    @pl.when(step == pl.num_programs(0) - 1)
    def _():
        for pair in range(peers // 2):
            line = jnp.sum(partial[pair * LANES : (pair + 1) * LANES, :].T, axis=0, keepdims=True)
            grad_ref[2 * pair : 2 * pair + 2, :] = jnp.broadcast_to(line, (2, LANES))


def expert(me, groups, plans, weight, saved, half, capacity):
    slots, hidden_width = saved.shape
    width = weight.shape[1]
    column = 256 if hidden_width % 256 == 0 else hidden_width
    whole = pl.BlockSpec(memory_space=pltpu.VMEM)
    return pl.pallas_call(
        functools.partial(expert_kernel, half, capacity, plans),
        grid=(hidden_width // column,),
        out_shape=[
            jax.ShapeDtypeStruct((slots, hidden_width), BF16),
            jax.ShapeDtypeStruct((2 * half, LANES), F32),
        ],
        in_specs=[pl.BlockSpec(memory_space=pltpu.SMEM)]
        + [whole] * (len(plans) * half)
        + [
            pl.BlockSpec((column, width), lambda i: (i, 0)),
            pl.BlockSpec((slots, column), lambda i: (0, i)),
        ],
        out_specs=[
            pl.BlockSpec((slots, column), lambda i: (0, i)),
            pl.BlockSpec((2 * half, LANES), lambda i: (0, 0)),
        ],
        scratch_shapes=[
            pltpu.VMEM((slots, width), BF16),
            pltpu.VMEM((slots, column), F32),
            pltpu.VMEM((slots, LANES), F32),
            pltpu.VMEM((2 * half * MB_TOK, LANES), F32),
        ],
        compiler_params=pltpu.CompilerParams(vmem_limit_bytes=VMEM_LIMIT),
    )(me, *[block for group in groups for block in group], weight, saved)


def router_kernel(capacity, me_ref, info_ref, grads_ref, router_ref, out_ref):
    me = me_ref[0]
    info = info_ref[...]
    expert_rows = iota((8, LANES), 0)
    rank, _ = ranks(info, expert_rows)
    columns = jnp.concatenate([grads_ref[...], jnp.zeros((LANES - 8, LANES), F32)], axis=0).T
    columns = jnp.where(lax.rem(me, 2) == 0, columns[0:MB_TOK], columns[MB_TOK:])
    slot = iota((capacity, LANES), 0)
    token = iota((capacity, LANES), 1)
    half = MB_TOK // 2
    rows = []
    for e in range(8):
        here = jnp.where(
            token // MB_TOK == 0, columns[0:capacity, e : e + 1], columns[half : half + capacity, e : e + 1]
        )
        rows.append(jnp.sum(jnp.where(slot == rank[e : e + 1, :], here, 0.0), axis=0, keepdims=True))
    grads = jnp.concatenate(rows, axis=0)
    on_first = expert_rows == info[0:1, :].astype(jnp.int32)
    on_second = expert_rows == info[1:2, :].astype(jnp.int32)
    w_first, w_second = info[2:3, :], info[3:4, :]
    g_first = jnp.sum(jnp.where(on_first, grads, 0.0), axis=0, keepdims=True)
    g_second = jnp.sum(jnp.where(on_second, grads, 0.0), axis=0, keepdims=True)
    mean = w_first * g_first + w_second * g_second
    logit = jnp.where(on_first, w_first * (g_first - mean), 0.0)
    logit = logit + jnp.where(on_second, w_second * (g_second - mean), 0.0)
    high = logit.astype(BF16).astype(F32)
    middle = (logit - high).astype(BF16).astype(F32)
    low = logit - high - middle
    parts = jnp.concatenate([high, middle, low, jnp.zeros((LANES - 24, LANES), F32)], axis=0).T
    router = router_ref[...].astype(F32)
    router = jnp.concatenate([router, router, router, jnp.zeros((LANES - 24, router.shape[1]), F32)], axis=0)
    out_ref[...] = jnp.dot(parts.astype(BF16), router.astype(BF16), preferred_element_type=F32).astype(BF16)


def joint(block, flip, back):
    sections, peers = lax.axis_size("pipe"), lax.axis_size("expert")
    route = [
        (p * peers + e, ((p - back) % sections) * peers + (e ^ flip)) for p in range(sections) for e in range(peers)
    ]
    return lax.ppermute(block, ("pipe", "expert"), route)


def by_halves(grad_sent, routes, router_probs, saved_hidden, w_down, w_router):
    peers = lax.axis_size("expert")
    half = peers // 2
    capacity = saved_hidden.shape[1] // (MICRO * peers)
    me = lax.axis_index("expert").astype(jnp.int32).reshape(1)
    tokens = grad_sent[0]
    vmem = pl.BlockSpec(memory_space=pltpu.VMEM)
    far = [joint(tokens[m * MB_TOK : (m + 1) * MB_TOK], half, 1) for m in range(MICRO)]
    own = joint(tokens, 0, 1)
    info = pl.pallas_call(
        info_kernel,
        out_shape=jax.ShapeDtypeStruct((8, LANES), F32),
        in_specs=[vmem, vmem],
        out_specs=vmem,
    )(routes[0], router_probs[0])
    far_info = joint(info, half, 0)
    router = w_router.T
    early = pack(me, [info, far_info], [own, far[0]], ((0, (0, 1)), (1, (0,))), half, capacity)
    early = [early[0]] + [joint(early[j], j, 0) for j in range(1, half)]
    late = pack(me, [far_info], [far[1]], ((0, (1,)),), half, capacity)
    late = [late[0]] + [joint(late[j], j, 0) for j in range(1, half)]
    plans = (((False, 0), (False, 1), (True, 0)), ((True, 1),))
    d_hidden, slot_grad = expert(me, [early, late], plans, w_down[0], saved_hidden[0], half, capacity)
    returned = lax.all_to_all(slot_grad, "expert", split_axis=0, concat_axis=0, tiled=True)
    grad_in = pl.pallas_call(
        functools.partial(router_kernel, capacity),
        out_shape=jax.ShapeDtypeStruct(tokens.shape, BF16),
        in_specs=[pl.BlockSpec(memory_space=pltpu.SMEM), vmem, vmem, vmem],
        out_specs=vmem,
        compiler_params=pltpu.CompilerParams(vmem_limit_bytes=VMEM_LIMIT),
    )(me, info, returned, router)
    return d_hidden[None], grad_in[None]


def from_behind(block, axis, distance):
    devices = range(lax.axis_size(axis))
    route = [((i - distance) % len(devices), i) for i in devices]
    return lax.ppermute(block, axis, route)


def route_slots(route_rows, peer_count, capacity):
    onehot = (route_rows[..., None] == jnp.arange(peer_count, dtype=jnp.int32)).astype(jnp.int32)
    rank_of = jnp.sum((jnp.cumsum(onehot, axis=1) - onehot) * onehot, axis=2)
    return route_rows * capacity + rank_of


def by_slots(grad_sent, routes, router_probs, saved_hidden, w_down, w_router):
    peer_count = lax.axis_size("expert")
    slot_count = saved_hidden.shape[1]
    capacity = slot_count // (MICRO * peer_count)
    send_width = peer_count * capacity
    model_width = grad_sent.shape[2]
    hidden_width = saved_hidden.shape[2]
    tokens = routes.shape[1]
    incoming = from_behind(grad_sent, "pipe", -1)[0]
    route_rows = routes[0].reshape(MICRO, MB_TOK * TOP)
    position = route_slots(route_rows, peer_count, capacity)
    chosen = jnp.take_along_axis(router_probs[0], routes[0], axis=1)
    weights = chosen / jnp.sum(chosen, axis=1, keepdims=True)
    rounded = weights.astype(jnp.bfloat16)
    micro_index = jnp.arange(MICRO, dtype=jnp.int32)[:, None]
    token_index = jnp.broadcast_to(
        jnp.arange(MB_TOK * TOP, dtype=jnp.int32)[None, :] // TOP, (MICRO, MB_TOK * TOP)
    )
    slot_token = (
        jnp.zeros((MICRO, send_width), jnp.int32).at[micro_index, position].set(token_index)
    )
    slot_used = jnp.zeros((MICRO, send_width), jnp.bool_).at[micro_index, position].set(True)
    send_scale = (
        jnp.zeros((MICRO, send_width), jnp.bfloat16)
        .at[micro_index, position]
        .set(rounded.reshape(MICRO, MB_TOK * TOP))
    )
    micro_grad = incoming.reshape(MICRO, MB_TOK, model_width)
    picked = jnp.take_along_axis(micro_grad, slot_token[..., None], axis=1)
    send_rows = jnp.where(slot_used[..., None], picked, jnp.zeros((), jnp.bfloat16))
    hidden = saved_hidden[0].reshape(MICRO, send_width, hidden_width)
    weight = w_down[0]
    arrived, arrived_scale = (
        lax.all_to_all(send_rows, "expert", split_axis=1, concat_axis=1, tiled=True),
        lax.all_to_all(send_scale, "expert", split_axis=1, concat_axis=1, tiled=True),
    )
    flat_rows = arrived.reshape(-1, model_width)
    flat_saved = hidden.reshape(flat_rows.shape[0], hidden_width)
    grad_hidden = lax.dot_general(
        flat_rows, weight, (((1,), (1,)), ((), ())), preferred_element_type=jnp.float32
    )
    route_grad = jnp.sum(grad_hidden * flat_saved.astype(jnp.float32), axis=1)
    scaled = (arrived_scale.reshape(-1, 1).astype(jnp.float32) * grad_hidden).astype(jnp.bfloat16)
    d_hidden, route_grad = (scaled, route_grad.reshape(arrived_scale.shape))
    returned = lax.all_to_all(route_grad, "expert", split_axis=1, concat_axis=1, tiled=True)
    slot_grad = jnp.take_along_axis(returned, position, axis=1).reshape(tokens, TOP)
    centred = slot_grad - jnp.sum(weights * slot_grad, axis=1, keepdims=True)
    logit_part = weights * centred
    onehot_tok = (routes[0][..., None] == jnp.arange(peer_count, dtype=jnp.int32)).astype(
        jnp.float32
    )
    logit_grad = jnp.sum(logit_part[..., None] * onehot_tok, axis=1)
    grad_in = jnp.dot(logit_grad, w_router.astype(jnp.float32).T, precision=lax.Precision.HIGHEST)
    return (d_hidden.reshape(1, slot_count, hidden_width), grad_in.astype(jnp.bfloat16)[None])


def on_device(*blocks):
    peers, slots = lax.axis_size("expert"), blocks[3].shape[1]
    capacity = slots // (MICRO * peers)
    if peers == 8 and capacity % 8 == 0 and capacity <= MB_TOK // 2:
        return by_halves(*blocks)
    return by_slots(*blocks)


def solution(mesh):
    placed = (
        P("pipe", "expert", None),
        P("pipe", "expert", None),
        P("pipe", "expert", None),
        P("pipe", "expert", None),
        P("expert", None, None),
        P(),
    )
    return jax.shard_map(
        on_device,
        mesh=mesh,
        in_specs=placed,
        out_specs=(P("pipe", "expert", None), P("pipe", "expert", None)),
        check_vma=False,
    )
```

```python
import functools

import jax
import jax.numpy as jnp
from jax import lax
from jax.experimental import pallas as pl
from jax.experimental.pallas import tpu as pltpu
from jax.sharding import PartitionSpec as P

TOP = 2
MICRO = 2
MB_TOK = 64
LANES = 128
F32, BF16 = jnp.float32, jnp.bfloat16
VMEM_LIMIT = 16 * 1024 * 1024


def iota(shape, axis):
    return lax.broadcasted_iota(jnp.int32, shape, axis)


def first_kernel(routes_ref, probs_ref, tokens_ref, info_ref, copy_ref):
    probs = probs_ref[...]
    expert = iota(probs.shape, 0)
    first, second = routes_ref[0:1, :], routes_ref[1:2, :]
    p_first = jnp.sum(jnp.where(expert == first, probs, 0.0), axis=0, keepdims=True)
    p_second = jnp.sum(jnp.where(expert == second, probs, 0.0), axis=0, keepdims=True)
    total = p_first + p_second
    info_ref[0:1, :] = first.astype(F32)
    info_ref[1:2, :] = second.astype(F32)
    info_ref[2:3, :] = p_first / total
    info_ref[3:4, :] = p_second / total
    info_ref[4:8, :] = jnp.zeros((4, LANES), F32)
    copy_ref[...] = tokens_ref[...]


def first(routes, probs, tokens):
    width = tokens.shape[1]
    return pl.pallas_call(
        first_kernel,
        grid=(1,),
        out_shape=[jax.ShapeDtypeStruct((8, LANES), F32), jax.ShapeDtypeStruct((MB_TOK, width), BF16)],
        in_specs=[
            pl.BlockSpec(routes.shape, lambda i: (0, 0)),
            pl.BlockSpec(probs.shape, lambda i: (0, 0)),
            pl.BlockSpec((MB_TOK, width), lambda i: (0, 0)),
        ],
        out_specs=[pl.BlockSpec((8, LANES), lambda i: (0, 0)), pl.BlockSpec((MB_TOK, width), lambda i: (0, 0))],
        name="first",
    )(routes, probs, tokens)


def ranks(info, expert_rows):
    first, second = info[0:1, :].astype(jnp.int32), info[1:2, :].astype(jnp.int32)
    on_first, on_second = expert_rows == first, expert_rows == second
    named = on_first | on_second
    before = iota((LANES, LANES), 0)
    after = iota((LANES, LANES), 1)
    earlier = ((before < after) & (before // MB_TOK == after // MB_TOK)).astype(F32).astype(BF16)
    rank = jnp.dot(named.astype(F32).astype(BF16), earlier, preferred_element_type=F32)
    rank = jnp.where(named, rank.astype(jnp.int32), -1)
    weight = jnp.where(on_first, info[2:3, :], 0.0) + jnp.where(on_second, info[3:4, :], 0.0)
    return rank, weight.astype(BF16).astype(F32)


def pick(rank_row, weight_row, micro, capacity):
    slot = iota((capacity, LANES), 0)
    token = iota((capacity, LANES), 1)
    hit = (slot == rank_row) & (token // MB_TOK == micro)
    onehot = jnp.where(hit, 1.0, 0.0)
    scale = jnp.sum(jnp.where(hit, weight_row, 0.0), axis=1, keepdims=True)
    return onehot, jnp.broadcast_to(scale, (capacity, LANES))


def pack_kernel(half, capacity, micros, me_ref, info_ref, token_ref, *outs):
    rows = jnp.bitwise_xor(me_ref[0], iota((8, LANES), 0))
    rank, weight = ranks(info_ref[...], rows)
    pieces, scales = [], []
    for j in range(half):
        for micro in micros:
            onehot, scale = pick(rank[j : j + 1, :], weight[j : j + 1, :], micro, capacity)
            pieces.append(onehot)
            scales.append(scale)
    lead, width = micros[0] * MB_TOK, token_ref.shape[1]
    chosen = jnp.concatenate(pieces, axis=0)[:, lead : lead + token_ref.shape[0]].astype(BF16)
    packed = jnp.dot(chosen, token_ref[...], preferred_element_type=F32).astype(BF16)
    size = capacity * len(micros)
    for j in range(half):
        outs[j][:, 0:width] = packed[j * size : (j + 1) * size]
        outs[j][:, width:] = jnp.concatenate(scales[j * len(micros) : (j + 1) * len(micros)], axis=0).astype(BF16)


def pack(me, info, tokens, micros, half, capacity, name):
    block = jax.ShapeDtypeStruct((capacity * len(micros), tokens.shape[1] + LANES), BF16)
    vmem = pl.BlockSpec(memory_space=pltpu.VMEM)
    return pl.pallas_call(
        functools.partial(pack_kernel, half, capacity, micros),
        out_shape=[block] * half,
        in_specs=[pl.BlockSpec(memory_space=pltpu.SMEM), vmem, vmem],
        out_specs=[vmem] * half,
        compiler_params=pltpu.CompilerParams(vmem_limit_bytes=VMEM_LIMIT),
        name=name,
    )(me, info, tokens)


def back_kernel(half, capacity, me_ref, saved_ref, w_ref, tokens_ref, *refs):
    outs, copy_ref, product = refs[:half], refs[half], refs[half + 1]
    copy_ref[...] = tokens_ref[...]
    run = half * capacity
    saved = jnp.concatenate([saved_ref[m, 0] for m in range(MICRO)], axis=0)
    product[...] = jnp.dot(saved, w_ref[...], preferred_element_type=F32)
    here = lax.rem(me_ref[0], half)
    for j in range(half):
        for m in range(MICRO):
            slot = pl.multiple_of(m * run + jnp.bitwise_xor(here, j) * capacity, 8)
            outs[j][m * capacity : (m + 1) * capacity, :] = product[pl.ds(slot, capacity), :].astype(BF16)


def back(me, saved, weight, tokens, half, capacity):
    hidden_width, width = weight.shape
    column = 512 if width % 512 == 0 else width
    run = half * capacity
    block = jax.ShapeDtypeStruct((MICRO * capacity, width), BF16)
    return pl.pallas_call(
        functools.partial(back_kernel, half, capacity),
        grid_spec=pltpu.PrefetchScalarGridSpec(
            num_scalar_prefetch=1,
            grid=(width // column,),
            in_specs=[
                pl.BlockSpec((MICRO, 1, run, hidden_width), lambda i, me: (0, 1 - me[0] // half, 0, 0)),
                pl.BlockSpec((hidden_width, column), lambda i, me: (0, i)),
                pl.BlockSpec((MB_TOK, column), lambda i, me: (1, i)),
            ],
            out_specs=[pl.BlockSpec((MICRO * capacity, column), lambda i, me: (0, i))] * half
            + [pl.BlockSpec((MB_TOK, column), lambda i, me: (0, i))],
            scratch_shapes=[pltpu.VMEM((MICRO * run, column), F32)],
        ),
        out_shape=[block] * half + [jax.ShapeDtypeStruct((MB_TOK, width), BF16)],
        compiler_params=pltpu.CompilerParams(vmem_limit_bytes=VMEM_LIMIT),
        name="back",
    )(me, saved, weight, tokens)


def lines(spread):
    out = []
    for pair in range(spread.shape[0] // LANES):
        line = jnp.sum(spread[pair * LANES : (pair + 1) * LANES, :].T, axis=0, keepdims=True)
        out += [line, line]
    return jnp.concatenate(out + [jnp.zeros((8 - len(out), LANES), F32)], axis=0)


def far_grad_kernel(half, capacity, *refs):
    blocks, backs = refs[: MICRO * half], refs[MICRO * half : (MICRO + 1) * half]
    grad_ref, spread = refs[(MICRO + 1) * half :]
    width = backs[0].shape[1]
    spread[...] = jnp.zeros_like(spread)
    for j in range(half):
        for m in range(MICRO):
            total = jnp.zeros((capacity, LANES), F32)
            for lane in range(0, width, LANES):
                sent = blocks[m * half + j][:, lane : lane + LANES].astype(F32)
                held = backs[j][m * capacity : (m + 1) * capacity, lane : lane + LANES].astype(F32)
                total = total + sent * held
            at = j * MB_TOK + m * (MB_TOK // 2)
            spread[at : at + capacity, :] = total
    grad_ref[...] = lines(spread[...])


def far_grad(blocks, backs, half, capacity):
    vmem = pl.BlockSpec(memory_space=pltpu.VMEM)
    return pl.pallas_call(
        functools.partial(far_grad_kernel, half, capacity),
        out_shape=jax.ShapeDtypeStruct((8, LANES), F32),
        in_specs=[vmem] * (len(blocks) + len(backs)),
        out_specs=vmem,
        scratch_shapes=[pltpu.VMEM((half * MB_TOK, LANES), F32)],
        compiler_params=pltpu.CompilerParams(vmem_limit_bytes=VMEM_LIMIT),
        name="far_grad",
    )(*blocks, *backs)


def expert_kernel(half, capacity, plans, graded, me_ref, *refs):
    n_blocks = len(plans) * half
    blocks, (w_ref, saved_ref), refs = refs[:n_blocks], refs[n_blocks : n_blocks + 2], refs[n_blocks + 2 :]
    if graded:
        d_ref, grad_ref, lhs, product, scale, partial = refs
    else:
        _, d_ref, lhs, product, scale = refs
    width = w_ref.shape[1]
    run = half * capacity
    here = lax.rem(me_ref[0], half)
    step = pl.program_id(0)
    places = []
    at = 0
    for group, plan in enumerate(plans):
        for j in range(half):
            for i, micro in enumerate(plan):
                slot = pl.multiple_of(micro * run + jnp.bitwise_xor(here, j) * capacity, 8)
                places.append((at, group * half + j, i * capacity, slot, j, micro))
                at += capacity

    @pl.when(step == 0)
    def _():
        start = 0
        for block in blocks:
            lhs[start : start + block.shape[0], :] = block[:, 0:width]
            start += block.shape[0]
        for _, which, row, slot, _, _ in places:
            scale[pl.ds(slot, capacity), :] = blocks[which][row : row + capacity, width:].astype(F32)
        if graded:
            partial[...] = jnp.zeros_like(partial)

    got = lax.dot_general(lhs[...], w_ref[...], (((1,), (1,)), ((), ())), preferred_element_type=F32)
    for begin, _, _, slot, _, _ in places:
        product[pl.ds(slot, capacity), :] = got[begin : begin + capacity, :]
    for lane in range(0, product.shape[1], LANES):
        part = (scale[...] * product[:, lane : lane + LANES]).astype(BF16)
        for micro in range(MICRO):
            d_ref[micro, 0, :, lane : lane + LANES] = part[micro * run : (micro + 1) * run]
    if graded:
        total = jnp.zeros((MICRO * run, LANES), F32)
        for lane in range(0, product.shape[1], LANES):
            held = jnp.concatenate([saved_ref[m, 0, :, lane : lane + LANES] for m in range(MICRO)], axis=0)
            total = total + product[:, lane : lane + LANES] * held.astype(F32)
        product[:, 0:LANES] = total
        for _, _, _, slot, j, micro in places:
            row = j * MB_TOK + micro * (MB_TOK // 2)
            partial[row : row + capacity, :] += product[pl.ds(slot, capacity), 0:LANES]

        @pl.when(step == pl.num_programs(0) - 1)
        def _():
            grad_ref[...] = lines(partial[...])


def expert(me, groups, plans, weight, saved, half, capacity, held=None):
    hidden_width, width = weight.shape
    column = 256 if hidden_width % 256 == 0 else hidden_width
    run = half * capacity
    graded = held is None
    whole = pl.BlockSpec(memory_space=pltpu.VMEM)
    side = (lambda me: me[0] // half) if graded else (lambda me: 1 - me[0] // half)
    slots = pl.BlockSpec((MICRO, 1, run, column), lambda i, me: (0, side(me), 0, i))
    operands = [block for group in groups for block in group] + [weight, saved]
    in_specs = [whole] * (len(plans) * half) + [pl.BlockSpec((column, width), lambda i, me: (i, 0)), slots]
    out_shape, out_specs = [jax.ShapeDtypeStruct(saved.shape, BF16)], [slots]
    scratch = [
        pltpu.VMEM((MICRO * run, width), BF16),
        pltpu.VMEM((MICRO * run, column), F32),
        pltpu.VMEM((MICRO * run, LANES), F32),
    ]
    aliases = {}
    if graded:
        out_shape.append(jax.ShapeDtypeStruct((8, LANES), F32))
        out_specs.append(pl.BlockSpec((8, LANES), lambda i, me: (0, 0)))
        scratch.append(pltpu.VMEM((half * MB_TOK, LANES), F32))
    else:
        operands.append(held)
        in_specs.append(pl.BlockSpec(memory_space=pl.ANY))
        aliases = {len(operands): 0}
    return pl.pallas_call(
        functools.partial(expert_kernel, half, capacity, plans, graded),
        grid_spec=pltpu.PrefetchScalarGridSpec(
            num_scalar_prefetch=1,
            grid=(hidden_width // column,),
            in_specs=in_specs,
            out_specs=out_specs,
            scratch_shapes=scratch,
        ),
        out_shape=out_shape,
        input_output_aliases=aliases,
        compiler_params=pltpu.CompilerParams(vmem_limit_bytes=VMEM_LIMIT),
        name="expert_own" if graded else "expert_far",
    )(me, *operands)


def router_kernel(half, capacity, me_ref, info_ref, *refs):
    own, (far_ref, router_ref, out_ref) = refs[:half], refs[half:]
    info = info_ref[...]
    rank, _ = ranks(info, jnp.bitwise_xor(me_ref[0], iota((8, LANES), 0)))
    grads = [own[j][j : j + 1, :] for j in range(half)] + [far_ref[0:half, :]]
    columns = jnp.concatenate(grads + [jnp.zeros((LANES - 2 * half, LANES), F32)], axis=0).T
    slot = iota((capacity, LANES), 0)
    token = iota((capacity, LANES), 1)
    rows = []
    for j in range(2 * half):
        at = (j % 2) * MB_TOK
        second = at + MB_TOK // 2
        here = jnp.where(
            token // MB_TOK == 0, columns[at : at + capacity, j : j + 1], columns[second : second + capacity, j : j + 1]
        )
        rows.append(jnp.sum(jnp.where(slot == rank[j : j + 1, :], here, 0.0), axis=0, keepdims=True))
    grads = jnp.concatenate(rows, axis=0)
    first, second = info[0:1, :].astype(jnp.int32), info[1:2, :].astype(jnp.int32)
    w_first, w_second = info[2:3, :], info[3:4, :]
    relative = jnp.bitwise_xor(me_ref[0], iota((8, LANES), 0))
    g_first = jnp.sum(jnp.where(relative == first, grads, 0.0), axis=0, keepdims=True)
    g_second = jnp.sum(jnp.where(relative == second, grads, 0.0), axis=0, keepdims=True)
    mean = w_first * g_first + w_second * g_second
    expert_rows = iota((8, LANES), 0)
    logit = jnp.where(expert_rows == first, w_first * (g_first - mean), 0.0)
    logit = logit + jnp.where(expert_rows == second, w_second * (g_second - mean), 0.0)
    high = logit.astype(BF16).astype(F32)
    middle = (logit - high).astype(BF16).astype(F32)
    low = logit - high - middle
    parts = jnp.concatenate([high, middle, low, jnp.zeros((LANES - 24, LANES), F32)], axis=0).T
    router = router_ref[...].astype(F32)
    router = jnp.concatenate([router, router, router, jnp.zeros((LANES - 24, router.shape[1]), F32)], axis=0)
    out_ref[...] = jnp.dot(parts.astype(BF16), router.astype(BF16), preferred_element_type=F32).astype(BF16)


def route(block, flip, back):
    sections, peers = lax.axis_size("pipe"), lax.axis_size("expert")
    pairs = [
        (p * peers + e, ((p - back) % sections) * peers + (e ^ flip)) for p in range(sections) for e in range(peers)
    ]
    return lax.ppermute(block, ("pipe", "expert"), pairs)


def by_halves(grad_sent, routes, router_probs, saved_hidden, w_down, w_router):
    peers = lax.axis_size("expert")
    half = peers // 2
    slots, hidden_width = saved_hidden.shape[1:]
    capacity = slots // (MICRO * peers)
    me = lax.axis_index("expert").astype(jnp.int32).reshape(1)
    tokens, weight = grad_sent[0], w_down[0]
    saved = saved_hidden.reshape(MICRO, 2, half * capacity, hidden_width)
    vmem = pl.BlockSpec(memory_space=pltpu.VMEM)

    def spread(blocks):
        return [blocks[0]] + [route(blocks[j], j, 0) for j in range(1, half)]

    info, first_tokens = first(routes[0].T, router_probs[0].T, tokens)
    far_first = route(first_tokens, half, 1)
    own = route(tokens, 0, 1)
    far_info = route(info, half, 0)
    *backs, second_tokens = back(me, saved, weight, tokens, half, capacity)
    far_second = route(second_tokens, half, 1)
    backs = spread(backs)
    own_blocks = spread(pack(me, info, own, (0, 1), half, capacity, "pack_own"))
    early = pack(me, far_info, far_first, (0,), half, capacity, "pack_early")
    early_blocks = spread(early)
    held, own_grad = expert(me, [own_blocks], ((0, 1),), weight, saved, half, capacity)
    own_grads = [own_grad] + [route(own_grad, j, 0) for j in range(1, half)]
    late = pack(me, far_info, far_second, (1,), half, capacity, "pack_late")
    late_blocks = spread(late)
    far_grads = route(far_grad([*early, *late], backs, half, capacity), half, 0)
    (d_hidden,) = expert(me, [early_blocks, late_blocks], ((0,), (1,)), weight, saved, half, capacity, held)
    grad_in = pl.pallas_call(
        functools.partial(router_kernel, half, capacity),
        out_shape=jax.ShapeDtypeStruct(tokens.shape, BF16),
        in_specs=[pl.BlockSpec(memory_space=pltpu.SMEM)] + [vmem] * (half + 3),
        out_specs=vmem,
        compiler_params=pltpu.CompilerParams(vmem_limit_bytes=VMEM_LIMIT),
        name="router",
    )(me, info, *own_grads, far_grads, w_router.T)
    return d_hidden.reshape(saved_hidden.shape), grad_in[None]


def from_behind(block, axis, distance):
    devices = range(lax.axis_size(axis))
    route = [((i - distance) % len(devices), i) for i in devices]
    return lax.ppermute(block, axis, route)


def route_slots(route_rows, peer_count, capacity):
    onehot = (route_rows[..., None] == jnp.arange(peer_count, dtype=jnp.int32)).astype(jnp.int32)
    rank_of = jnp.sum((jnp.cumsum(onehot, axis=1) - onehot) * onehot, axis=2)
    return route_rows * capacity + rank_of


def by_slots(grad_sent, routes, router_probs, saved_hidden, w_down, w_router):
    peer_count = lax.axis_size("expert")
    slot_count = saved_hidden.shape[1]
    capacity = slot_count // (MICRO * peer_count)
    send_width = peer_count * capacity
    model_width = grad_sent.shape[2]
    hidden_width = saved_hidden.shape[2]
    tokens = routes.shape[1]
    incoming = from_behind(grad_sent, "pipe", -1)[0]
    route_rows = routes[0].reshape(MICRO, MB_TOK * TOP)
    position = route_slots(route_rows, peer_count, capacity)
    chosen = jnp.take_along_axis(router_probs[0], routes[0], axis=1)
    weights = chosen / jnp.sum(chosen, axis=1, keepdims=True)
    rounded = weights.astype(jnp.bfloat16)
    micro_index = jnp.arange(MICRO, dtype=jnp.int32)[:, None]
    token_index = jnp.broadcast_to(
        jnp.arange(MB_TOK * TOP, dtype=jnp.int32)[None, :] // TOP, (MICRO, MB_TOK * TOP)
    )
    slot_token = (
        jnp.zeros((MICRO, send_width), jnp.int32).at[micro_index, position].set(token_index)
    )
    slot_used = jnp.zeros((MICRO, send_width), jnp.bool_).at[micro_index, position].set(True)
    send_scale = (
        jnp.zeros((MICRO, send_width), jnp.bfloat16)
        .at[micro_index, position]
        .set(rounded.reshape(MICRO, MB_TOK * TOP))
    )
    micro_grad = incoming.reshape(MICRO, MB_TOK, model_width)
    picked = jnp.take_along_axis(micro_grad, slot_token[..., None], axis=1)
    send_rows = jnp.where(slot_used[..., None], picked, jnp.zeros((), jnp.bfloat16))
    hidden = saved_hidden[0].reshape(MICRO, send_width, hidden_width)
    weight = w_down[0]
    arrived, arrived_scale = (
        lax.all_to_all(send_rows, "expert", split_axis=1, concat_axis=1, tiled=True),
        lax.all_to_all(send_scale, "expert", split_axis=1, concat_axis=1, tiled=True),
    )
    flat_rows = arrived.reshape(-1, model_width)
    flat_saved = hidden.reshape(flat_rows.shape[0], hidden_width)
    grad_hidden = lax.dot_general(
        flat_rows, weight, (((1,), (1,)), ((), ())), preferred_element_type=jnp.float32
    )
    route_grad = jnp.sum(grad_hidden * flat_saved.astype(jnp.float32), axis=1)
    scaled = (arrived_scale.reshape(-1, 1).astype(jnp.float32) * grad_hidden).astype(jnp.bfloat16)
    d_hidden, route_grad = (scaled, route_grad.reshape(arrived_scale.shape))
    returned = lax.all_to_all(route_grad, "expert", split_axis=1, concat_axis=1, tiled=True)
    slot_grad = jnp.take_along_axis(returned, position, axis=1).reshape(tokens, TOP)
    centred = slot_grad - jnp.sum(weights * slot_grad, axis=1, keepdims=True)
    logit_part = weights * centred
    onehot_tok = (routes[0][..., None] == jnp.arange(peer_count, dtype=jnp.int32)).astype(
        jnp.float32
    )
    logit_grad = jnp.sum(logit_part[..., None] * onehot_tok, axis=1)
    grad_in = jnp.dot(logit_grad, w_router.astype(jnp.float32).T, precision=lax.Precision.HIGHEST)
    return (d_hidden.reshape(1, slot_count, hidden_width), grad_in.astype(jnp.bfloat16)[None])


def on_device(*blocks):
    peers, slots = lax.axis_size("expert"), blocks[3].shape[1]
    capacity = slots // (MICRO * peers)
    if peers == 8 and capacity % 8 == 0 and capacity <= MB_TOK // 2:
        return by_halves(*blocks)
    return by_slots(*blocks)


def solution(mesh):
    placed = (
        P("pipe", "expert", None),
        P("pipe", "expert", None),
        P("pipe", "expert", None),
        P("pipe", "expert", None),
        P("expert", None, None),
        P(),
    )
    return jax.shard_map(
        on_device,
        mesh=mesh,
        in_specs=placed,
        out_specs=(P("pipe", "expert", None), P("pipe", "expert", None)),
        check_vma=False,
    )
```

```python
import functools

import jax
import jax.numpy as jnp
from jax import lax
from jax.experimental import pallas as pl
from jax.experimental.pallas import tpu as pltpu
from jax.sharding import PartitionSpec as P

TOP = 2
MICRO = 2
MB_TOK = 64
LANES = 128
F32, BF16 = jnp.float32, jnp.bfloat16
VMEM_LIMIT = 16 * 1024 * 1024
COLUMN = 256


def iota(shape, axis):
    return lax.broadcasted_iota(jnp.int32, shape, axis)


def info_kernel(routes_ref, probs_ref, info_ref):
    probs = probs_ref[...]
    expert = iota(probs.shape, 0)
    first, second = routes_ref[0:1, :], routes_ref[1:2, :]
    p_first = jnp.sum(jnp.where(expert == first, probs, 0.0), axis=0, keepdims=True)
    p_second = jnp.sum(jnp.where(expert == second, probs, 0.0), axis=0, keepdims=True)
    total = p_first + p_second
    info_ref[0:1, :] = first.astype(F32)
    info_ref[1:2, :] = second.astype(F32)
    info_ref[2:3, :] = p_first / total
    info_ref[3:4, :] = p_second / total
    info_ref[4:8, :] = jnp.zeros((4, LANES), F32)


def split(column):
    high = column.astype(BF16).astype(F32)
    middle = (column - high).astype(BF16).astype(F32)
    return high, middle, column - high - middle


def ranks(info, expert_rows):
    first, second = info[0:1, :].astype(jnp.int32), info[1:2, :].astype(jnp.int32)
    on_first, on_second = expert_rows == first, expert_rows == second
    named = on_first | on_second
    before = iota((LANES, LANES), 0)
    after = iota((LANES, LANES), 1)
    earlier = ((before < after) & (before // MB_TOK == after // MB_TOK)).astype(F32).astype(BF16)
    rank = jnp.dot(named.astype(F32).astype(BF16), earlier, preferred_element_type=F32)
    rank = jnp.where(named, rank.astype(jnp.int32), -1)
    weight = jnp.where(on_first, info[2:3, :], 0.0) + jnp.where(on_second, info[3:4, :], 0.0)
    return rank, weight.astype(BF16).astype(F32)


def pick(rank_row, weight_row, micro, capacity):
    slot = iota((capacity, LANES), 0)
    token = iota((capacity, LANES), 1)
    hit = (slot == rank_row) & (token // MB_TOK == micro)
    onehot = jnp.where(hit, 1.0, 0.0)
    scale = jnp.sum(jnp.where(hit, weight_row, 0.0), axis=1, keepdims=True)
    return onehot, jnp.broadcast_to(scale, (capacity, LANES))


def pack_kernel(half, capacity, me_ref, info_ref, token_ref, *refs):
    outs = refs[-half:]
    rows = jnp.bitwise_xor(me_ref[0], iota((8, LANES), 0))
    rank, weight = ranks(info_ref[...], rows)
    pieces, scales = [], []
    for j in range(half):
        for micro in range(MICRO):
            onehot, scale = pick(rank[j : j + 1, :], weight[j : j + 1, :], micro, capacity)
            pieces.append(onehot)
            scales.append(scale)
    width = token_ref.shape[1]
    chosen = jnp.concatenate(pieces, axis=0).astype(BF16)
    packed = jnp.dot(chosen, token_ref[...], preferred_element_type=F32).astype(BF16)
    size = MICRO * capacity
    for j in range(half):
        outs[j][:, 0:width] = packed[j * size : (j + 1) * size]
        outs[j][:, width:] = jnp.concatenate(scales[j * MICRO : (j + 1) * MICRO], axis=0).astype(BF16)


def pack(me, info, tokens, half, capacity, name, into=()):
    rows, width = MICRO * capacity, tokens.shape[1] + LANES
    at = 1 if into else 0
    return pl.pallas_call(
        functools.partial(pack_kernel, half, capacity),
        grid=(1,),
        out_shape=[jax.ShapeDtypeStruct(((1 + at) * rows, width), BF16)] * half,
        in_specs=[
            pl.BlockSpec(memory_space=pltpu.SMEM),
            pl.BlockSpec(info.shape, lambda i: (0, 0)),
            pl.BlockSpec(tokens.shape, lambda i: (0, 0)),
        ]
        + [pl.BlockSpec(memory_space=pl.ANY)] * len(into),
        out_specs=[pl.BlockSpec((rows, width), lambda i: (at, 0))] * half,
        input_output_aliases={3 + j: j for j in range(len(into))},
        compiler_params=pltpu.CompilerParams(vmem_limit_bytes=VMEM_LIMIT),
        name=name,
    )(me, info, tokens, *into)


def chunks(width):
    step = COLUMN if width % COLUMN == 0 else width
    return [pl.ds(start, step) for start in range(0, width, step)]


def back_kernel(half, capacity, turn, me_ref, saved_ref, w_ref, *refs):
    outs, product = refs[:half], refs[half]
    run = half * capacity
    saved = jnp.concatenate([saved_ref[m, 0] for m in range(MICRO)], axis=0)
    here = jnp.bitwise_xor(lax.rem(me_ref[0], half), turn)
    for columns in chunks(w_ref.shape[1]):
        product[:, columns] = jnp.dot(saved, w_ref[:, columns], preferred_element_type=F32)
    for j in range(half):
        for m in range(MICRO):
            slot = pl.multiple_of(m * run + jnp.bitwise_xor(here, j) * capacity, 8)
            outs[j][m * capacity : (m + 1) * capacity, :] = product[pl.ds(slot, capacity), :].astype(BF16)


def back(me, saved, weight, half, capacity, turn):
    hidden_width, width = weight.shape
    run, rows = half * capacity, MICRO * capacity
    return pl.pallas_call(
        functools.partial(back_kernel, half, capacity, turn),
        grid_spec=pltpu.PrefetchScalarGridSpec(
            num_scalar_prefetch=1,
            grid=(1,),
            in_specs=[
                pl.BlockSpec((MICRO, 1, run, hidden_width), lambda i, me: (0, 1 - me[0] // half, 0, 0)),
                pl.BlockSpec(memory_space=pltpu.VMEM),
            ],
            out_specs=[pl.BlockSpec((rows, width), lambda i, me: (0, 0))] * half,
            scratch_shapes=[pltpu.VMEM((MICRO * run, width), F32)],
        ),
        out_shape=[jax.ShapeDtypeStruct((2 * rows, width + LANES), BF16)] * half,
        compiler_params=pltpu.CompilerParams(vmem_limit_bytes=VMEM_LIMIT),
        name="back",
    )(me, saved, weight)


def far_grad_kernel(half, capacity, *refs):
    blocks, backs, (grad_ref,) = refs[:half], refs[half : 2 * half], refs[2 * half :]
    width = blocks[0].shape[1] - LANES
    rows = MICRO * capacity
    where = iota((rows, LANES), 1)
    table = jnp.zeros((rows, LANES), F32)
    for j in range(half):
        total = jnp.zeros((rows, LANES), F32)
        for lane in range(0, width, LANES):
            sent = blocks[j][:, lane : lane + LANES].astype(F32)
            total = total + sent * backs[j][:, lane : lane + LANES].astype(F32)
        for i, part in enumerate(split(jnp.sum(total, axis=1, keepdims=True))):
            table = jnp.where(where == 3 * j + i, part, table)
    grad_ref[...] = table.astype(BF16)


def far_grad(blocks, backs, half, capacity):
    vmem = pl.BlockSpec(memory_space=pltpu.VMEM)
    rows, width = blocks[0].shape
    return pl.pallas_call(
        functools.partial(far_grad_kernel, half, capacity),
        grid=(1,),
        out_shape=jax.ShapeDtypeStruct((rows, LANES), BF16),
        in_specs=[vmem] * half + [pl.BlockSpec((rows, width), lambda i: (0, 0))] * half,
        out_specs=vmem,
        compiler_params=pltpu.CompilerParams(vmem_limit_bytes=VMEM_LIMIT),
        name="far_grad",
    )(*blocks, *backs)


def expert_kernel(half, capacity, turn, graded, me_ref, *refs):
    blocks, w_ref, refs = refs[:half], refs[half], refs[half + 1 :]
    if graded:
        saved_ref, _, d_ref, *grads, lhs, product, scale, partial = refs
    else:
        _, d_ref, lhs, product, scale = refs
    hidden_width, width = w_ref.shape
    run = half * capacity
    here = jnp.bitwise_xor(lax.rem(me_ref[0], half), turn)
    places = []
    for j in range(half):
        for m in range(MICRO):
            slot = pl.multiple_of(m * run + jnp.bitwise_xor(here, j) * capacity, 8)
            places.append((j, m * capacity, (j * MICRO + m) * capacity, slot))
    for j in range(half):
        lhs[j * MICRO * capacity : (j + 1) * MICRO * capacity, :] = blocks[j][:, 0:width]
    for j, row, _, slot in places:
        scale[pl.ds(slot, capacity), :] = blocks[j][row : row + capacity, width:].astype(F32)
    for columns in chunks(hidden_width):
        got = lax.dot_general(lhs[...], w_ref[columns, :], (((1,), (1,)), ((), ())), preferred_element_type=F32)
        for _, _, begin, slot in places:
            product[pl.ds(slot, capacity), columns] = got[begin : begin + capacity, :]
    total = jnp.zeros((MICRO * run, LANES), F32)
    for lane in range(0, hidden_width, LANES):
        part = product[:, lane : lane + LANES]
        scaled = (scale[...] * part).astype(BF16)
        for m in range(MICRO):
            d_ref[m, 0, :, lane : lane + LANES] = scaled[m * run : (m + 1) * run]
        if graded:
            held = jnp.concatenate([saved_ref[m, 0, :, lane : lane + LANES] for m in range(MICRO)], axis=0)
            total = total + part * held.astype(F32)
    if graded:
        partial[...] = total
        lane = iota((capacity, LANES), 1)
        for j, row, _, slot in places:
            parts = split(jnp.sum(partial[pl.ds(slot, capacity), :], axis=1, keepdims=True))
            table = jnp.where(lane == 0, parts[0], jnp.where(lane == 1, parts[1], parts[2]))
            grads[j][row : row + capacity, :] = table.astype(BF16)


def expert(me, blocks, weight, half, capacity, turn, saved=None, wait=None, held=None):
    hidden_width, width = weight.shape
    run, rows = half * capacity, MICRO * capacity
    graded = held is None
    row_block = 1 if graded else 0
    anywhere = pl.BlockSpec(memory_space=pl.ANY)
    side = (lambda me: me[0] // half) if graded else (lambda me: 1 - me[0] // half)
    slots = pl.BlockSpec((MICRO, 1, run, hidden_width), lambda i, me: (0, side(me), 0, 0))
    in_specs = [pl.BlockSpec((rows, width + LANES), lambda i, me: (row_block, 0))] * half
    in_specs += [pl.BlockSpec(memory_space=pltpu.VMEM)]
    scratch = [
        pltpu.VMEM((MICRO * run, width), BF16),
        pltpu.VMEM((MICRO * run, hidden_width), F32),
        pltpu.VMEM((MICRO * run, LANES), F32),
    ]
    if graded:
        out_shape = [jax.ShapeDtypeStruct(saved.shape, BF16)] + [jax.ShapeDtypeStruct((rows, LANES), BF16)] * half
        out_specs = [slots] + [pl.BlockSpec((rows, LANES), lambda i, me: (0, 0))] * half
        scratch.append(pltpu.VMEM((MICRO * run, LANES), F32))
        operands, in_specs, aliases = [saved, wait], in_specs + [slots, anywhere], {}
    else:
        out_shape, out_specs = [jax.ShapeDtypeStruct(held.shape, BF16)], [slots]
        operands, in_specs, aliases = [held], in_specs + [anywhere], {half + 2: 0}
    return pl.pallas_call(
        functools.partial(expert_kernel, half, capacity, turn, graded),
        grid_spec=pltpu.PrefetchScalarGridSpec(
            num_scalar_prefetch=1,
            grid=(1,),
            in_specs=in_specs,
            out_specs=out_specs,
            scratch_shapes=scratch,
        ),
        out_shape=out_shape,
        input_output_aliases=aliases,
        compiler_params=pltpu.CompilerParams(vmem_limit_bytes=VMEM_LIMIT),
        name="expert_own" if graded else "expert_far",
    )(me, *blocks, weight, *operands)


def router_kernel(half, capacity, turn, me_ref, info_ref, *refs):
    own, (far_ref, router_ref, out_ref) = refs[:half], refs[half:]
    info = info_ref[...]
    relative = jnp.bitwise_xor(me_ref[0], iota((8, LANES), 0))
    rank, _ = ranks(info, relative)
    slot = iota((capacity, LANES), 0)
    token = iota((capacity, LANES), 1)
    far = far_ref[...].astype(F32)
    rows = []
    for j in range(2 * half):
        if j < half:
            table, lane = own[j][...].astype(F32), 0
        else:
            table, lane = far, 3 * ((j - half) ^ turn)
        column = table[:, lane : lane + 1] + table[:, lane + 1 : lane + 2] + table[:, lane + 2 : lane + 3]
        here = jnp.where(token // MB_TOK == 0, column[0:capacity], column[capacity : 2 * capacity])
        rows.append(jnp.sum(jnp.where(slot == rank[j : j + 1, :], here, 0.0), axis=0, keepdims=True))
    grads = jnp.concatenate(rows, axis=0)
    first, second = info[0:1, :].astype(jnp.int32), info[1:2, :].astype(jnp.int32)
    w_first, w_second = info[2:3, :], info[3:4, :]
    g_first = jnp.sum(jnp.where(relative == first, grads, 0.0), axis=0, keepdims=True)
    g_second = jnp.sum(jnp.where(relative == second, grads, 0.0), axis=0, keepdims=True)
    mean = w_first * g_first + w_second * g_second
    expert_rows = iota((8, LANES), 0)
    logit = jnp.where(expert_rows == first, w_first * (g_first - mean), 0.0)
    logit = logit + jnp.where(expert_rows == second, w_second * (g_second - mean), 0.0)
    parts = jnp.concatenate([*split(logit), jnp.zeros((LANES - 24, LANES), F32)], axis=0).T
    router = router_ref[...].astype(F32)
    router = jnp.concatenate([router, router, router, jnp.zeros((LANES - 24, router.shape[1]), F32)], axis=0)
    out_ref[...] = jnp.dot(parts.astype(BF16), router.astype(BF16), preferred_element_type=F32).astype(BF16)


def router(me, info, own, far, table, tokens, half, capacity, turn):
    vmem = pl.BlockSpec(memory_space=pltpu.VMEM)
    return pl.pallas_call(
        functools.partial(router_kernel, half, capacity, turn),
        out_shape=jax.ShapeDtypeStruct(tokens.shape, BF16),
        in_specs=[pl.BlockSpec(memory_space=pltpu.SMEM)] + [vmem] * (half + 3),
        out_specs=vmem,
        compiler_params=pltpu.CompilerParams(vmem_limit_bytes=VMEM_LIMIT),
        name="router",
    )(me, info, *own, far, table)


def route(block, flip, back):
    sections, peers = lax.axis_size("pipe"), lax.axis_size("expert")
    pairs = [
        (p * peers + e, ((p - back) % sections) * peers + (e ^ flip)) for p in range(sections) for e in range(peers)
    ]
    return lax.ppermute(block, ("pipe", "expert"), pairs)


def by_halves(grad_sent, routes, router_probs, saved_hidden, w_down, w_router):
    peers = lax.axis_size("expert")
    half, turn = peers // 2, 2
    slots, hidden_width = saved_hidden.shape[1:]
    capacity = slots // (MICRO * peers)
    me = lax.axis_index("expert").astype(jnp.int32).reshape(1)
    tokens, weight = grad_sent[0], w_down[0]
    saved = saved_hidden.reshape(MICRO, 2, half * capacity, hidden_width)
    vmem = pl.BlockSpec(memory_space=pltpu.VMEM)

    def spread(blocks):
        return [blocks[0]] + [route(blocks[j], j, 0) for j in range(1, half)]

    own_tokens = route(tokens, 0, 1)
    info = pl.pallas_call(
        info_kernel,
        out_shape=jax.ShapeDtypeStruct((8, LANES), F32),
        in_specs=[vmem, vmem],
        out_specs=vmem,
        name="info",
    )(routes[0].T, router_probs[0].T)
    far_info = route(info, half + turn, 0)
    far_tokens = route(lax.optimization_barrier((tokens, info))[0], half + turn, 1)
    backs = back(me, saved, weight, half, capacity, turn)
    near = spread(pack(me, info, own_tokens, half, capacity, "pack_own", backs))
    far = pack(me, far_info, far_tokens, half, capacity, "pack_far")
    far_own = far_grad(far, near, half, capacity)
    far_grads = route(far_own, half + turn, 0)
    far = spread(far)
    held, *own_grads = expert(me, near, weight, half, capacity, 0, saved=saved, wait=far_own)
    own_grads = spread(own_grads)
    (d_hidden,) = expert(me, far, weight, half, capacity, turn, held=held)
    grad_in = router(me, info, own_grads, far_grads, w_router.T, tokens, half, capacity, turn)
    return d_hidden.reshape(saved_hidden.shape), grad_in[None]


def from_behind(block, axis, distance):
    devices = range(lax.axis_size(axis))
    route = [((i - distance) % len(devices), i) for i in devices]
    return lax.ppermute(block, axis, route)


def route_slots(route_rows, peer_count, capacity):
    onehot = (route_rows[..., None] == jnp.arange(peer_count, dtype=jnp.int32)).astype(jnp.int32)
    rank_of = jnp.sum((jnp.cumsum(onehot, axis=1) - onehot) * onehot, axis=2)
    return route_rows * capacity + rank_of


def by_slots(grad_sent, routes, router_probs, saved_hidden, w_down, w_router):
    peer_count = lax.axis_size("expert")
    slot_count = saved_hidden.shape[1]
    capacity = slot_count // (MICRO * peer_count)
    send_width = peer_count * capacity
    model_width = grad_sent.shape[2]
    hidden_width = saved_hidden.shape[2]
    tokens = routes.shape[1]
    incoming = from_behind(grad_sent, "pipe", -1)[0]
    route_rows = routes[0].reshape(MICRO, MB_TOK * TOP)
    position = route_slots(route_rows, peer_count, capacity)
    chosen = jnp.take_along_axis(router_probs[0], routes[0], axis=1)
    weights = chosen / jnp.sum(chosen, axis=1, keepdims=True)
    rounded = weights.astype(jnp.bfloat16)
    micro_index = jnp.arange(MICRO, dtype=jnp.int32)[:, None]
    token_index = jnp.broadcast_to(
        jnp.arange(MB_TOK * TOP, dtype=jnp.int32)[None, :] // TOP, (MICRO, MB_TOK * TOP)
    )
    slot_token = (
        jnp.zeros((MICRO, send_width), jnp.int32).at[micro_index, position].set(token_index)
    )
    slot_used = jnp.zeros((MICRO, send_width), jnp.bool_).at[micro_index, position].set(True)
    send_scale = (
        jnp.zeros((MICRO, send_width), jnp.bfloat16)
        .at[micro_index, position]
        .set(rounded.reshape(MICRO, MB_TOK * TOP))
    )
    micro_grad = incoming.reshape(MICRO, MB_TOK, model_width)
    picked = jnp.take_along_axis(micro_grad, slot_token[..., None], axis=1)
    send_rows = jnp.where(slot_used[..., None], picked, jnp.zeros((), jnp.bfloat16))
    hidden = saved_hidden[0].reshape(MICRO, send_width, hidden_width)
    weight = w_down[0]
    arrived, arrived_scale = (
        lax.all_to_all(send_rows, "expert", split_axis=1, concat_axis=1, tiled=True),
        lax.all_to_all(send_scale, "expert", split_axis=1, concat_axis=1, tiled=True),
    )
    flat_rows = arrived.reshape(-1, model_width)
    flat_saved = hidden.reshape(flat_rows.shape[0], hidden_width)
    grad_hidden = lax.dot_general(
        flat_rows, weight, (((1,), (1,)), ((), ())), preferred_element_type=jnp.float32
    )
    route_grad = jnp.sum(grad_hidden * flat_saved.astype(jnp.float32), axis=1)
    scaled = (arrived_scale.reshape(-1, 1).astype(jnp.float32) * grad_hidden).astype(jnp.bfloat16)
    d_hidden, route_grad = (scaled, route_grad.reshape(arrived_scale.shape))
    returned = lax.all_to_all(route_grad, "expert", split_axis=1, concat_axis=1, tiled=True)
    slot_grad = jnp.take_along_axis(returned, position, axis=1).reshape(tokens, TOP)
    centred = slot_grad - jnp.sum(weights * slot_grad, axis=1, keepdims=True)
    logit_part = weights * centred
    onehot_tok = (routes[0][..., None] == jnp.arange(peer_count, dtype=jnp.int32)).astype(
        jnp.float32
    )
    logit_grad = jnp.sum(logit_part[..., None] * onehot_tok, axis=1)
    grad_in = jnp.dot(logit_grad, w_router.astype(jnp.float32).T, precision=lax.Precision.HIGHEST)
    return (d_hidden.reshape(1, slot_count, hidden_width), grad_in.astype(jnp.bfloat16)[None])


def on_device(*blocks):
    peers, slots = lax.axis_size("expert"), blocks[3].shape[1]
    capacity = slots // (MICRO * peers)
    if peers == 8 and capacity % 8 == 0 and capacity <= MB_TOK // 2:
        return by_halves(*blocks)
    return by_slots(*blocks)


def solution(mesh):
    placed = (
        P("pipe", "expert", None),
        P("pipe", "expert", None),
        P("pipe", "expert", None),
        P("pipe", "expert", None),
        P("expert", None, None),
        P(),
    )
    return jax.shard_map(
        on_device,
        mesh=mesh,
        in_specs=placed,
        out_specs=(P("pipe", "expert", None), P("pipe", "expert", None)),
        check_vma=False,
    )
```

```python
import functools

import jax
import jax.numpy as jnp
from jax import lax
from jax.experimental import pallas as pl
from jax.experimental.pallas import tpu as pltpu
from jax.sharding import PartitionSpec as P

TOP = 2
MICRO = 2
MB_TOK = 64
LANES = 128
F32, BF16 = jnp.float32, jnp.bfloat16
VMEM_LIMIT = 16 * 1024 * 1024
COLUMN = 256
SCALE = 3
OWN_ORDER, BACK_ORDER, FAR_ORDER = (0, 1, 2, 3), (0, 3, 2, 1), (0, 3, 2, 1)


def iota(shape, axis):
    return lax.broadcasted_iota(jnp.int32, shape, axis)


def info_kernel(routes_ref, probs_ref, info_ref):
    probs = probs_ref[...]
    expert = iota(probs.shape, 0)
    first, second = routes_ref[0:1, :], routes_ref[1:2, :]
    p_first = jnp.sum(jnp.where(expert == first, probs, 0.0), axis=0, keepdims=True)
    p_second = jnp.sum(jnp.where(expert == second, probs, 0.0), axis=0, keepdims=True)
    total = p_first + p_second
    info_ref[0:1, :] = first.astype(F32)
    info_ref[1:2, :] = second.astype(F32)
    info_ref[2:3, :] = p_first / total
    info_ref[3:4, :] = p_second / total
    info_ref[4:8, :] = jnp.zeros((4, LANES), F32)


def split(column):
    high = column.astype(BF16).astype(F32)
    middle = (column - high).astype(BF16).astype(F32)
    return high, middle, column - high - middle


def ranks(info, expert_rows):
    first, second = info[0:1, :].astype(jnp.int32), info[1:2, :].astype(jnp.int32)
    on_first, on_second = expert_rows == first, expert_rows == second
    named = on_first | on_second
    before = iota((LANES, LANES), 0)
    after = iota((LANES, LANES), 1)
    earlier = ((before < after) & (before // MB_TOK == after // MB_TOK)).astype(F32).astype(BF16)
    rank = jnp.dot(named.astype(F32).astype(BF16), earlier, preferred_element_type=F32)
    rank = jnp.where(named, rank.astype(jnp.int32), -1)
    weight = jnp.where(on_first, info[2:3, :], 0.0) + jnp.where(on_second, info[3:4, :], 0.0)
    return rank, weight.astype(BF16).astype(F32)


def pick(rank_row, weight_row, micro, capacity):
    slot = iota((capacity, LANES), 0)
    token = iota((capacity, LANES), 1)
    hit = (slot == rank_row) & (token // MB_TOK == micro)
    onehot = jnp.where(hit, 1.0, 0.0)
    scale = jnp.sum(jnp.where(hit, weight_row, 0.0), axis=1, keepdims=True)
    return onehot, jnp.broadcast_to(scale, (capacity, LANES))


def pack_kernel(half, capacity, me_ref, info_ref, token_ref, *refs):
    grads, outs = refs[:-half], refs[-half:]
    rows = jnp.bitwise_xor(me_ref[0], iota((8, LANES), 0))
    rank, weight = ranks(info_ref[...], rows)
    pieces, scales = [], []
    for j in range(half):
        for micro in range(MICRO):
            onehot, scale = pick(rank[j : j + 1, :], weight[j : j + 1, :], micro, capacity)
            pieces.append(onehot)
            scales.append(scale)
    width = token_ref.shape[1]
    chosen = jnp.concatenate(pieces, axis=0).astype(BF16)
    packed = jnp.dot(chosen, token_ref[...], preferred_element_type=F32).astype(BF16)
    size = MICRO * capacity
    lane = iota((size, LANES), 1)
    for j in range(half):
        outs[j][:, 0:width] = packed[j * size : (j + 1) * size]
        tail = jnp.concatenate(scales[j * MICRO : (j + 1) * MICRO], axis=0)
        if grads:
            tail = jnp.where(lane < SCALE, grads[j][...].astype(F32), tail)
        outs[j][:, width:] = tail.astype(BF16)


def pack(me, info, tokens, half, capacity, name, grads=()):
    block = jax.ShapeDtypeStruct((MICRO * capacity, tokens.shape[1] + LANES), BF16)
    vmem = pl.BlockSpec(memory_space=pltpu.VMEM)
    return pl.pallas_call(
        functools.partial(pack_kernel, half, capacity),
        out_shape=[block] * half,
        in_specs=[pl.BlockSpec(memory_space=pltpu.SMEM)] + [vmem] * (2 + len(grads)),
        out_specs=[vmem] * half,
        compiler_params=pltpu.CompilerParams(vmem_limit_bytes=VMEM_LIMIT),
        name=name,
    )(me, info, tokens, *grads)


def chunks(width):
    step = COLUMN if width % COLUMN == 0 else width
    return [pl.ds(start, step) for start in range(0, width, step)]


def back_kernel(half, capacity, turn, me_ref, saved_ref, w_ref, *refs):
    outs, product = refs[:half], refs[half]
    run = half * capacity
    saved = jnp.concatenate([saved_ref[m, 0] for m in range(MICRO)], axis=0)
    here = jnp.bitwise_xor(lax.rem(me_ref[0], half), turn)
    for columns in chunks(w_ref.shape[1]):
        product[:, columns] = jnp.dot(saved, w_ref[:, columns], preferred_element_type=F32)
    for j in range(half):
        for m in range(MICRO):
            slot = pl.multiple_of(m * run + jnp.bitwise_xor(here, j) * capacity, 8)
            outs[j][m * capacity : (m + 1) * capacity, :] = product[pl.ds(slot, capacity), :].astype(BF16)


def back(me, saved, weight, half, capacity, turn):
    hidden_width, width = weight.shape
    run, rows = half * capacity, MICRO * capacity
    return pl.pallas_call(
        functools.partial(back_kernel, half, capacity, turn),
        grid_spec=pltpu.PrefetchScalarGridSpec(
            num_scalar_prefetch=1,
            grid=(1,),
            in_specs=[
                pl.BlockSpec((MICRO, 1, run, hidden_width), lambda i, me: (0, 1 - me[0] // half, 0, 0)),
                pl.BlockSpec(memory_space=pltpu.VMEM),
            ],
            out_specs=[pl.BlockSpec((rows, width), lambda i, me: (0, 0))] * half,
            scratch_shapes=[pltpu.VMEM((MICRO * run, width), F32)],
        ),
        out_shape=[jax.ShapeDtypeStruct((rows, width), BF16)] * half,
        compiler_params=pltpu.CompilerParams(vmem_limit_bytes=VMEM_LIMIT),
        name="back",
    )(me, saved, weight)


def turn_kernel(w_ref, after_ref, out_ref):
    del after_ref
    for columns in chunks(w_ref.shape[1]):
        out_ref[columns, :] = w_ref[:, columns].T


def turned(weight, after):
    vmem = pl.BlockSpec(memory_space=pltpu.VMEM)
    return pl.pallas_call(
        turn_kernel,
        out_shape=jax.ShapeDtypeStruct(weight.shape[::-1], BF16),
        in_specs=[vmem, pl.BlockSpec(memory_space=pl.ANY)],
        out_specs=vmem,
        compiler_params=pltpu.CompilerParams(vmem_limit_bytes=VMEM_LIMIT),
        name="turned",
    )(weight, after)


def far_grad_kernel(half, capacity, *refs):
    blocks, (grad_ref,) = refs[:half], refs[2 * half :]
    backs = [refs[half + BACK_ORDER.index(j)] for j in range(half)]
    width = blocks[0].shape[1] - LANES
    rows = MICRO * capacity
    where = iota((rows, LANES), 1)
    table = jnp.zeros((rows, LANES), F32)
    for j in range(half):
        total = jnp.zeros((rows, LANES), F32)
        for lane in range(0, width, LANES):
            sent = blocks[j][:, lane : lane + LANES].astype(F32)
            total = total + sent * backs[j][:, lane : lane + LANES].astype(F32)
        for i, part in enumerate(split(jnp.sum(total, axis=1, keepdims=True))):
            table = jnp.where(where == 3 * j + i, part, table)
    grad_ref[...] = table.astype(BF16)


def far_grad(blocks, backs, half, capacity):
    vmem = pl.BlockSpec(memory_space=pltpu.VMEM)
    return pl.pallas_call(
        functools.partial(far_grad_kernel, half, capacity),
        out_shape=jax.ShapeDtypeStruct((MICRO * capacity, LANES), BF16),
        in_specs=[vmem] * (2 * half),
        out_specs=vmem,
        compiler_params=pltpu.CompilerParams(vmem_limit_bytes=VMEM_LIMIT),
        name="far_grad",
    )(*blocks, *[backs[j] for j in BACK_ORDER])


def expert_kernel(half, capacity, turn, graded, me_ref, *refs):
    order = OWN_ORDER if graded else FAR_ORDER
    blocks, w_ref, refs = [refs[order.index(j)] for j in range(half)], refs[half], refs[half + 1 :]
    if graded:
        saved_ref, d_ref, *grads, lhs, product, scale, partial = refs
    else:
        _, d_ref, lhs, product, scale = refs
    width, hidden_width = w_ref.shape
    run = half * capacity
    here = jnp.bitwise_xor(lax.rem(me_ref[0], half), turn)
    places = []
    for j in range(half):
        for m in range(MICRO):
            slot = pl.multiple_of(m * run + jnp.bitwise_xor(here, j) * capacity, 8)
            places.append((j, m * capacity, (j * MICRO + m) * capacity, slot))
    for j in range(half):
        lhs[j * MICRO * capacity : (j + 1) * MICRO * capacity, :] = blocks[j][:, 0:width]
    for j, row, _, slot in places:
        tail = blocks[j][row : row + capacity, width:].astype(F32)
        scale[pl.ds(slot, capacity), :] = jnp.broadcast_to(tail[:, SCALE : SCALE + 1], tail.shape)
    for columns in chunks(hidden_width):
        got = jnp.dot(lhs[...], w_ref[:, columns], preferred_element_type=F32)
        for _, _, begin, slot in places:
            product[pl.ds(slot, capacity), columns] = got[begin : begin + capacity, :]
    total = jnp.zeros((MICRO * run, LANES), F32)
    for lane in range(0, hidden_width, LANES):
        part = product[:, lane : lane + LANES]
        scaled = (scale[...] * part).astype(BF16)
        for m in range(MICRO):
            d_ref[m, 0, :, lane : lane + LANES] = scaled[m * run : (m + 1) * run]
        if graded:
            held = jnp.concatenate([saved_ref[m, 0, :, lane : lane + LANES] for m in range(MICRO)], axis=0)
            total = total + part * held.astype(F32)
    if graded:
        partial[...] = total
        lane = iota((capacity, LANES), 1)
        for j, row, _, slot in places:
            parts = split(jnp.sum(partial[pl.ds(slot, capacity), :], axis=1, keepdims=True))
            table = jnp.where(lane == 0, parts[0], jnp.where(lane == 1, parts[1], parts[2]))
            grads[j][row : row + capacity, :] = table.astype(BF16)


def expert(me, blocks, weight, half, capacity, turn, saved=None, held=None):
    width, hidden_width = weight.shape
    run, rows = half * capacity, MICRO * capacity
    graded = held is None
    anywhere = pl.BlockSpec(memory_space=pl.ANY)
    side = (lambda me: me[0] // half) if graded else (lambda me: 1 - me[0] // half)
    slots = pl.BlockSpec((MICRO, 1, run, hidden_width), lambda i, me: (0, side(me), 0, 0))
    in_specs = [pl.BlockSpec(memory_space=pltpu.VMEM)] * (half + 1)
    scratch = [
        pltpu.VMEM((MICRO * run, width), BF16),
        pltpu.VMEM((MICRO * run, hidden_width), F32),
        pltpu.VMEM((MICRO * run, LANES), F32),
    ]
    if graded:
        out_shape = [jax.ShapeDtypeStruct(saved.shape, BF16)] + [jax.ShapeDtypeStruct((rows, LANES), BF16)] * half
        out_specs = [slots] + [pl.BlockSpec((rows, LANES), lambda i, me: (0, 0))] * half
        scratch.append(pltpu.VMEM((MICRO * run, LANES), F32))
        operands, in_specs, aliases = [saved], in_specs + [slots], {}
    else:
        out_shape, out_specs = [jax.ShapeDtypeStruct(held.shape, BF16)], [slots]
        operands, in_specs, aliases = [held], in_specs + [anywhere], {half + 2: 0}
    return pl.pallas_call(
        functools.partial(expert_kernel, half, capacity, turn, graded),
        grid_spec=pltpu.PrefetchScalarGridSpec(
            num_scalar_prefetch=1,
            grid=(1,),
            in_specs=in_specs,
            out_specs=out_specs,
            scratch_shapes=scratch,
        ),
        out_shape=out_shape,
        input_output_aliases=aliases,
        compiler_params=pltpu.CompilerParams(vmem_limit_bytes=VMEM_LIMIT),
        name="expert_own" if graded else "expert_far",
    )(me, *[blocks[j] for j in (OWN_ORDER if graded else FAR_ORDER)], weight, *operands)


def router_kernel(half, capacity, turn, me_ref, info_ref, *refs):
    own, (far_ref, router_ref, out_ref) = refs[:half], refs[half:]
    info = info_ref[...]
    relative = jnp.bitwise_xor(me_ref[0], iota((8, LANES), 0))
    rank, _ = ranks(info, relative)
    slot = iota((capacity, LANES), 0)
    token = iota((capacity, LANES), 1)
    far = far_ref[...].astype(F32)
    rows = []
    for j in range(2 * half):
        if j < half:
            table, lane = own[j][...].astype(F32), 0
        else:
            table, lane = far, 3 * ((j - half) ^ turn)
        column = table[:, lane : lane + 1] + table[:, lane + 1 : lane + 2] + table[:, lane + 2 : lane + 3]
        here = jnp.where(token // MB_TOK == 0, column[0:capacity], column[capacity : 2 * capacity])
        rows.append(jnp.sum(jnp.where(slot == rank[j : j + 1, :], here, 0.0), axis=0, keepdims=True))
    grads = jnp.concatenate(rows, axis=0)
    first, second = info[0:1, :].astype(jnp.int32), info[1:2, :].astype(jnp.int32)
    w_first, w_second = info[2:3, :], info[3:4, :]
    g_first = jnp.sum(jnp.where(relative == first, grads, 0.0), axis=0, keepdims=True)
    g_second = jnp.sum(jnp.where(relative == second, grads, 0.0), axis=0, keepdims=True)
    mean = w_first * g_first + w_second * g_second
    expert_rows = iota((8, LANES), 0)
    logit = jnp.where(expert_rows == first, w_first * (g_first - mean), 0.0)
    logit = logit + jnp.where(expert_rows == second, w_second * (g_second - mean), 0.0)
    parts = jnp.concatenate([*split(logit), jnp.zeros((LANES - 24, LANES), F32)], axis=0).T
    router = router_ref[...].astype(F32)
    router = jnp.concatenate([router, router, router, jnp.zeros((LANES - 24, router.shape[1]), F32)], axis=0)
    out_ref[...] = jnp.dot(parts.astype(BF16), router.astype(BF16), preferred_element_type=F32).astype(BF16)


def router(me, info, own, far, table, tokens, half, capacity, turn):
    width = tokens.shape[1]
    vmem = pl.BlockSpec(memory_space=pltpu.VMEM)
    tail = pl.BlockSpec((MICRO * capacity, LANES), lambda i: (0, width // LANES))
    return pl.pallas_call(
        functools.partial(router_kernel, half, capacity, turn),
        grid=(1,),
        out_shape=jax.ShapeDtypeStruct(tokens.shape, BF16),
        in_specs=[pl.BlockSpec(memory_space=pltpu.SMEM), vmem] + [tail] * half + [vmem] * 2,
        out_specs=vmem,
        compiler_params=pltpu.CompilerParams(vmem_limit_bytes=VMEM_LIMIT),
        name="router",
    )(me, info, *own, far, table)


def route(block, flip, back):
    sections, peers = lax.axis_size("pipe"), lax.axis_size("expert")
    pairs = [
        (p * peers + e, ((p - back) % sections) * peers + (e ^ flip)) for p in range(sections) for e in range(peers)
    ]
    return lax.ppermute(block, ("pipe", "expert"), pairs)


def by_halves(grad_sent, routes, router_probs, saved_hidden, w_down, w_router):
    peers = lax.axis_size("expert")
    half, turn = peers // 2, 2
    slots, hidden_width = saved_hidden.shape[1:]
    capacity = slots // (MICRO * peers)
    me = lax.axis_index("expert").astype(jnp.int32).reshape(1)
    tokens, weight = grad_sent[0], w_down[0]
    saved = saved_hidden.reshape(MICRO, 2, half * capacity, hidden_width)
    vmem = pl.BlockSpec(memory_space=pltpu.VMEM)

    def spread(blocks):
        return [blocks[0]] + [route(blocks[j], j, 0) for j in range(1, half)]

    info = pl.pallas_call(
        info_kernel,
        out_shape=jax.ShapeDtypeStruct((8, LANES), F32),
        in_specs=[vmem, vmem],
        out_specs=vmem,
        name="info",
    )(routes[0].T, router_probs[0].T)
    next_info = route(info, 0, -1)
    far_info = route(info, half + turn, 0)
    far_tokens = route(tokens, half + turn, 1)
    packed = pack(me, next_info, tokens, half, capacity, "pack_own")
    weight_t = turned(weight, packed[0])
    saved, packed = lax.optimization_barrier((saved, packed))
    backs = back(me, saved, weight, half, capacity, turn)
    own = [route(packed[j], j, 1) for j in range(half)]
    backs = spread(backs)
    held, *own_grads = expert(me, own, weight_t, half, capacity, 0, saved=saved)
    far = pack(me, far_info, far_tokens, half, capacity, "pack_far", own_grads)
    far_grads = route(far_grad(far, backs, half, capacity), half + turn, 0)
    far = spread(far)
    (d_hidden,) = expert(me, far, weight_t, half, capacity, turn, held=held)
    grad_in = router(me, info, far, far_grads, w_router.T, tokens, half, capacity, turn)
    return d_hidden.reshape(saved_hidden.shape), grad_in[None]


def from_behind(block, axis, distance):
    devices = range(lax.axis_size(axis))
    route = [((i - distance) % len(devices), i) for i in devices]
    return lax.ppermute(block, axis, route)


def route_slots(route_rows, peer_count, capacity):
    onehot = (route_rows[..., None] == jnp.arange(peer_count, dtype=jnp.int32)).astype(jnp.int32)
    rank_of = jnp.sum((jnp.cumsum(onehot, axis=1) - onehot) * onehot, axis=2)
    return route_rows * capacity + rank_of


def by_slots(grad_sent, routes, router_probs, saved_hidden, w_down, w_router):
    peer_count = lax.axis_size("expert")
    slot_count = saved_hidden.shape[1]
    capacity = slot_count // (MICRO * peer_count)
    send_width = peer_count * capacity
    model_width = grad_sent.shape[2]
    hidden_width = saved_hidden.shape[2]
    tokens = routes.shape[1]
    incoming = from_behind(grad_sent, "pipe", -1)[0]
    route_rows = routes[0].reshape(MICRO, MB_TOK * TOP)
    position = route_slots(route_rows, peer_count, capacity)
    chosen = jnp.take_along_axis(router_probs[0], routes[0], axis=1)
    weights = chosen / jnp.sum(chosen, axis=1, keepdims=True)
    rounded = weights.astype(jnp.bfloat16)
    micro_index = jnp.arange(MICRO, dtype=jnp.int32)[:, None]
    token_index = jnp.broadcast_to(
        jnp.arange(MB_TOK * TOP, dtype=jnp.int32)[None, :] // TOP, (MICRO, MB_TOK * TOP)
    )
    slot_token = (
        jnp.zeros((MICRO, send_width), jnp.int32).at[micro_index, position].set(token_index)
    )
    slot_used = jnp.zeros((MICRO, send_width), jnp.bool_).at[micro_index, position].set(True)
    send_scale = (
        jnp.zeros((MICRO, send_width), jnp.bfloat16)
        .at[micro_index, position]
        .set(rounded.reshape(MICRO, MB_TOK * TOP))
    )
    micro_grad = incoming.reshape(MICRO, MB_TOK, model_width)
    picked = jnp.take_along_axis(micro_grad, slot_token[..., None], axis=1)
    send_rows = jnp.where(slot_used[..., None], picked, jnp.zeros((), jnp.bfloat16))
    hidden = saved_hidden[0].reshape(MICRO, send_width, hidden_width)
    weight = w_down[0]
    arrived, arrived_scale = (
        lax.all_to_all(send_rows, "expert", split_axis=1, concat_axis=1, tiled=True),
        lax.all_to_all(send_scale, "expert", split_axis=1, concat_axis=1, tiled=True),
    )
    flat_rows = arrived.reshape(-1, model_width)
    flat_saved = hidden.reshape(flat_rows.shape[0], hidden_width)
    grad_hidden = lax.dot_general(
        flat_rows, weight, (((1,), (1,)), ((), ())), preferred_element_type=jnp.float32
    )
    route_grad = jnp.sum(grad_hidden * flat_saved.astype(jnp.float32), axis=1)
    scaled = (arrived_scale.reshape(-1, 1).astype(jnp.float32) * grad_hidden).astype(jnp.bfloat16)
    d_hidden, route_grad = (scaled, route_grad.reshape(arrived_scale.shape))
    returned = lax.all_to_all(route_grad, "expert", split_axis=1, concat_axis=1, tiled=True)
    slot_grad = jnp.take_along_axis(returned, position, axis=1).reshape(tokens, TOP)
    centred = slot_grad - jnp.sum(weights * slot_grad, axis=1, keepdims=True)
    logit_part = weights * centred
    onehot_tok = (routes[0][..., None] == jnp.arange(peer_count, dtype=jnp.int32)).astype(
        jnp.float32
    )
    logit_grad = jnp.sum(logit_part[..., None] * onehot_tok, axis=1)
    grad_in = jnp.dot(logit_grad, w_router.astype(jnp.float32).T, precision=lax.Precision.HIGHEST)
    return (d_hidden.reshape(1, slot_count, hidden_width), grad_in.astype(jnp.bfloat16)[None])


def on_device(*blocks):
    peers, slots = lax.axis_size("expert"), blocks[3].shape[1]
    capacity = slots // (MICRO * peers)
    if peers == 8 and capacity % 8 == 0 and capacity <= MB_TOK // 2:
        return by_halves(*blocks)
    return by_slots(*blocks)


def solution(mesh):
    placed = (
        P("pipe", "expert", None),
        P("pipe", "expert", None),
        P("pipe", "expert", None),
        P("pipe", "expert", None),
        P("expert", None, None),
        P(),
    )
    return jax.shard_map(
        on_device,
        mesh=mesh,
        in_specs=placed,
        out_specs=(P("pipe", "expert", None), P("pipe", "expert", None)),
        check_vma=False,
    )
```

```python
import functools

import jax
import jax.numpy as jnp
from jax import lax
from jax.experimental import pallas as pl
from jax.experimental.pallas import tpu as pltpu
from jax.sharding import PartitionSpec as P

TOP = 2
MICRO = 2
MB_TOK = 64
LANES = 128
F32, BF16 = jnp.float32, jnp.bfloat16
VMEM_LIMIT = 16 * 1024 * 1024
COLUMN = 256
SCALE = 3
OWN_ORDER, BACK_ORDER, FAR_ORDER = (0, 1, 2, 3), (0, 3, 2, 1), (0, 3, 2, 1)


def iota(shape, axis):
    return lax.broadcasted_iota(jnp.int32, shape, axis)


def info_kernel(routes_ref, probs_ref, info_ref):
    probs = probs_ref[...]
    expert = iota(probs.shape, 0)
    first, second = routes_ref[0:1, :], routes_ref[1:2, :]
    p_first = jnp.sum(jnp.where(expert == first, probs, 0.0), axis=0, keepdims=True)
    p_second = jnp.sum(jnp.where(expert == second, probs, 0.0), axis=0, keepdims=True)
    total = p_first + p_second
    info_ref[0:1, :] = first.astype(F32)
    info_ref[1:2, :] = second.astype(F32)
    info_ref[2:3, :] = p_first / total
    info_ref[3:4, :] = p_second / total
    info_ref[4:8, :] = jnp.zeros((4, LANES), F32)


def split(column):
    high = column.astype(BF16).astype(F32)
    middle = (column - high).astype(BF16).astype(F32)
    return high, middle, column - high - middle


def ranks(info, expert_rows):
    first, second = info[0:1, :].astype(jnp.int32), info[1:2, :].astype(jnp.int32)
    on_first, on_second = expert_rows == first, expert_rows == second
    named = on_first | on_second
    before = iota((LANES, LANES), 0)
    after = iota((LANES, LANES), 1)
    earlier = ((before < after) & (before // MB_TOK == after // MB_TOK)).astype(F32).astype(BF16)
    rank = jnp.dot(named.astype(F32).astype(BF16), earlier, preferred_element_type=F32)
    rank = jnp.where(named, rank.astype(jnp.int32), -1)
    weight = jnp.where(on_first, info[2:3, :], 0.0) + jnp.where(on_second, info[3:4, :], 0.0)
    return rank, weight.astype(BF16).astype(F32)


def pick(rank_row, weight_row, micro, capacity):
    slot = iota((capacity, LANES), 0)
    token = iota((capacity, LANES), 1)
    hit = (slot == rank_row) & (token // MB_TOK == micro)
    onehot = jnp.where(hit, 1.0, 0.0)
    scale = jnp.sum(jnp.where(hit, weight_row, 0.0), axis=1, keepdims=True)
    return onehot, jnp.broadcast_to(scale, (capacity, LANES))


def pack_kernel(half, capacity, me_ref, info_ref, token_ref, *refs):
    grads, outs = refs[:-half], refs[-half:]
    rows = jnp.bitwise_xor(me_ref[0], iota((8, LANES), 0))
    rank, weight = ranks(info_ref[...], rows)
    pieces, scales = [], []
    for j in range(half):
        for micro in range(MICRO):
            onehot, scale = pick(rank[j : j + 1, :], weight[j : j + 1, :], micro, capacity)
            pieces.append(onehot)
            scales.append(scale)
    width = token_ref.shape[1]
    chosen = jnp.concatenate(pieces, axis=0).astype(BF16)
    packed = jnp.dot(chosen, token_ref[...], preferred_element_type=F32).astype(BF16)
    size = MICRO * capacity
    lane = iota((size, LANES), 1)
    for j in range(half):
        outs[j][:, 0:width] = packed[j * size : (j + 1) * size]
        tail = jnp.concatenate(scales[j * MICRO : (j + 1) * MICRO], axis=0)
        if grads:
            tail = jnp.where(lane < SCALE, grads[j][...].astype(F32), tail)
        outs[j][:, width:] = tail.astype(BF16)


def pack(me, info, tokens, half, capacity, name, grads=()):
    block = jax.ShapeDtypeStruct((MICRO * capacity, tokens.shape[1] + LANES), BF16)
    vmem = pl.BlockSpec(memory_space=pltpu.VMEM)
    return pl.pallas_call(
        functools.partial(pack_kernel, half, capacity),
        out_shape=[block] * half,
        in_specs=[pl.BlockSpec(memory_space=pltpu.SMEM)] + [vmem] * (2 + len(grads)),
        out_specs=[vmem] * half,
        compiler_params=pltpu.CompilerParams(vmem_limit_bytes=VMEM_LIMIT),
        name=name,
    )(me, info, tokens, *grads)


def chunks(width):
    step = COLUMN if width % COLUMN == 0 else width
    return [pl.ds(start, step) for start in range(0, width, step)]


def back_kernel(half, capacity, turn, me_ref, saved_ref, w_ref, *refs):
    outs, product = refs[:half], refs[half]
    run = half * capacity
    saved = jnp.concatenate([saved_ref[m, 0] for m in range(MICRO)], axis=0)
    here = jnp.bitwise_xor(lax.rem(me_ref[0], half), turn)
    for columns in chunks(w_ref.shape[1]):
        product[:, columns] = jnp.dot(saved, w_ref[:, columns], preferred_element_type=F32)
    for j in range(half):
        for m in range(MICRO):
            slot = pl.multiple_of(m * run + jnp.bitwise_xor(here, j) * capacity, 8)
            outs[j][m * capacity : (m + 1) * capacity, :] = product[pl.ds(slot, capacity), :].astype(BF16)


def back(me, saved, weight, half, capacity, turn):
    hidden_width, width = weight.shape
    run, rows = half * capacity, MICRO * capacity
    return pl.pallas_call(
        functools.partial(back_kernel, half, capacity, turn),
        grid_spec=pltpu.PrefetchScalarGridSpec(
            num_scalar_prefetch=1,
            grid=(1,),
            in_specs=[
                pl.BlockSpec((MICRO, 1, run, hidden_width), lambda i, me: (0, 1 - me[0] // half, 0, 0)),
                pl.BlockSpec(memory_space=pltpu.VMEM),
            ],
            out_specs=[pl.BlockSpec((rows, width), lambda i, me: (0, 0))] * half,
            scratch_shapes=[pltpu.VMEM((MICRO * run, width), F32)],
        ),
        out_shape=[jax.ShapeDtypeStruct((rows, width), BF16)] * half,
        compiler_params=pltpu.CompilerParams(vmem_limit_bytes=VMEM_LIMIT),
        name="back",
    )(me, saved, weight)


def turn_kernel(w_ref, after_ref, out_ref):
    del after_ref
    for columns in chunks(w_ref.shape[1]):
        out_ref[columns, :] = w_ref[:, columns].T


def turned(weight, after):
    vmem = pl.BlockSpec(memory_space=pltpu.VMEM)
    return pl.pallas_call(
        turn_kernel,
        out_shape=jax.ShapeDtypeStruct(weight.shape[::-1], BF16),
        in_specs=[vmem, pl.BlockSpec(memory_space=pl.ANY)],
        out_specs=vmem,
        compiler_params=pltpu.CompilerParams(vmem_limit_bytes=VMEM_LIMIT),
        name="turned",
    )(weight, after)


def far_grad_kernel(half, capacity, *refs):
    blocks, (grad_ref,) = refs[:half], refs[2 * half :]
    backs = [refs[half + BACK_ORDER.index(j)] for j in range(half)]
    width = blocks[0].shape[1] - LANES
    rows = MICRO * capacity
    where = iota((rows, LANES), 1)
    table = jnp.zeros((rows, LANES), F32)
    for j in range(half):
        total = jnp.zeros((rows, LANES), F32)
        for lane in range(0, width, LANES):
            sent = blocks[j][:, lane : lane + LANES].astype(F32)
            total = total + sent * backs[j][:, lane : lane + LANES].astype(F32)
        for i, part in enumerate(split(jnp.sum(total, axis=1, keepdims=True))):
            table = jnp.where(where == 3 * j + i, part, table)
    grad_ref[...] = table.astype(BF16)


def far_grad(blocks, backs, half, capacity):
    vmem = pl.BlockSpec(memory_space=pltpu.VMEM)
    return pl.pallas_call(
        functools.partial(far_grad_kernel, half, capacity),
        out_shape=jax.ShapeDtypeStruct((MICRO * capacity, LANES), BF16),
        in_specs=[vmem] * (2 * half),
        out_specs=vmem,
        compiler_params=pltpu.CompilerParams(vmem_limit_bytes=VMEM_LIMIT),
        name="far_grad",
    )(*blocks, *[backs[j] for j in BACK_ORDER])


def expert_kernel(half, capacity, turn, graded, me_ref, *refs):
    order = OWN_ORDER if graded else FAR_ORDER
    blocks, w_ref, refs = [refs[order.index(j)] for j in range(half)], refs[half], refs[half + 1 :]
    if graded:
        saved_ref, d_ref, *grads, lhs, product, scale, partial = refs
    else:
        _, d_ref, lhs, product, scale = refs
    width, hidden_width = w_ref.shape
    run = half * capacity
    here = jnp.bitwise_xor(lax.rem(me_ref[0], half), turn)
    places = []
    for j in range(half):
        for m in range(MICRO):
            slot = pl.multiple_of(m * run + jnp.bitwise_xor(here, j) * capacity, 8)
            places.append((j, m * capacity, (j * MICRO + m) * capacity, slot))
    for j in range(half):
        lhs[j * MICRO * capacity : (j + 1) * MICRO * capacity, :] = blocks[j][:, 0:width]
    for j, row, _, slot in places:
        tail = blocks[j][row : row + capacity, width:].astype(F32)
        scale[pl.ds(slot, capacity), :] = jnp.broadcast_to(tail[:, SCALE : SCALE + 1], tail.shape)
    for columns in chunks(hidden_width):
        got = jnp.dot(lhs[...], w_ref[:, columns], preferred_element_type=F32)
        for _, _, begin, slot in places:
            product[pl.ds(slot, capacity), columns] = got[begin : begin + capacity, :]
    total = jnp.zeros((MICRO * run, LANES), F32)
    for lane in range(0, hidden_width, LANES):
        part = product[:, lane : lane + LANES]
        scaled = (scale[...] * part).astype(BF16)
        for m in range(MICRO):
            d_ref[m, 0, :, lane : lane + LANES] = scaled[m * run : (m + 1) * run]
        if graded:
            held = jnp.concatenate([saved_ref[m, 0, :, lane : lane + LANES] for m in range(MICRO)], axis=0)
            total = total + part * held.astype(F32)
    if graded:
        partial[...] = total
        lane = iota((capacity, LANES), 1)
        for j, row, _, slot in places:
            parts = split(jnp.sum(partial[pl.ds(slot, capacity), :], axis=1, keepdims=True))
            table = jnp.where(lane == 0, parts[0], jnp.where(lane == 1, parts[1], parts[2]))
            grads[j][row : row + capacity, :] = table.astype(BF16)


def expert(me, blocks, weight, half, capacity, turn, saved=None, held=None):
    width, hidden_width = weight.shape
    run, rows = half * capacity, MICRO * capacity
    graded = held is None
    anywhere = pl.BlockSpec(memory_space=pl.ANY)
    side = (lambda me: me[0] // half) if graded else (lambda me: 1 - me[0] // half)
    slots = pl.BlockSpec((MICRO, 1, run, hidden_width), lambda i, me: (0, side(me), 0, 0))
    in_specs = [pl.BlockSpec(memory_space=pltpu.VMEM)] * (half + 1)
    scratch = [
        pltpu.VMEM((MICRO * run, width), BF16),
        pltpu.VMEM((MICRO * run, hidden_width), F32),
        pltpu.VMEM((MICRO * run, LANES), F32),
    ]
    if graded:
        out_shape = [jax.ShapeDtypeStruct(saved.shape, BF16)] + [jax.ShapeDtypeStruct((rows, LANES), BF16)] * half
        out_specs = [slots] + [pl.BlockSpec((rows, LANES), lambda i, me: (0, 0))] * half
        scratch.append(pltpu.VMEM((MICRO * run, LANES), F32))
        operands, in_specs, aliases = [saved], in_specs + [slots], {}
    else:
        out_shape, out_specs = [jax.ShapeDtypeStruct(held.shape, BF16)], [slots]
        operands, in_specs, aliases = [held], in_specs + [anywhere], {half + 2: 0}
    return pl.pallas_call(
        functools.partial(expert_kernel, half, capacity, turn, graded),
        grid_spec=pltpu.PrefetchScalarGridSpec(
            num_scalar_prefetch=1,
            grid=(1,),
            in_specs=in_specs,
            out_specs=out_specs,
            scratch_shapes=scratch,
        ),
        out_shape=out_shape,
        input_output_aliases=aliases,
        compiler_params=pltpu.CompilerParams(vmem_limit_bytes=VMEM_LIMIT),
        name="expert_own" if graded else "expert_far",
    )(me, *[blocks[j] for j in (OWN_ORDER if graded else FAR_ORDER)], weight, *operands)


def router_rows(half, capacity, turn, me, info_ref, own, far_ref, router_ref):
    info = info_ref[...]
    relative = jnp.bitwise_xor(me, iota((8, LANES), 0))
    rank, _ = ranks(info, relative)
    slot = iota((capacity, LANES), 0)
    token = iota((capacity, LANES), 1)
    far = far_ref[...].astype(F32)
    rows = []
    for j in range(2 * half):
        if j < half:
            table, lane = own[j].astype(F32), 0
        else:
            table, lane = far, 3 * ((j - half) ^ turn)
        column = table[:, lane : lane + 1] + table[:, lane + 1 : lane + 2] + table[:, lane + 2 : lane + 3]
        here = jnp.where(token // MB_TOK == 0, column[0:capacity], column[capacity : 2 * capacity])
        rows.append(jnp.sum(jnp.where(slot == rank[j : j + 1, :], here, 0.0), axis=0, keepdims=True))
    grads = jnp.concatenate(rows, axis=0)
    first, second = info[0:1, :].astype(jnp.int32), info[1:2, :].astype(jnp.int32)
    w_first, w_second = info[2:3, :], info[3:4, :]
    g_first = jnp.sum(jnp.where(relative == first, grads, 0.0), axis=0, keepdims=True)
    g_second = jnp.sum(jnp.where(relative == second, grads, 0.0), axis=0, keepdims=True)
    mean = w_first * g_first + w_second * g_second
    expert_rows = iota((8, LANES), 0)
    logit = jnp.where(expert_rows == first, w_first * (g_first - mean), 0.0)
    logit = logit + jnp.where(expert_rows == second, w_second * (g_second - mean), 0.0)
    parts = jnp.concatenate([*split(logit), jnp.zeros((LANES - 24, LANES), F32)], axis=0).T
    router = router_ref[...].astype(F32)
    router = jnp.concatenate([router, router, router, jnp.zeros((LANES - 24, router.shape[1]), F32)], axis=0)
    return jnp.dot(parts.astype(BF16), router.astype(BF16), preferred_element_type=F32).astype(BF16)


def last_kernel(half, capacity, turn, me_ref, *refs):
    blocks, refs = [refs[FAR_ORDER.index(j)] for j in range(half)], refs[half:]
    w_ref, info_ref, far_ref, router_ref, _, d_ref, out_ref = refs[:7]
    lhs, product, scale, rows, hidden, row_sem, hidden_sem = refs[7:]
    width, hidden_width = w_ref.shape
    run, size = half * capacity, MICRO * capacity
    me = me_ref[0]
    here = jnp.bitwise_xor(lax.rem(me, half), turn)
    side = 1 - me // half
    own = [block[:, width:] for block in blocks]
    rows[...] = router_rows(half, capacity, turn, me, info_ref, own, far_ref, router_ref)
    row_copy = pltpu.make_async_copy(rows, out_ref, row_sem)
    row_copy.start()
    places = []
    for j in range(half):
        lhs[j * size : (j + 1) * size, :] = blocks[j][:, 0:width]
        for m in range(MICRO):
            slot = pl.multiple_of(m * run + jnp.bitwise_xor(here, j) * capacity, 8)
            places.append((j * size + m * capacity, slot))
            tail = own[j][m * capacity : (m + 1) * capacity].astype(F32)
            scale[pl.ds(slot, capacity), :] = jnp.broadcast_to(tail[:, SCALE : SCALE + 1], tail.shape)
    for columns in chunks(hidden_width):
        got = jnp.dot(lhs[...], w_ref[:, columns], preferred_element_type=F32)
        for begin, slot in places:
            product[pl.ds(slot, capacity), columns] = got[begin : begin + capacity, :]
    copies = []
    for m in range(MICRO):
        at = slice(m * run, (m + 1) * run)
        for lane in range(0, hidden_width, LANES):
            lanes = slice(lane, lane + LANES)
            hidden[m, :, lanes] = (scale[at, :] * product[at, lanes]).astype(BF16)
        copies.append(pltpu.make_async_copy(hidden.at[m], d_ref.at[m, side], hidden_sem.at[m]))
        copies[m].start()
    for copy in copies:
        copy.wait()
    row_copy.wait()


def last(me, blocks, weight, info, far, table, held, tokens, half, capacity, turn):
    width, hidden_width = weight.shape
    run = half * capacity
    vmem, anywhere = pl.BlockSpec(memory_space=pltpu.VMEM), pl.BlockSpec(memory_space=pl.ANY)
    return pl.pallas_call(
        functools.partial(last_kernel, half, capacity, turn),
        out_shape=[jax.ShapeDtypeStruct(held.shape, BF16), jax.ShapeDtypeStruct(tokens.shape, BF16)],
        in_specs=[pl.BlockSpec(memory_space=pltpu.SMEM)] + [vmem] * (half + 4) + [anywhere],
        out_specs=[anywhere, anywhere],
        scratch_shapes=[
            pltpu.VMEM((MICRO * run, width), BF16),
            pltpu.VMEM((MICRO * run, hidden_width), F32),
            pltpu.VMEM((MICRO * run, LANES), F32),
            pltpu.VMEM(tokens.shape, BF16),
            pltpu.VMEM((MICRO, run, hidden_width), BF16),
            pltpu.SemaphoreType.DMA,
            pltpu.SemaphoreType.DMA((MICRO,)),
        ],
        input_output_aliases={half + 5: 0},
        compiler_params=pltpu.CompilerParams(vmem_limit_bytes=VMEM_LIMIT),
        name="last",
    )(me, *[blocks[j] for j in FAR_ORDER], weight, info, far, table, held)


def route(block, flip, back):
    sections, peers = lax.axis_size("pipe"), lax.axis_size("expert")
    pairs = [
        (p * peers + e, ((p - back) % sections) * peers + (e ^ flip)) for p in range(sections) for e in range(peers)
    ]
    return lax.ppermute(block, ("pipe", "expert"), pairs)


def by_halves(grad_sent, routes, router_probs, saved_hidden, w_down, w_router):
    peers = lax.axis_size("expert")
    half, turn = peers // 2, 2
    slots, hidden_width = saved_hidden.shape[1:]
    capacity = slots // (MICRO * peers)
    me = lax.axis_index("expert").astype(jnp.int32).reshape(1)
    tokens, weight = grad_sent[0], w_down[0]
    saved = saved_hidden.reshape(MICRO, 2, half * capacity, hidden_width)
    vmem = pl.BlockSpec(memory_space=pltpu.VMEM)

    def spread(blocks):
        return [blocks[0]] + [route(blocks[j], j, 0) for j in range(1, half)]

    info = pl.pallas_call(
        info_kernel,
        out_shape=jax.ShapeDtypeStruct((8, LANES), F32),
        in_specs=[vmem, vmem],
        out_specs=vmem,
        name="info",
    )(routes[0].T, router_probs[0].T)
    next_info = route(info, 0, -1)
    far_info = route(info, half + turn, 0)
    far_tokens = route(tokens, half + turn, 1)
    packed = pack(me, next_info, tokens, half, capacity, "pack_own")
    weight_t = turned(weight, packed[0])
    saved, packed = lax.optimization_barrier((saved, packed))
    backs = back(me, saved, weight, half, capacity, turn)
    own = [route(packed[j], j, 1) for j in range(half)]
    backs = spread(backs)
    held, *own_grads = expert(me, own, weight_t, half, capacity, 0, saved=saved)
    far = pack(me, far_info, far_tokens, half, capacity, "pack_far", own_grads)
    far_grads = route(far_grad(far, backs, half, capacity), half + turn, 0)
    far = spread(far)
    d_hidden, grad_in = last(me, far, weight_t, info, far_grads, w_router.T, held, tokens, half, capacity, turn)
    return d_hidden.reshape(saved_hidden.shape), grad_in[None]


def from_behind(block, axis, distance):
    devices = range(lax.axis_size(axis))
    route = [((i - distance) % len(devices), i) for i in devices]
    return lax.ppermute(block, axis, route)


def route_slots(route_rows, peer_count, capacity):
    onehot = (route_rows[..., None] == jnp.arange(peer_count, dtype=jnp.int32)).astype(jnp.int32)
    rank_of = jnp.sum((jnp.cumsum(onehot, axis=1) - onehot) * onehot, axis=2)
    return route_rows * capacity + rank_of


def by_slots(grad_sent, routes, router_probs, saved_hidden, w_down, w_router):
    peer_count = lax.axis_size("expert")
    slot_count = saved_hidden.shape[1]
    capacity = slot_count // (MICRO * peer_count)
    send_width = peer_count * capacity
    model_width = grad_sent.shape[2]
    hidden_width = saved_hidden.shape[2]
    tokens = routes.shape[1]
    incoming = from_behind(grad_sent, "pipe", -1)[0]
    route_rows = routes[0].reshape(MICRO, MB_TOK * TOP)
    position = route_slots(route_rows, peer_count, capacity)
    chosen = jnp.take_along_axis(router_probs[0], routes[0], axis=1)
    weights = chosen / jnp.sum(chosen, axis=1, keepdims=True)
    rounded = weights.astype(jnp.bfloat16)
    micro_index = jnp.arange(MICRO, dtype=jnp.int32)[:, None]
    token_index = jnp.broadcast_to(
        jnp.arange(MB_TOK * TOP, dtype=jnp.int32)[None, :] // TOP, (MICRO, MB_TOK * TOP)
    )
    slot_token = (
        jnp.zeros((MICRO, send_width), jnp.int32).at[micro_index, position].set(token_index)
    )
    slot_used = jnp.zeros((MICRO, send_width), jnp.bool_).at[micro_index, position].set(True)
    send_scale = (
        jnp.zeros((MICRO, send_width), jnp.bfloat16)
        .at[micro_index, position]
        .set(rounded.reshape(MICRO, MB_TOK * TOP))
    )
    micro_grad = incoming.reshape(MICRO, MB_TOK, model_width)
    picked = jnp.take_along_axis(micro_grad, slot_token[..., None], axis=1)
    send_rows = jnp.where(slot_used[..., None], picked, jnp.zeros((), jnp.bfloat16))
    hidden = saved_hidden[0].reshape(MICRO, send_width, hidden_width)
    weight = w_down[0]
    arrived, arrived_scale = (
        lax.all_to_all(send_rows, "expert", split_axis=1, concat_axis=1, tiled=True),
        lax.all_to_all(send_scale, "expert", split_axis=1, concat_axis=1, tiled=True),
    )
    flat_rows = arrived.reshape(-1, model_width)
    flat_saved = hidden.reshape(flat_rows.shape[0], hidden_width)
    grad_hidden = lax.dot_general(
        flat_rows, weight, (((1,), (1,)), ((), ())), preferred_element_type=jnp.float32
    )
    route_grad = jnp.sum(grad_hidden * flat_saved.astype(jnp.float32), axis=1)
    scaled = (arrived_scale.reshape(-1, 1).astype(jnp.float32) * grad_hidden).astype(jnp.bfloat16)
    d_hidden, route_grad = (scaled, route_grad.reshape(arrived_scale.shape))
    returned = lax.all_to_all(route_grad, "expert", split_axis=1, concat_axis=1, tiled=True)
    slot_grad = jnp.take_along_axis(returned, position, axis=1).reshape(tokens, TOP)
    centred = slot_grad - jnp.sum(weights * slot_grad, axis=1, keepdims=True)
    logit_part = weights * centred
    onehot_tok = (routes[0][..., None] == jnp.arange(peer_count, dtype=jnp.int32)).astype(
        jnp.float32
    )
    logit_grad = jnp.sum(logit_part[..., None] * onehot_tok, axis=1)
    grad_in = jnp.dot(logit_grad, w_router.astype(jnp.float32).T, precision=lax.Precision.HIGHEST)
    return (d_hidden.reshape(1, slot_count, hidden_width), grad_in.astype(jnp.bfloat16)[None])


def on_device(*blocks):
    peers, slots = lax.axis_size("expert"), blocks[3].shape[1]
    capacity = slots // (MICRO * peers)
    if peers == 8 and capacity % 8 == 0 and capacity <= MB_TOK // 2:
        return by_halves(*blocks)
    return by_slots(*blocks)


def solution(mesh):
    placed = (
        P("pipe", "expert", None),
        P("pipe", "expert", None),
        P("pipe", "expert", None),
        P("pipe", "expert", None),
        P("expert", None, None),
        P(),
    )
    return jax.shard_map(
        on_device,
        mesh=mesh,
        in_specs=placed,
        out_specs=(P("pipe", "expert", None), P("pipe", "expert", None)),
        check_vma=False,
    )
```

```python
import functools

import jax
import jax.numpy as jnp
from jax import lax
from jax.experimental import pallas as pl
from jax.experimental.pallas import tpu as pltpu
from jax.sharding import PartitionSpec as P

TOP = 2
MICRO = 2
MB_TOK = 64
LANES = 128
F32, BF16 = jnp.float32, jnp.bfloat16
VMEM_LIMIT = 16 * 1024 * 1024
COLUMN = 256
SCALE = 4
OWN_ORDER, BACK_ORDER, FAR_ORDER = (0, 1, 2, 3), (0, 3, 2, 1), (0, 3, 2, 1)


def iota(shape, axis):
    return lax.broadcasted_iota(jnp.int32, shape, axis)


def info_kernel(routes_ref, probs_ref, info_ref):
    probs = probs_ref[...]
    expert = iota(probs.shape, 0)
    first, second = routes_ref[0:1, :], routes_ref[1:2, :]
    p_first = jnp.sum(jnp.where(expert == first, probs, 0.0), axis=0, keepdims=True)
    p_second = jnp.sum(jnp.where(expert == second, probs, 0.0), axis=0, keepdims=True)
    total = p_first + p_second
    info_ref[0:1, :] = first.astype(F32)
    info_ref[1:2, :] = second.astype(F32)
    info_ref[2:3, :] = p_first / total
    info_ref[3:4, :] = p_second / total
    info_ref[4:8, :] = jnp.zeros((4, LANES), F32)


def split(column):
    high = column.astype(BF16).astype(F32)
    middle = (column - high).astype(BF16).astype(F32)
    return high, middle, column - high - middle


def ranks(info, expert_rows):
    first, second = info[0:1, :].astype(jnp.int32), info[1:2, :].astype(jnp.int32)
    on_first, on_second = expert_rows == first, expert_rows == second
    named = on_first | on_second
    before = iota((LANES, LANES), 0)
    after = iota((LANES, LANES), 1)
    earlier = ((before < after) & (before // MB_TOK == after // MB_TOK)).astype(F32).astype(BF16)
    rank = jnp.dot(named.astype(F32).astype(BF16), earlier, preferred_element_type=F32)
    rank = jnp.where(named, rank.astype(jnp.int32), -1)
    weight = jnp.where(on_first, info[2:3, :], 0.0) + jnp.where(on_second, info[3:4, :], 0.0)
    return rank, weight.astype(BF16).astype(F32)


def pick(rank_row, weight_row, micro, capacity):
    slot = iota((capacity, LANES), 0)
    token = iota((capacity, LANES), 1)
    hit = (slot == rank_row) & (token // MB_TOK == micro)
    onehot = jnp.where(hit, 1.0, 0.0)
    scale = jnp.sum(jnp.where(hit, weight_row, 0.0), axis=1, keepdims=True)
    return onehot, jnp.broadcast_to(scale, (capacity, LANES))


def pack_kernel(half, capacity, me_ref, info_ref, token_ref, *refs):
    grads, outs = refs[:-half], refs[-half:]
    rows = jnp.bitwise_xor(me_ref[0], iota((8, LANES), 0))
    rank, weight = ranks(info_ref[...], rows)
    pieces, scales = [], []
    for j in range(half):
        for micro in range(MICRO):
            onehot, scale = pick(rank[j : j + 1, :], weight[j : j + 1, :], micro, capacity)
            pieces.append(onehot)
            scales.append(scale)
    width = token_ref.shape[1]
    chosen = jnp.concatenate(pieces, axis=0).astype(BF16)
    packed = jnp.dot(chosen, token_ref[...], preferred_element_type=F32).astype(BF16)
    size = MICRO * capacity
    lane = iota((size, LANES), 1)
    for j in range(half):
        outs[j][:, 0:width] = packed[j * size : (j + 1) * size]
        if grads:
            tail = jnp.concatenate(scales[j * MICRO : (j + 1) * MICRO], axis=0)
            outs[j][:, width:] = jnp.where(lane < SCALE, grads[j][...].astype(F32), tail).astype(BF16)


def pack(me, info, tokens, half, capacity, name, grads=()):
    block = jax.ShapeDtypeStruct((MICRO * capacity, tokens.shape[1] + LANES * bool(grads)), BF16)
    vmem = pl.BlockSpec(memory_space=pltpu.VMEM)
    return pl.pallas_call(
        functools.partial(pack_kernel, half, capacity),
        out_shape=[block] * half,
        in_specs=[pl.BlockSpec(memory_space=pltpu.SMEM)] + [vmem] * (2 + len(grads)),
        out_specs=[vmem] * half,
        compiler_params=pltpu.CompilerParams(vmem_limit_bytes=VMEM_LIMIT),
        name=name,
    )(me, info, tokens, *grads)


def chunks(width):
    step = COLUMN if width % COLUMN == 0 else width
    return [pl.ds(start, step) for start in range(0, width, step)]


def back_kernel(half, capacity, turn, me_ref, saved_ref, w_ref, *refs):
    outs, product = refs[:half], refs[half]
    run = half * capacity
    saved = jnp.concatenate([saved_ref[m, 0] for m in range(MICRO)], axis=0)
    here = jnp.bitwise_xor(lax.rem(me_ref[0], half), turn)
    for columns in chunks(w_ref.shape[1]):
        product[:, columns] = jnp.dot(saved, w_ref[:, columns], preferred_element_type=F32)
    for j in range(half):
        for m in range(MICRO):
            slot = pl.multiple_of(m * run + jnp.bitwise_xor(here, j) * capacity, 8)
            outs[j][m * capacity : (m + 1) * capacity, :] = product[pl.ds(slot, capacity), :].astype(BF16)


def back(me, saved, weight, half, capacity, turn):
    hidden_width, width = weight.shape
    run, rows = half * capacity, MICRO * capacity
    return pl.pallas_call(
        functools.partial(back_kernel, half, capacity, turn),
        grid_spec=pltpu.PrefetchScalarGridSpec(
            num_scalar_prefetch=1,
            grid=(1,),
            in_specs=[
                pl.BlockSpec((MICRO, 1, run, hidden_width), lambda i, me: (0, 1 - me[0] // half, 0, 0)),
                pl.BlockSpec(memory_space=pltpu.VMEM),
            ],
            out_specs=[pl.BlockSpec((rows, width), lambda i, me: (0, 0))] * half,
            scratch_shapes=[pltpu.VMEM((MICRO * run, width), F32)],
        ),
        out_shape=[jax.ShapeDtypeStruct((rows, width), BF16)] * half,
        compiler_params=pltpu.CompilerParams(vmem_limit_bytes=VMEM_LIMIT),
        name="back",
    )(me, saved, weight)


def turn_kernel(half, capacity, me_ref, w_ref, info_ref, after_ref, out_ref, scale_ref):
    del after_ref
    for columns in chunks(w_ref.shape[1]):
        out_ref[columns, :] = w_ref[:, columns].T
    rank, weight = ranks(info_ref[...], jnp.bitwise_xor(me_ref[0], iota((8, LANES), 0)))
    for j in range(half):
        for m in range(MICRO):
            _, scale = pick(rank[j : j + 1, :], weight[j : j + 1, :], m, capacity)
            scale_ref[j, m * capacity : (m + 1) * capacity, :] = scale


def turned(me, weight, info, after, half, capacity):
    vmem = pl.BlockSpec(memory_space=pltpu.VMEM)
    return pl.pallas_call(
        functools.partial(turn_kernel, half, capacity),
        out_shape=[
            jax.ShapeDtypeStruct(weight.shape[::-1], BF16),
            jax.ShapeDtypeStruct((half, MICRO * capacity, LANES), F32),
        ],
        in_specs=[pl.BlockSpec(memory_space=pltpu.SMEM), vmem, vmem, pl.BlockSpec(memory_space=pl.ANY)],
        out_specs=[vmem, vmem],
        compiler_params=pltpu.CompilerParams(vmem_limit_bytes=VMEM_LIMIT),
        name="turned",
    )(me, weight, info, after)


def far_grad_kernel(half, capacity, *refs):
    blocks, (grad_ref,) = refs[:half], refs[2 * half :]
    backs = [refs[half + BACK_ORDER.index(j)] for j in range(half)]
    width = blocks[0].shape[1] - LANES
    rows = MICRO * capacity
    where = iota((rows, LANES), 1)
    table = jnp.zeros((rows, LANES), F32)
    for j in range(half):
        total = jnp.zeros((rows, LANES), F32)
        for lane in range(0, width, LANES):
            sent = blocks[j][:, lane : lane + LANES].astype(F32)
            total = total + sent * backs[j][:, lane : lane + LANES].astype(F32)
        for i, part in enumerate(split(jnp.sum(total, axis=1, keepdims=True))):
            table = jnp.where(where == 3 * j + i, part, table)
    grad_ref[...] = table.astype(BF16)


def far_grad(blocks, backs, half, capacity):
    vmem = pl.BlockSpec(memory_space=pltpu.VMEM)
    return pl.pallas_call(
        functools.partial(far_grad_kernel, half, capacity),
        out_shape=jax.ShapeDtypeStruct((MICRO * capacity, LANES), BF16),
        in_specs=[vmem] * (2 * half),
        out_specs=vmem,
        compiler_params=pltpu.CompilerParams(vmem_limit_bytes=VMEM_LIMIT),
        name="far_grad",
    )(*blocks, *[backs[j] for j in BACK_ORDER])


def own_kernel(half, capacity, me_ref, *refs):
    blocks, refs = [refs[OWN_ORDER.index(j)] for j in range(half)], refs[half:]
    w_ref, saved_ref, scale_ref, product, grads = refs[0], refs[1], refs[2], refs[3], refs[4 : 4 + half]
    lhs, partial = refs[4 + half :]
    hidden_width = w_ref.shape[1]
    run, size = half * capacity, MICRO * capacity
    me = me_ref[0]
    here, side = lax.rem(me, half), me // half
    places = []
    for j in range(half):
        lhs[j * size : (j + 1) * size, :] = blocks[j][...]
        for m in range(MICRO):
            slot = pl.multiple_of(m * run + jnp.bitwise_xor(here, j) * capacity, 8)
            places.append((j, m * capacity, slot))
    for columns in chunks(hidden_width):
        got = jnp.dot(lhs[...], w_ref[:, columns], preferred_element_type=F32)
        for j, row, slot in places:
            product[pl.ds(slot, capacity), columns] = got[j * size + row : j * size + row + capacity, :]
    for m in range(MICRO):
        total = jnp.zeros((run, LANES), F32)
        for lane in range(0, hidden_width, LANES):
            held = saved_ref[m, side, :, lane : lane + LANES].astype(F32)
            total = total + product[m * run : (m + 1) * run, lane : lane + LANES] * held
        partial[m * run : (m + 1) * run, :] = total
    lane = iota((capacity, LANES), 1)
    for j, row, slot in places:
        parts = split(jnp.sum(partial[pl.ds(slot, capacity), :], axis=1, keepdims=True))
        table = scale_ref[j, row : row + capacity, :]
        for i, part in enumerate(parts):
            table = jnp.where(lane == i, part, table)
        grads[j][row : row + capacity, :] = table.astype(BF16)


def own_expert(me, blocks, weight, saved, scales, half, capacity):
    width, hidden_width = weight.shape
    rows = MICRO * capacity
    vmem = pl.BlockSpec(memory_space=pltpu.VMEM)
    return pl.pallas_call(
        functools.partial(own_kernel, half, capacity),
        out_shape=[jax.ShapeDtypeStruct((half * rows, hidden_width), F32)]
        + [jax.ShapeDtypeStruct((rows, LANES), BF16)] * half,
        in_specs=[pl.BlockSpec(memory_space=pltpu.SMEM)] + [vmem] * (half + 3),
        out_specs=[vmem] * (1 + half),
        scratch_shapes=[pltpu.VMEM((half * rows, width), BF16), pltpu.VMEM((half * rows, LANES), F32)],
        compiler_params=pltpu.CompilerParams(vmem_limit_bytes=VMEM_LIMIT),
        name="own_expert",
    )(me, *[blocks[j] for j in OWN_ORDER], weight, saved, scales)


def router_rows(half, capacity, turn, me, info_ref, own, far_ref, router_ref):
    info = info_ref[...]
    relative = jnp.bitwise_xor(me, iota((8, LANES), 0))
    rank, _ = ranks(info, relative)
    slot = iota((capacity, LANES), 0)
    token = iota((capacity, LANES), 1)
    far = far_ref[...].astype(F32)
    rows = []
    for j in range(2 * half):
        if j < half:
            table, lane = own[j].astype(F32), 0
        else:
            table, lane = far, 3 * ((j - half) ^ turn)
        column = table[:, lane : lane + 1] + table[:, lane + 1 : lane + 2] + table[:, lane + 2 : lane + 3]
        here = jnp.where(token // MB_TOK == 0, column[0:capacity], column[capacity : 2 * capacity])
        rows.append(jnp.sum(jnp.where(slot == rank[j : j + 1, :], here, 0.0), axis=0, keepdims=True))
    grads = jnp.concatenate(rows, axis=0)
    first, second = info[0:1, :].astype(jnp.int32), info[1:2, :].astype(jnp.int32)
    w_first, w_second = info[2:3, :], info[3:4, :]
    g_first = jnp.sum(jnp.where(relative == first, grads, 0.0), axis=0, keepdims=True)
    g_second = jnp.sum(jnp.where(relative == second, grads, 0.0), axis=0, keepdims=True)
    mean = w_first * g_first + w_second * g_second
    expert_rows = iota((8, LANES), 0)
    logit = jnp.where(expert_rows == first, w_first * (g_first - mean), 0.0)
    logit = logit + jnp.where(expert_rows == second, w_second * (g_second - mean), 0.0)
    parts = jnp.concatenate([*split(logit), jnp.zeros((LANES - 24, LANES), F32)], axis=0).T
    router = router_ref[...].astype(F32)
    router = jnp.concatenate([router, router, router, jnp.zeros((LANES - 24, router.shape[1]), F32)], axis=0)
    return jnp.dot(parts.astype(BF16), router.astype(BF16), preferred_element_type=F32).astype(BF16)


def last_kernel(half, capacity, turn, me_ref, *refs):
    blocks, refs = [refs[FAR_ORDER.index(j)] for j in range(half)], refs[half:]
    w_ref, own_ref, info_ref, far_ref, router_ref, d_ref, out_ref = refs[:7]
    lhs, product, scale, rows, hidden, row_sem, hidden_sem = refs[7:]
    width, hidden_width = w_ref.shape
    run, size = half * capacity, MICRO * capacity
    me = me_ref[0]
    side = me // half
    tails = [block[:, width:] for block in blocks]
    rows[...] = router_rows(half, capacity, turn, me, info_ref, tails, far_ref, router_ref)
    copies = [pltpu.make_async_copy(rows, out_ref, row_sem)]
    copies[0].start()
    here = lax.rem(me, half)

    def scaled(far, source, lane_of, slots):
        for j in range(half):
            for m in range(MICRO):
                tail = tails[j][m * capacity : (m + 1) * capacity].astype(F32)
                column = jnp.broadcast_to(tail[:, lane_of : lane_of + 1], tail.shape)
                scale[pl.ds(slots[j][m], capacity), :] = column
        for m in range(MICRO):
            at = slice(m * run, (m + 1) * run)
            for lane in range(0, hidden_width, LANES):
                lanes = slice(lane, lane + LANES)
                hidden[far, m, :, lanes] = (scale[at, :] * source[at, lanes]).astype(BF16)
            to = d_ref.at[m, 1 - side if far else side]
            copies.append(pltpu.make_async_copy(hidden.at[far, m], to, hidden_sem.at[far, m]))
            copies[-1].start()

    def slots_of(first):
        return [
            [pl.multiple_of(m * run + jnp.bitwise_xor(first, j) * capacity, 8) for m in range(MICRO)] for j in range(half)
        ]

    scaled(0, own_ref, SCALE - 1, slots_of(here))
    far_slots = slots_of(jnp.bitwise_xor(here, turn))
    for j in range(half):
        lhs[j * size : (j + 1) * size, :] = blocks[j][:, 0:width]
    for columns in chunks(hidden_width):
        got = jnp.dot(lhs[...], w_ref[:, columns], preferred_element_type=F32)
        for j in range(half):
            for m in range(MICRO):
                begin = j * size + m * capacity
                product[pl.ds(far_slots[j][m], capacity), columns] = got[begin : begin + capacity, :]
    scaled(1, product, SCALE, far_slots)
    for copy in copies:
        copy.wait()


def last(me, blocks, weight, own, info, far, table, saved, tokens, half, capacity, turn):
    width, hidden_width = weight.shape
    run = half * capacity
    vmem, anywhere = pl.BlockSpec(memory_space=pltpu.VMEM), pl.BlockSpec(memory_space=pl.ANY)
    return pl.pallas_call(
        functools.partial(last_kernel, half, capacity, turn),
        out_shape=[jax.ShapeDtypeStruct(saved.shape, BF16), jax.ShapeDtypeStruct(tokens.shape, BF16)],
        in_specs=[pl.BlockSpec(memory_space=pltpu.SMEM)] + [vmem] * (half + 5),
        out_specs=[anywhere, anywhere],
        scratch_shapes=[
            pltpu.VMEM((MICRO * run, width), BF16),
            pltpu.VMEM((MICRO * run, hidden_width), F32),
            pltpu.VMEM((MICRO * run, LANES), F32),
            pltpu.VMEM(tokens.shape, BF16),
            pltpu.VMEM((2, MICRO, run, hidden_width), BF16),
            pltpu.SemaphoreType.DMA,
            pltpu.SemaphoreType.DMA((2, MICRO)),
        ],
        compiler_params=pltpu.CompilerParams(vmem_limit_bytes=VMEM_LIMIT),
        name="last",
    )(me, *[blocks[j] for j in FAR_ORDER], weight, own, info, far, table)


def route(block, flip, back):
    sections, peers = lax.axis_size("pipe"), lax.axis_size("expert")
    pairs = [
        (p * peers + e, ((p - back) % sections) * peers + (e ^ flip)) for p in range(sections) for e in range(peers)
    ]
    return lax.ppermute(block, ("pipe", "expert"), pairs)


def by_halves(grad_sent, routes, router_probs, saved_hidden, w_down, w_router):
    peers = lax.axis_size("expert")
    half, turn = peers // 2, 2
    slots, hidden_width = saved_hidden.shape[1:]
    capacity = slots // (MICRO * peers)
    me = lax.axis_index("expert").astype(jnp.int32).reshape(1)
    tokens, weight = grad_sent[0], w_down[0]
    saved = saved_hidden.reshape(MICRO, 2, half * capacity, hidden_width)
    vmem = pl.BlockSpec(memory_space=pltpu.VMEM)

    def spread(blocks):
        return [blocks[0]] + [route(blocks[j], j, 0) for j in range(1, half)]

    info = pl.pallas_call(
        info_kernel,
        out_shape=jax.ShapeDtypeStruct((8, LANES), F32),
        in_specs=[vmem, vmem],
        out_specs=vmem,
        name="info",
    )(routes[0].T, router_probs[0].T)
    next_info = route(info, 0, -1)
    far_info = route(info, half + turn, 0)
    far_tokens = route(tokens, half + turn, 1)
    packed = pack(me, next_info, tokens, half, capacity, "pack_own")
    weight_t, scales = turned(me, weight, info, packed[0], half, capacity)
    saved, packed = lax.optimization_barrier((saved, packed))
    backs = back(me, saved, weight, half, capacity, turn)
    own = [route(packed[j], j, 1) for j in range(half)]
    backs = spread(backs)
    own_product, *own_grads = own_expert(me, own, weight_t, saved, scales, half, capacity)
    far = pack(me, far_info, far_tokens, half, capacity, "pack_far", own_grads)
    far_grads = route(far_grad(far, backs, half, capacity), half + turn, 0)
    far = spread(far)
    d_hidden, grad_in = last(
        me, far, weight_t, own_product, info, far_grads, w_router.T, saved, tokens, half, capacity, turn
    )
    return d_hidden.reshape(saved_hidden.shape), grad_in[None]


def from_behind(block, axis, distance):
    devices = range(lax.axis_size(axis))
    route = [((i - distance) % len(devices), i) for i in devices]
    return lax.ppermute(block, axis, route)


def route_slots(route_rows, peer_count, capacity):
    onehot = (route_rows[..., None] == jnp.arange(peer_count, dtype=jnp.int32)).astype(jnp.int32)
    rank_of = jnp.sum((jnp.cumsum(onehot, axis=1) - onehot) * onehot, axis=2)
    return route_rows * capacity + rank_of


def by_slots(grad_sent, routes, router_probs, saved_hidden, w_down, w_router):
    peer_count = lax.axis_size("expert")
    slot_count = saved_hidden.shape[1]
    capacity = slot_count // (MICRO * peer_count)
    send_width = peer_count * capacity
    model_width = grad_sent.shape[2]
    hidden_width = saved_hidden.shape[2]
    tokens = routes.shape[1]
    incoming = from_behind(grad_sent, "pipe", -1)[0]
    route_rows = routes[0].reshape(MICRO, MB_TOK * TOP)
    position = route_slots(route_rows, peer_count, capacity)
    chosen = jnp.take_along_axis(router_probs[0], routes[0], axis=1)
    weights = chosen / jnp.sum(chosen, axis=1, keepdims=True)
    rounded = weights.astype(jnp.bfloat16)
    micro_index = jnp.arange(MICRO, dtype=jnp.int32)[:, None]
    token_index = jnp.broadcast_to(
        jnp.arange(MB_TOK * TOP, dtype=jnp.int32)[None, :] // TOP, (MICRO, MB_TOK * TOP)
    )
    slot_token = (
        jnp.zeros((MICRO, send_width), jnp.int32).at[micro_index, position].set(token_index)
    )
    slot_used = jnp.zeros((MICRO, send_width), jnp.bool_).at[micro_index, position].set(True)
    send_scale = (
        jnp.zeros((MICRO, send_width), jnp.bfloat16)
        .at[micro_index, position]
        .set(rounded.reshape(MICRO, MB_TOK * TOP))
    )
    micro_grad = incoming.reshape(MICRO, MB_TOK, model_width)
    picked = jnp.take_along_axis(micro_grad, slot_token[..., None], axis=1)
    send_rows = jnp.where(slot_used[..., None], picked, jnp.zeros((), jnp.bfloat16))
    hidden = saved_hidden[0].reshape(MICRO, send_width, hidden_width)
    weight = w_down[0]
    arrived, arrived_scale = (
        lax.all_to_all(send_rows, "expert", split_axis=1, concat_axis=1, tiled=True),
        lax.all_to_all(send_scale, "expert", split_axis=1, concat_axis=1, tiled=True),
    )
    flat_rows = arrived.reshape(-1, model_width)
    flat_saved = hidden.reshape(flat_rows.shape[0], hidden_width)
    grad_hidden = lax.dot_general(
        flat_rows, weight, (((1,), (1,)), ((), ())), preferred_element_type=jnp.float32
    )
    route_grad = jnp.sum(grad_hidden * flat_saved.astype(jnp.float32), axis=1)
    scaled = (arrived_scale.reshape(-1, 1).astype(jnp.float32) * grad_hidden).astype(jnp.bfloat16)
    d_hidden, route_grad = (scaled, route_grad.reshape(arrived_scale.shape))
    returned = lax.all_to_all(route_grad, "expert", split_axis=1, concat_axis=1, tiled=True)
    slot_grad = jnp.take_along_axis(returned, position, axis=1).reshape(tokens, TOP)
    centred = slot_grad - jnp.sum(weights * slot_grad, axis=1, keepdims=True)
    logit_part = weights * centred
    onehot_tok = (routes[0][..., None] == jnp.arange(peer_count, dtype=jnp.int32)).astype(
        jnp.float32
    )
    logit_grad = jnp.sum(logit_part[..., None] * onehot_tok, axis=1)
    grad_in = jnp.dot(logit_grad, w_router.astype(jnp.float32).T, precision=lax.Precision.HIGHEST)
    return (d_hidden.reshape(1, slot_count, hidden_width), grad_in.astype(jnp.bfloat16)[None])


def on_device(*blocks):
    peers, slots = lax.axis_size("expert"), blocks[3].shape[1]
    capacity = slots // (MICRO * peers)
    if peers == 8 and capacity % 8 == 0 and capacity <= MB_TOK // 2:
        return by_halves(*blocks)
    return by_slots(*blocks)


def solution(mesh):
    placed = (
        P("pipe", "expert", None),
        P("pipe", "expert", None),
        P("pipe", "expert", None),
        P("pipe", "expert", None),
        P("expert", None, None),
        P(),
    )
    return jax.shard_map(
        on_device,
        mesh=mesh,
        in_specs=placed,
        out_specs=(P("pipe", "expert", None), P("pipe", "expert", None)),
        check_vma=False,
    )
```

```python
import functools

import jax
import jax.numpy as jnp
from jax import lax
from jax.experimental import pallas as pl
from jax.experimental.pallas import tpu as pltpu
from jax.sharding import PartitionSpec as P

TOP = 2
MICRO = 2
MB_TOK = 64
LANES = 128
F32, BF16 = jnp.float32, jnp.bfloat16
VMEM_LIMIT = 16 * 1024 * 1024
COLUMN = 256
SCALE = 4
OWN_ORDER, BACK_ORDER, FAR_ORDER = (0, 1, 2, 3), (0, 3, 2, 1), (0, 3, 2, 1)


def iota(shape, axis):
    return lax.broadcasted_iota(jnp.int32, shape, axis)


def info_kernel(routes_ref, probs_ref, info_ref):
    probs = probs_ref[...]
    expert = iota(probs.shape, 0)
    first, second = routes_ref[0:1, :], routes_ref[1:2, :]
    p_first = jnp.sum(jnp.where(expert == first, probs, 0.0), axis=0, keepdims=True)
    p_second = jnp.sum(jnp.where(expert == second, probs, 0.0), axis=0, keepdims=True)
    total = p_first + p_second
    info_ref[0:1, :] = first.astype(F32)
    info_ref[1:2, :] = second.astype(F32)
    info_ref[2:3, :] = p_first / total
    info_ref[3:4, :] = p_second / total
    info_ref[4:8, :] = jnp.zeros((4, LANES), F32)


def split(column):
    high = column.astype(BF16).astype(F32)
    middle = (column - high).astype(BF16).astype(F32)
    return high, middle, column - high - middle


def ranks(info, expert_rows):
    first, second = info[0:1, :].astype(jnp.int32), info[1:2, :].astype(jnp.int32)
    on_first, on_second = expert_rows == first, expert_rows == second
    named = on_first | on_second
    before = iota((LANES, LANES), 0)
    after = iota((LANES, LANES), 1)
    earlier = ((before < after) & (before // MB_TOK == after // MB_TOK)).astype(F32).astype(BF16)
    rank = jnp.dot(named.astype(F32).astype(BF16), earlier, preferred_element_type=F32)
    rank = jnp.where(named, rank.astype(jnp.int32), -1)
    weight = jnp.where(on_first, info[2:3, :], 0.0) + jnp.where(on_second, info[3:4, :], 0.0)
    return rank, weight.astype(BF16).astype(F32)


def pick(rank_row, weight_row, micro, capacity):
    slot = iota((capacity, LANES), 0)
    token = iota((capacity, LANES), 1)
    hit = (slot == rank_row) & (token // MB_TOK == micro)
    onehot = jnp.where(hit, 1.0, 0.0)
    scale = jnp.sum(jnp.where(hit, weight_row, 0.0), axis=1, keepdims=True)
    return onehot, jnp.broadcast_to(scale, (capacity, LANES))


def pack_kernel(half, capacity, me_ref, info_ref, token_ref, *refs):
    grads, outs = refs[:-half], refs[-half:]
    rows = jnp.bitwise_xor(me_ref[0], iota((8, LANES), 0))
    rank, weight = ranks(info_ref[...], rows)
    pieces, scales = [], []
    for j in range(half):
        for micro in range(MICRO):
            onehot, scale = pick(rank[j : j + 1, :], weight[j : j + 1, :], micro, capacity)
            pieces.append(onehot)
            scales.append(scale)
    width = token_ref.shape[1]
    chosen = jnp.concatenate(pieces, axis=0).astype(BF16)
    packed = jnp.dot(chosen, token_ref[...], preferred_element_type=F32).astype(BF16)
    size = MICRO * capacity
    lane = iota((size, LANES), 1)
    for j in range(half):
        outs[j][:, 0:width] = packed[j * size : (j + 1) * size]
        if grads:
            tail = jnp.concatenate(scales[j * MICRO : (j + 1) * MICRO], axis=0)
            outs[j][:, width:] = jnp.where(lane < SCALE, grads[j][...].astype(F32), tail).astype(BF16)


def pack(me, info, tokens, half, capacity, name, grads=()):
    block = jax.ShapeDtypeStruct((MICRO * capacity, tokens.shape[1] + LANES * bool(grads)), BF16)
    vmem = pl.BlockSpec(memory_space=pltpu.VMEM)
    return pl.pallas_call(
        functools.partial(pack_kernel, half, capacity),
        out_shape=[block] * half,
        in_specs=[pl.BlockSpec(memory_space=pltpu.SMEM)] + [vmem] * (2 + len(grads)),
        out_specs=[vmem] * half,
        compiler_params=pltpu.CompilerParams(vmem_limit_bytes=VMEM_LIMIT),
        name=name,
    )(me, info, tokens, *grads)


def chunks(width):
    step = COLUMN if width % COLUMN == 0 else width
    return [pl.ds(start, step) for start in range(0, width, step)]


def back_kernel(half, capacity, turn, me_ref, saved_ref, w_ref, *refs):
    outs, product = refs[:half], refs[half]
    run = half * capacity
    saved = jnp.concatenate([saved_ref[m, 0] for m in range(MICRO)], axis=0)
    here = jnp.bitwise_xor(lax.rem(me_ref[0], half), turn)
    for columns in chunks(w_ref.shape[1]):
        product[:, columns] = jnp.dot(saved, w_ref[:, columns], preferred_element_type=F32)
    for j in range(half):
        slots = [pl.multiple_of(m * run + jnp.bitwise_xor(here, j) * capacity, 8) for m in range(MICRO)]
        rows = jnp.concatenate([product[pl.ds(slot, capacity), :] for slot in slots], axis=0)
        outs[j][...] = rows.astype(BF16)


def back(me, saved, weight, half, capacity, turn):
    hidden_width, width = weight.shape
    run, rows = half * capacity, MICRO * capacity
    return pl.pallas_call(
        functools.partial(back_kernel, half, capacity, turn),
        grid_spec=pltpu.PrefetchScalarGridSpec(
            num_scalar_prefetch=1,
            grid=(1,),
            in_specs=[
                pl.BlockSpec((MICRO, 1, run, hidden_width), lambda i, me: (0, 1 - me[0] // half, 0, 0)),
                pl.BlockSpec(memory_space=pltpu.VMEM),
            ],
            out_specs=[pl.BlockSpec((rows, width), lambda i, me: (0, 0))] * half,
            scratch_shapes=[pltpu.VMEM((MICRO * run, width), F32)],
        ),
        out_shape=[jax.ShapeDtypeStruct((rows, width), BF16)] * half,
        compiler_params=pltpu.CompilerParams(vmem_limit_bytes=VMEM_LIMIT),
        name="back",
    )(me, saved, weight)


def turn_kernel(half, capacity, me_ref, w_ref, info_ref, router_ref, after_ref, out_ref, scale_ref, rank_ref, table_ref):
    del after_ref
    router = router_ref[...].astype(F32)
    router = jnp.concatenate([router, router, router, jnp.zeros((LANES - 24, router.shape[1]), F32)], axis=0)
    table_ref[...] = router.astype(BF16)
    for columns in chunks(w_ref.shape[1]):
        out_ref[columns, :] = w_ref[:, columns].T
    rank, weight = ranks(info_ref[...], jnp.bitwise_xor(me_ref[0], iota((8, LANES), 0)))
    rank_ref[...] = rank
    for j in range(half):
        for m in range(MICRO):
            _, scale = pick(rank[j : j + 1, :], weight[j : j + 1, :], m, capacity)
            scale_ref[j, m * capacity : (m + 1) * capacity, :] = scale


def turned(me, weight, info, router, after, half, capacity):
    vmem = pl.BlockSpec(memory_space=pltpu.VMEM)
    return pl.pallas_call(
        functools.partial(turn_kernel, half, capacity),
        out_shape=[
            jax.ShapeDtypeStruct(weight.shape[::-1], BF16),
            jax.ShapeDtypeStruct((half, MICRO * capacity, LANES), F32),
            jax.ShapeDtypeStruct((8, LANES), jnp.int32),
            jax.ShapeDtypeStruct((LANES, router.shape[1]), BF16),
        ],
        in_specs=[pl.BlockSpec(memory_space=pltpu.SMEM), vmem, vmem, vmem, pl.BlockSpec(memory_space=pl.ANY)],
        out_specs=[vmem] * 4,
        compiler_params=pltpu.CompilerParams(vmem_limit_bytes=VMEM_LIMIT),
        name="turned",
    )(me, weight, info, router, after)


def far_grad_kernel(half, capacity, *refs):
    blocks, (grad_ref,) = refs[:half], refs[2 * half :]
    backs = [refs[half + BACK_ORDER.index(j)] for j in range(half)]
    width = blocks[0].shape[1] - LANES
    rows = MICRO * capacity
    where = iota((rows, LANES), 1)
    table = jnp.zeros((rows, LANES), F32)
    for j in range(half):
        total = jnp.zeros((rows, LANES), F32)
        for lane in range(0, width, LANES):
            sent = blocks[j][:, lane : lane + LANES].astype(F32)
            total = total + sent * backs[j][:, lane : lane + LANES].astype(F32)
        for i, part in enumerate(split(jnp.sum(total, axis=1, keepdims=True))):
            table = jnp.where(where == 3 * j + i, part, table)
    grad_ref[...] = table.astype(BF16)


def far_grad(blocks, backs, half, capacity):
    vmem = pl.BlockSpec(memory_space=pltpu.VMEM)
    return pl.pallas_call(
        functools.partial(far_grad_kernel, half, capacity),
        out_shape=jax.ShapeDtypeStruct((MICRO * capacity, LANES), BF16),
        in_specs=[vmem] * (2 * half),
        out_specs=vmem,
        compiler_params=pltpu.CompilerParams(vmem_limit_bytes=VMEM_LIMIT),
        name="far_grad",
    )(*blocks, *[backs[j] for j in BACK_ORDER])


def own_kernel(half, capacity, me_ref, *refs):
    blocks, refs = [refs[OWN_ORDER.index(j)] for j in range(half)], refs[half:]
    w_ref, saved_ref, scale_ref, product, grads = refs[0], refs[1], refs[2], refs[3], refs[4 : 4 + half]
    lhs, partial = refs[4 + half :]
    hidden_width = w_ref.shape[1]
    run, size = half * capacity, MICRO * capacity
    me = me_ref[0]
    here, side = lax.rem(me, half), me // half
    places = []
    for j in range(half):
        lhs[j * size : (j + 1) * size, :] = blocks[j][...]
        for m in range(MICRO):
            slot = pl.multiple_of(m * run + jnp.bitwise_xor(here, j) * capacity, 8)
            places.append((j, m * capacity, slot))
    for columns in chunks(hidden_width):
        got = jnp.dot(lhs[...], w_ref[:, columns], preferred_element_type=F32)
        for j, row, slot in places:
            product[pl.ds(slot, capacity), columns] = got[j * size + row : j * size + row + capacity, :]
    for m in range(MICRO):
        total = jnp.zeros((run, LANES), F32)
        for lane in range(0, hidden_width, LANES):
            held = saved_ref[m, side, :, lane : lane + LANES].astype(F32)
            total = total + product[m * run : (m + 1) * run, lane : lane + LANES] * held
        partial[m * run : (m + 1) * run, :] = total
    lane = iota((size, LANES), 1)
    for j in range(half):
        slots = [slot for which, _, slot in places if which == j]
        sums = jnp.concatenate([partial[pl.ds(slot, capacity), :] for slot in slots], axis=0)
        table = scale_ref[j]
        for i, part in enumerate(split(jnp.sum(sums, axis=1, keepdims=True))):
            table = jnp.where(lane == i, part, table)
        grads[j][...] = table.astype(BF16)


def own_expert(me, blocks, weight, saved, scales, half, capacity):
    width, hidden_width = weight.shape
    rows = MICRO * capacity
    vmem = pl.BlockSpec(memory_space=pltpu.VMEM)
    return pl.pallas_call(
        functools.partial(own_kernel, half, capacity),
        out_shape=[jax.ShapeDtypeStruct((half * rows, hidden_width), F32)]
        + [jax.ShapeDtypeStruct((rows, LANES), BF16)] * half,
        in_specs=[pl.BlockSpec(memory_space=pltpu.SMEM)] + [vmem] * (half + 3),
        out_specs=[vmem] * (1 + half),
        scratch_shapes=[pltpu.VMEM((half * rows, width), BF16), pltpu.VMEM((half * rows, LANES), F32)],
        compiler_params=pltpu.CompilerParams(vmem_limit_bytes=VMEM_LIMIT),
        name="own_expert",
    )(me, *[blocks[j] for j in OWN_ORDER], weight, saved, scales)


def router_rows(half, capacity, turn, me, info_ref, own, far_ref, rank, table_ref):
    info = info_ref[...]
    relative = jnp.bitwise_xor(me, iota((8, LANES), 0))
    slot = iota((capacity, LANES), 0)
    token = iota((capacity, LANES), 1)
    far = far_ref[...].astype(F32)
    rows = []
    for j in range(2 * half):
        if j < half:
            table, lane = own[j], 0
        else:
            table, lane = far, 3 * ((j - half) ^ turn)
        column = table[:, lane : lane + 1] + table[:, lane + 1 : lane + 2] + table[:, lane + 2 : lane + 3]
        here = jnp.where(token // MB_TOK == 0, column[0:capacity], column[capacity : 2 * capacity])
        rows.append(jnp.sum(jnp.where(slot == rank[j : j + 1, :], here, 0.0), axis=0, keepdims=True))
    grads = jnp.concatenate(rows, axis=0)
    first, second = info[0:1, :].astype(jnp.int32), info[1:2, :].astype(jnp.int32)
    w_first, w_second = info[2:3, :], info[3:4, :]
    g_first = jnp.sum(jnp.where(relative == first, grads, 0.0), axis=0, keepdims=True)
    g_second = jnp.sum(jnp.where(relative == second, grads, 0.0), axis=0, keepdims=True)
    mean = w_first * g_first + w_second * g_second
    expert_rows = iota((8, LANES), 0)
    logit = jnp.where(expert_rows == first, w_first * (g_first - mean), 0.0)
    logit = logit + jnp.where(expert_rows == second, w_second * (g_second - mean), 0.0)
    parts = jnp.concatenate([*split(logit), jnp.zeros((LANES - 24, LANES), F32)], axis=0).T
    return jnp.dot(parts.astype(BF16), table_ref[...], preferred_element_type=F32).astype(BF16)


def last_kernel(half, capacity, turn, me_ref, *refs):
    blocks, refs = [refs[FAR_ORDER.index(j)] for j in range(half)], refs[half:]
    w_ref, own_ref, info_ref, far_ref, rank_ref, table_ref, d_ref, out_ref = refs[:8]
    lhs, product, scale, rows, hidden, row_sem, hidden_sem = refs[8:]
    width, hidden_width = w_ref.shape
    run, size = half * capacity, MICRO * capacity
    me = me_ref[0]
    side = me // half
    tails = [block[:, width:].astype(F32) for block in blocks]
    rows[...] = router_rows(half, capacity, turn, me, info_ref, tails, far_ref, rank_ref[...], table_ref)
    copies = [pltpu.make_async_copy(rows, out_ref, row_sem)]
    copies[0].start()
    here = lax.rem(me, half)

    def spread_scale(lane_of, slots):
        for j in range(half):
            for m in range(MICRO):
                tail = tails[j][m * capacity : (m + 1) * capacity]
                column = jnp.broadcast_to(tail[:, lane_of : lane_of + 1], tail.shape)
                scale[pl.ds(slots[j][m], capacity), :] = column

    def scaled(far, source, columns):
        for m in range(MICRO):
            at = slice(m * run, (m + 1) * run)
            for lane in range(columns.start, columns.start + columns.size, LANES):
                lanes = slice(lane, lane + LANES)
                hidden[far, m, :, lanes] = (scale[at, :] * source[at, lanes]).astype(BF16)
            to = d_ref.at[m, 1 - side if far else side, :, columns]
            part = columns.start // columns.size
            copies.append(pltpu.make_async_copy(hidden.at[far, m, :, columns], to, hidden_sem.at[far, m, part]))
            copies[-1].start()

    def slots_of(first):
        return [
            [pl.multiple_of(m * run + jnp.bitwise_xor(first, j) * capacity, 8) for m in range(MICRO)] for j in range(half)
        ]

    spread_scale(SCALE - 1, slots_of(here))
    scaled(0, own_ref, pl.ds(0, hidden_width))
    far_slots = slots_of(jnp.bitwise_xor(here, turn))
    spread_scale(SCALE, far_slots)
    for j in range(half):
        lhs[j * size : (j + 1) * size, :] = blocks[j][:, 0:width]
    for columns in chunks(hidden_width):
        got = jnp.dot(lhs[...], w_ref[:, columns], preferred_element_type=F32)
        for j in range(half):
            for m in range(MICRO):
                begin = j * size + m * capacity
                product[pl.ds(far_slots[j][m], capacity), columns] = got[begin : begin + capacity, :]
        scaled(1, product, columns)
    for copy in copies:
        copy.wait()


def last(me, blocks, weight, own, info, far, rank, table, saved, tokens, half, capacity, turn):
    width, hidden_width = weight.shape
    run = half * capacity
    vmem, anywhere = pl.BlockSpec(memory_space=pltpu.VMEM), pl.BlockSpec(memory_space=pl.ANY)
    return pl.pallas_call(
        functools.partial(last_kernel, half, capacity, turn),
        out_shape=[jax.ShapeDtypeStruct(saved.shape, BF16), jax.ShapeDtypeStruct(tokens.shape, BF16)],
        in_specs=[pl.BlockSpec(memory_space=pltpu.SMEM)] + [vmem] * (half + 6),
        out_specs=[anywhere, anywhere],
        scratch_shapes=[
            pltpu.VMEM((MICRO * run, width), BF16),
            pltpu.VMEM((MICRO * run, hidden_width), F32),
            pltpu.VMEM((MICRO * run, LANES), F32),
            pltpu.VMEM(tokens.shape, BF16),
            pltpu.VMEM((2, MICRO, run, hidden_width), BF16),
            pltpu.SemaphoreType.DMA,
            pltpu.SemaphoreType.DMA((2, MICRO, len(chunks(hidden_width)))),
        ],
        compiler_params=pltpu.CompilerParams(vmem_limit_bytes=VMEM_LIMIT),
        name="last",
    )(me, *[blocks[j] for j in FAR_ORDER], weight, own, info, far, rank, table)


def route(block, flip, back):
    sections, peers = lax.axis_size("pipe"), lax.axis_size("expert")
    pairs = [
        (p * peers + e, ((p - back) % sections) * peers + (e ^ flip)) for p in range(sections) for e in range(peers)
    ]
    return lax.ppermute(block, ("pipe", "expert"), pairs)


def by_halves(grad_sent, routes, router_probs, saved_hidden, w_down, w_router):
    peers = lax.axis_size("expert")
    half, turn = peers // 2, 2
    slots, hidden_width = saved_hidden.shape[1:]
    capacity = slots // (MICRO * peers)
    me = lax.axis_index("expert").astype(jnp.int32).reshape(1)
    tokens, weight = grad_sent[0], w_down[0]
    saved = saved_hidden.reshape(MICRO, 2, half * capacity, hidden_width)
    vmem = pl.BlockSpec(memory_space=pltpu.VMEM)

    def spread(blocks):
        return [blocks[0]] + [route(blocks[j], j, 0) for j in range(1, half)]

    info = pl.pallas_call(
        info_kernel,
        out_shape=jax.ShapeDtypeStruct((8, LANES), F32),
        in_specs=[vmem, vmem],
        out_specs=vmem,
        name="info",
    )(routes[0].T, router_probs[0].T)
    next_info = route(info, 0, -1)
    far_info = route(info, half + turn, 0)
    far_tokens = route(tokens, half + turn, 1)
    packed = pack(me, next_info, tokens, half, capacity, "pack_own")
    weight_t, scales, rank, table = turned(me, weight, info, w_router.T, packed[0], half, capacity)
    saved, packed = lax.optimization_barrier((saved, packed))
    backs = back(me, saved, weight, half, capacity, turn)
    own = [route(packed[j], j, 1) for j in range(half)]
    backs = spread(backs)
    own_product, *own_grads = own_expert(me, own, weight_t, saved, scales, half, capacity)
    far = pack(me, far_info, far_tokens, half, capacity, "pack_far", own_grads)
    far_grads = route(far_grad(far, backs, half, capacity), half + turn, 0)
    far = spread(far)
    d_hidden, grad_in = last(
        me, far, weight_t, own_product, info, far_grads, rank, table, saved, tokens, half, capacity, turn
    )
    return d_hidden.reshape(saved_hidden.shape), grad_in[None]


def from_behind(block, axis, distance):
    devices = range(lax.axis_size(axis))
    route = [((i - distance) % len(devices), i) for i in devices]
    return lax.ppermute(block, axis, route)


def route_slots(route_rows, peer_count, capacity):
    onehot = (route_rows[..., None] == jnp.arange(peer_count, dtype=jnp.int32)).astype(jnp.int32)
    rank_of = jnp.sum((jnp.cumsum(onehot, axis=1) - onehot) * onehot, axis=2)
    return route_rows * capacity + rank_of


def by_slots(grad_sent, routes, router_probs, saved_hidden, w_down, w_router):
    peer_count = lax.axis_size("expert")
    slot_count = saved_hidden.shape[1]
    capacity = slot_count // (MICRO * peer_count)
    send_width = peer_count * capacity
    model_width = grad_sent.shape[2]
    hidden_width = saved_hidden.shape[2]
    tokens = routes.shape[1]
    incoming = from_behind(grad_sent, "pipe", -1)[0]
    route_rows = routes[0].reshape(MICRO, MB_TOK * TOP)
    position = route_slots(route_rows, peer_count, capacity)
    chosen = jnp.take_along_axis(router_probs[0], routes[0], axis=1)
    weights = chosen / jnp.sum(chosen, axis=1, keepdims=True)
    rounded = weights.astype(jnp.bfloat16)
    micro_index = jnp.arange(MICRO, dtype=jnp.int32)[:, None]
    token_index = jnp.broadcast_to(
        jnp.arange(MB_TOK * TOP, dtype=jnp.int32)[None, :] // TOP, (MICRO, MB_TOK * TOP)
    )
    slot_token = (
        jnp.zeros((MICRO, send_width), jnp.int32).at[micro_index, position].set(token_index)
    )
    slot_used = jnp.zeros((MICRO, send_width), jnp.bool_).at[micro_index, position].set(True)
    send_scale = (
        jnp.zeros((MICRO, send_width), jnp.bfloat16)
        .at[micro_index, position]
        .set(rounded.reshape(MICRO, MB_TOK * TOP))
    )
    micro_grad = incoming.reshape(MICRO, MB_TOK, model_width)
    picked = jnp.take_along_axis(micro_grad, slot_token[..., None], axis=1)
    send_rows = jnp.where(slot_used[..., None], picked, jnp.zeros((), jnp.bfloat16))
    hidden = saved_hidden[0].reshape(MICRO, send_width, hidden_width)
    weight = w_down[0]
    arrived, arrived_scale = (
        lax.all_to_all(send_rows, "expert", split_axis=1, concat_axis=1, tiled=True),
        lax.all_to_all(send_scale, "expert", split_axis=1, concat_axis=1, tiled=True),
    )
    flat_rows = arrived.reshape(-1, model_width)
    flat_saved = hidden.reshape(flat_rows.shape[0], hidden_width)
    grad_hidden = lax.dot_general(
        flat_rows, weight, (((1,), (1,)), ((), ())), preferred_element_type=jnp.float32
    )
    route_grad = jnp.sum(grad_hidden * flat_saved.astype(jnp.float32), axis=1)
    scaled = (arrived_scale.reshape(-1, 1).astype(jnp.float32) * grad_hidden).astype(jnp.bfloat16)
    d_hidden, route_grad = (scaled, route_grad.reshape(arrived_scale.shape))
    returned = lax.all_to_all(route_grad, "expert", split_axis=1, concat_axis=1, tiled=True)
    slot_grad = jnp.take_along_axis(returned, position, axis=1).reshape(tokens, TOP)
    centred = slot_grad - jnp.sum(weights * slot_grad, axis=1, keepdims=True)
    logit_part = weights * centred
    onehot_tok = (routes[0][..., None] == jnp.arange(peer_count, dtype=jnp.int32)).astype(
        jnp.float32
    )
    logit_grad = jnp.sum(logit_part[..., None] * onehot_tok, axis=1)
    grad_in = jnp.dot(logit_grad, w_router.astype(jnp.float32).T, precision=lax.Precision.HIGHEST)
    return (d_hidden.reshape(1, slot_count, hidden_width), grad_in.astype(jnp.bfloat16)[None])


def on_device(*blocks):
    peers, slots = lax.axis_size("expert"), blocks[3].shape[1]
    capacity = slots // (MICRO * peers)
    if peers == 8 and capacity % 8 == 0 and capacity <= MB_TOK // 2:
        return by_halves(*blocks)
    return by_slots(*blocks)


def solution(mesh):
    placed = (
        P("pipe", "expert", None),
        P("pipe", "expert", None),
        P("pipe", "expert", None),
        P("pipe", "expert", None),
        P("expert", None, None),
        P(),
    )
    return jax.shard_map(
        on_device,
        mesh=mesh,
        in_specs=placed,
        out_specs=(P("pipe", "expert", None), P("pipe", "expert", None)),
        check_vma=False,
    )
```

```python
import functools

import jax
import jax.numpy as jnp
from jax import lax
from jax.experimental import pallas as pl
from jax.experimental.pallas import tpu as pltpu
from jax.sharding import PartitionSpec as P

TOP = 2
MICRO = 2
MB_TOK = 64
LANES = 128
F32, BF16 = jnp.float32, jnp.bfloat16
VMEM_LIMIT = 16 * 1024 * 1024
COLUMN = 256
SCALE = 4
OWN_ORDER, BACK_ORDER, FAR_ORDER = (0, 1, 2, 3), (0, 3, 2, 1), (0, 3, 2, 1)


def iota(shape, axis):
    return lax.broadcasted_iota(jnp.int32, shape, axis)


def info_kernel(routes_ref, probs_ref, info_ref):
    probs = probs_ref[...]
    expert = iota(probs.shape, 0)
    first, second = routes_ref[0:1, :], routes_ref[1:2, :]
    p_first = jnp.sum(jnp.where(expert == first, probs, 0.0), axis=0, keepdims=True)
    p_second = jnp.sum(jnp.where(expert == second, probs, 0.0), axis=0, keepdims=True)
    total = p_first + p_second
    info_ref[0:1, :] = first.astype(F32)
    info_ref[1:2, :] = second.astype(F32)
    info_ref[2:3, :] = p_first / total
    info_ref[3:4, :] = p_second / total
    info_ref[4:8, :] = jnp.zeros((4, LANES), F32)


def split(column):
    high = column.astype(BF16).astype(F32)
    middle = (column - high).astype(BF16).astype(F32)
    return high, middle, column - high - middle


def ranks(info, expert_rows):
    first, second = info[0:1, :].astype(jnp.int32), info[1:2, :].astype(jnp.int32)
    on_first, on_second = expert_rows == first, expert_rows == second
    named = on_first | on_second
    before = iota((LANES, LANES), 0)
    after = iota((LANES, LANES), 1)
    earlier = ((before < after) & (before // MB_TOK == after // MB_TOK)).astype(F32).astype(BF16)
    rank = jnp.dot(named.astype(F32).astype(BF16), earlier, preferred_element_type=F32)
    rank = jnp.where(named, rank.astype(jnp.int32), -1)
    weight = jnp.where(on_first, info[2:3, :], 0.0) + jnp.where(on_second, info[3:4, :], 0.0)
    return rank, weight.astype(BF16).astype(F32)


def pick(rank_row, weight_row, micro, capacity):
    slot = iota((capacity, LANES), 0)
    token = iota((capacity, LANES), 1)
    hit = (slot == rank_row) & (token // MB_TOK == micro)
    onehot = jnp.where(hit, 1.0, 0.0)
    scale = jnp.sum(jnp.where(hit, weight_row, 0.0), axis=1, keepdims=True)
    return onehot, jnp.broadcast_to(scale, (capacity, LANES))


def pack_kernel(half, capacity, me_ref, info_ref, token_ref, *refs):
    grads, outs = refs[:-half], refs[-half:]
    rows = jnp.bitwise_xor(me_ref[0], iota((8, LANES), 0))
    rank, weight = ranks(info_ref[...], rows)
    pieces, scales = [], []
    for j in range(half):
        for micro in range(MICRO):
            onehot, scale = pick(rank[j : j + 1, :], weight[j : j + 1, :], micro, capacity)
            pieces.append(onehot)
            scales.append(scale)
    width = token_ref.shape[1]
    chosen = jnp.concatenate(pieces, axis=0).astype(BF16)
    packed = jnp.dot(chosen, token_ref[...], preferred_element_type=F32).astype(BF16)
    size = MICRO * capacity
    lane = iota((size, LANES), 1)
    for j in range(half):
        outs[j][:, 0:width] = packed[j * size : (j + 1) * size]
        if grads:
            tail = jnp.concatenate(scales[j * MICRO : (j + 1) * MICRO], axis=0)
            outs[j][:, width:] = jnp.where(lane < SCALE, grads[j][...].astype(F32), tail).astype(BF16)


def pack(me, info, tokens, half, capacity, name, grads=()):
    block = jax.ShapeDtypeStruct((MICRO * capacity, tokens.shape[1] + LANES * bool(grads)), BF16)
    vmem = pl.BlockSpec(memory_space=pltpu.VMEM)
    return pl.pallas_call(
        functools.partial(pack_kernel, half, capacity),
        out_shape=[block] * half,
        in_specs=[pl.BlockSpec(memory_space=pltpu.SMEM)] + [vmem] * (2 + len(grads)),
        out_specs=[vmem] * half,
        compiler_params=pltpu.CompilerParams(vmem_limit_bytes=VMEM_LIMIT),
        name=name,
    )(me, info, tokens, *grads)


def chunks(width):
    step = COLUMN if width % COLUMN == 0 else width
    return [pl.ds(start, step) for start in range(0, width, step)]


def back_kernel(half, capacity, turn, me_ref, saved_ref, w_ref, *refs):
    outs, product = refs[:half], refs[half]
    run = half * capacity
    saved = jnp.concatenate([saved_ref[m, 0] for m in range(MICRO)], axis=0)
    here = jnp.bitwise_xor(lax.rem(me_ref[0], half), turn)
    for columns in chunks(w_ref.shape[1]):
        product[:, columns] = jnp.dot(saved, w_ref[:, columns], preferred_element_type=F32)
    for j in range(half):
        slots = [pl.multiple_of(m * run + jnp.bitwise_xor(here, j) * capacity, 8) for m in range(MICRO)]
        rows = jnp.concatenate([product[pl.ds(slot, capacity), :] for slot in slots], axis=0)
        outs[j][...] = rows.astype(BF16)


def back(me, saved, weight, half, capacity, turn):
    hidden_width, width = weight.shape
    run, rows = half * capacity, MICRO * capacity
    return pl.pallas_call(
        functools.partial(back_kernel, half, capacity, turn),
        grid_spec=pltpu.PrefetchScalarGridSpec(
            num_scalar_prefetch=1,
            grid=(1,),
            in_specs=[
                pl.BlockSpec((MICRO, 1, run, hidden_width), lambda i, me: (0, 1 - me[0] // half, 0, 0)),
                pl.BlockSpec(memory_space=pltpu.VMEM),
            ],
            out_specs=[pl.BlockSpec((rows, width), lambda i, me: (0, 0))] * half,
            scratch_shapes=[pltpu.VMEM((MICRO * run, width), F32)],
        ),
        out_shape=[jax.ShapeDtypeStruct((rows, width), BF16)] * half,
        compiler_params=pltpu.CompilerParams(vmem_limit_bytes=VMEM_LIMIT),
        name="back",
    )(me, saved, weight)


def turn_kernel(half, capacity, me_ref, w_ref, info_ref, router_ref, after_ref, out_ref, scale_ref, rank_ref, table_ref):
    del after_ref
    router = router_ref[...].astype(F32)
    router = jnp.concatenate([router, router, router, jnp.zeros((LANES - 24, router.shape[1]), F32)], axis=0)
    table_ref[...] = router.astype(BF16)
    for columns in chunks(w_ref.shape[1]):
        out_ref[columns, :] = w_ref[:, columns].T
    rank, weight = ranks(info_ref[...], jnp.bitwise_xor(me_ref[0], iota((8, LANES), 0)))
    rank_ref[...] = rank
    for j in range(half):
        for m in range(MICRO):
            _, scale = pick(rank[j : j + 1, :], weight[j : j + 1, :], m, capacity)
            scale_ref[j, m * capacity : (m + 1) * capacity, :] = scale


def turned(me, weight, info, router, after, half, capacity):
    vmem = pl.BlockSpec(memory_space=pltpu.VMEM)
    return pl.pallas_call(
        functools.partial(turn_kernel, half, capacity),
        out_shape=[
            jax.ShapeDtypeStruct(weight.shape[::-1], BF16),
            jax.ShapeDtypeStruct((half, MICRO * capacity, LANES), F32),
            jax.ShapeDtypeStruct((8, LANES), jnp.int32),
            jax.ShapeDtypeStruct((LANES, router.shape[1]), BF16),
        ],
        in_specs=[pl.BlockSpec(memory_space=pltpu.SMEM), vmem, vmem, vmem, pl.BlockSpec(memory_space=pl.ANY)],
        out_specs=[vmem] * 4,
        compiler_params=pltpu.CompilerParams(vmem_limit_bytes=VMEM_LIMIT),
        name="turned",
    )(me, weight, info, router, after)


def far_grad_kernel(half, capacity, *refs):
    blocks, (grad_ref,) = refs[:half], refs[2 * half :]
    backs = [refs[half + BACK_ORDER.index(j)] for j in range(half)]
    width = blocks[0].shape[1] - LANES
    rows = MICRO * capacity
    where = iota((rows, LANES), 1)
    table = jnp.zeros((rows, LANES), F32)
    for j in range(half):
        total = jnp.zeros((rows, LANES), F32)
        for lane in range(0, width, LANES):
            sent = blocks[j][:, lane : lane + LANES].astype(F32)
            total = total + sent * backs[j][:, lane : lane + LANES].astype(F32)
        for i, part in enumerate(split(jnp.sum(total, axis=1, keepdims=True))):
            table = jnp.where(where == 3 * j + i, part, table)
    grad_ref[...] = table.astype(BF16)


def far_grad(blocks, backs, half, capacity):
    vmem = pl.BlockSpec(memory_space=pltpu.VMEM)
    return pl.pallas_call(
        functools.partial(far_grad_kernel, half, capacity),
        out_shape=jax.ShapeDtypeStruct((MICRO * capacity, LANES), BF16),
        in_specs=[vmem] * (2 * half),
        out_specs=vmem,
        compiler_params=pltpu.CompilerParams(vmem_limit_bytes=VMEM_LIMIT),
        name="far_grad",
    )(*blocks, *[backs[j] for j in BACK_ORDER])


def own_kernel(half, capacity, me_ref, *refs):
    blocks, refs = [refs[OWN_ORDER.index(j)] for j in range(half)], refs[half:]
    w_ref, saved_ref, scale_ref, product, grads = refs[0], refs[1], refs[2], refs[3], refs[4 : 4 + half]
    (partial,) = refs[4 + half :]
    hidden_width = w_ref.shape[1]
    run, size = half * capacity, MICRO * capacity
    me = me_ref[0]
    here, side = lax.rem(me, half), me // half
    places = []
    for j in range(half):
        for m in range(MICRO):
            slot = pl.multiple_of(m * run + jnp.bitwise_xor(here, j) * capacity, 8)
            places.append((j, m * capacity, slot))
    sent = jnp.concatenate([block[...] for block in blocks], axis=0)
    for columns in chunks(hidden_width):
        got = jnp.dot(sent, w_ref[:, columns], preferred_element_type=F32)
        for j, row, slot in places:
            product[pl.ds(slot, capacity), columns] = got[j * size + row : j * size + row + capacity, :]
    for m in range(MICRO):
        total = jnp.zeros((run, LANES), F32)
        for lane in range(0, hidden_width, LANES):
            held = saved_ref[m, side, :, lane : lane + LANES].astype(F32)
            total = total + product[m * run : (m + 1) * run, lane : lane + LANES] * held
        partial[m * run : (m + 1) * run, :] = total
    lane = iota((size, LANES), 1)
    for j in range(half):
        slots = [slot for which, _, slot in places if which == j]
        sums = jnp.concatenate([partial[pl.ds(slot, capacity), :] for slot in slots], axis=0)
        table = scale_ref[j]
        for i, part in enumerate(split(jnp.sum(sums, axis=1, keepdims=True))):
            table = jnp.where(lane == i, part, table)
        grads[j][...] = table.astype(BF16)


def own_expert(me, blocks, weight, saved, scales, half, capacity):
    hidden_width = weight.shape[1]
    rows = MICRO * capacity
    vmem = pl.BlockSpec(memory_space=pltpu.VMEM)
    return pl.pallas_call(
        functools.partial(own_kernel, half, capacity),
        out_shape=[jax.ShapeDtypeStruct((half * rows, hidden_width), F32)]
        + [jax.ShapeDtypeStruct((rows, LANES), BF16)] * half,
        in_specs=[pl.BlockSpec(memory_space=pltpu.SMEM)] + [vmem] * (half + 3),
        out_specs=[vmem] * (1 + half),
        scratch_shapes=[pltpu.VMEM((half * rows, LANES), F32)],
        compiler_params=pltpu.CompilerParams(vmem_limit_bytes=VMEM_LIMIT),
        name="own_expert",
    )(me, *[blocks[j] for j in OWN_ORDER], weight, saved, scales)


def router_rows(half, capacity, turn, me, info_ref, own, far_ref, rank, table_ref):
    info = info_ref[...]
    relative = jnp.bitwise_xor(me, iota((8, LANES), 0))
    slot = iota((capacity, LANES), 0)
    token = iota((capacity, LANES), 1)
    far = far_ref[...].astype(F32)
    rows = []
    for j in range(2 * half):
        if j < half:
            table, lane = own[j], 0
        else:
            table, lane = far, 3 * ((j - half) ^ turn)
        column = table[:, lane : lane + 1] + table[:, lane + 1 : lane + 2] + table[:, lane + 2 : lane + 3]
        here = jnp.where(token // MB_TOK == 0, column[0:capacity], column[capacity : 2 * capacity])
        rows.append(jnp.sum(jnp.where(slot == rank[j : j + 1, :], here, 0.0), axis=0, keepdims=True))
    grads = jnp.concatenate(rows, axis=0)
    first, second = info[0:1, :].astype(jnp.int32), info[1:2, :].astype(jnp.int32)
    w_first, w_second = info[2:3, :], info[3:4, :]
    g_first = jnp.sum(jnp.where(relative == first, grads, 0.0), axis=0, keepdims=True)
    g_second = jnp.sum(jnp.where(relative == second, grads, 0.0), axis=0, keepdims=True)
    mean = w_first * g_first + w_second * g_second
    expert_rows = iota((8, LANES), 0)
    logit = jnp.where(expert_rows == first, w_first * (g_first - mean), 0.0)
    logit = logit + jnp.where(expert_rows == second, w_second * (g_second - mean), 0.0)
    parts = jnp.concatenate([*split(logit), jnp.zeros((LANES - 24, LANES), F32)], axis=0).T
    return jnp.dot(parts.astype(BF16), table_ref[...], preferred_element_type=F32).astype(BF16)


def last_kernel(half, capacity, turn, me_ref, *refs):
    blocks, refs = [refs[FAR_ORDER.index(j)] for j in range(half)], refs[half:]
    w_ref, own_ref, info_ref, far_ref, rank_ref, table_ref, d_ref, out_ref = refs[:8]
    product, scale, rows, hidden, row_sem, hidden_sem = refs[8:]
    width, hidden_width = w_ref.shape
    run, size = half * capacity, MICRO * capacity
    me = me_ref[0]
    side = me // half
    tails = [block[:, width:].astype(F32) for block in blocks]
    rows[...] = router_rows(half, capacity, turn, me, info_ref, tails, far_ref, rank_ref[...], table_ref)
    copies = [pltpu.make_async_copy(rows, out_ref, row_sem)]
    copies[0].start()
    here = lax.rem(me, half)

    def spread_scale(lane_of, slots):
        for j in range(half):
            for m in range(MICRO):
                tail = tails[j][m * capacity : (m + 1) * capacity]
                column = jnp.broadcast_to(tail[:, lane_of : lane_of + 1], tail.shape)
                scale[pl.ds(slots[j][m], capacity), :] = column

    def scaled(far, source, columns):
        for m in range(MICRO):
            at = slice(m * run, (m + 1) * run)
            for lane in range(columns.start, columns.start + columns.size, LANES):
                lanes = slice(lane, lane + LANES)
                hidden[far, m, :, lanes] = (scale[at, :] * source[at, lanes]).astype(BF16)
            to = d_ref.at[m, 1 - side if far else side, :, columns]
            part = columns.start // columns.size
            copies.append(pltpu.make_async_copy(hidden.at[far, m, :, columns], to, hidden_sem.at[far, m, part]))
            copies[-1].start()

    def slots_of(first):
        return [
            [pl.multiple_of(m * run + jnp.bitwise_xor(first, j) * capacity, 8) for m in range(MICRO)] for j in range(half)
        ]

    spread_scale(SCALE - 1, slots_of(here))
    scaled(0, own_ref, pl.ds(0, hidden_width))
    far_slots = slots_of(jnp.bitwise_xor(here, turn))
    spread_scale(SCALE, far_slots)
    sent = jnp.concatenate([block[:, 0:width] for block in blocks], axis=0)
    for columns in chunks(hidden_width):
        got = jnp.dot(sent, w_ref[:, columns], preferred_element_type=F32)
        for j in range(half):
            for m in range(MICRO):
                begin = j * size + m * capacity
                product[pl.ds(far_slots[j][m], capacity), columns] = got[begin : begin + capacity, :]
        scaled(1, product, columns)
    for copy in copies:
        copy.wait()


def last(me, blocks, weight, own, info, far, rank, table, saved, tokens, half, capacity, turn):
    hidden_width = weight.shape[1]
    run = half * capacity
    vmem, anywhere = pl.BlockSpec(memory_space=pltpu.VMEM), pl.BlockSpec(memory_space=pl.ANY)
    return pl.pallas_call(
        functools.partial(last_kernel, half, capacity, turn),
        out_shape=[jax.ShapeDtypeStruct(saved.shape, BF16), jax.ShapeDtypeStruct(tokens.shape, BF16)],
        in_specs=[pl.BlockSpec(memory_space=pltpu.SMEM)] + [vmem] * (half + 6),
        out_specs=[anywhere, anywhere],
        scratch_shapes=[
            pltpu.VMEM((MICRO * run, hidden_width), F32),
            pltpu.VMEM((MICRO * run, LANES), F32),
            pltpu.VMEM(tokens.shape, BF16),
            pltpu.VMEM((2, MICRO, run, hidden_width), BF16),
            pltpu.SemaphoreType.DMA,
            pltpu.SemaphoreType.DMA((2, MICRO, len(chunks(hidden_width)))),
        ],
        compiler_params=pltpu.CompilerParams(vmem_limit_bytes=VMEM_LIMIT),
        name="last",
    )(me, *[blocks[j] for j in FAR_ORDER], weight, own, info, far, rank, table)


def route(block, flip, back):
    sections, peers = lax.axis_size("pipe"), lax.axis_size("expert")
    pairs = [
        (p * peers + e, ((p - back) % sections) * peers + (e ^ flip)) for p in range(sections) for e in range(peers)
    ]
    return lax.ppermute(block, ("pipe", "expert"), pairs)


def by_halves(grad_sent, routes, router_probs, saved_hidden, w_down, w_router):
    peers = lax.axis_size("expert")
    half, turn = peers // 2, 2
    slots, hidden_width = saved_hidden.shape[1:]
    capacity = slots // (MICRO * peers)
    me = lax.axis_index("expert").astype(jnp.int32).reshape(1)
    tokens, weight = grad_sent[0], w_down[0]
    saved = saved_hidden.reshape(MICRO, 2, half * capacity, hidden_width)
    vmem = pl.BlockSpec(memory_space=pltpu.VMEM)

    def spread(blocks):
        return [blocks[0]] + [route(blocks[j], j, 0) for j in range(1, half)]

    info = pl.pallas_call(
        info_kernel,
        out_shape=jax.ShapeDtypeStruct((8, LANES), F32),
        in_specs=[vmem, vmem],
        out_specs=vmem,
        name="info",
    )(routes[0].T, router_probs[0].T)
    next_info = route(info, 0, -1)
    far_info = route(info, half + turn, 0)
    far_tokens = route(tokens, half + turn, 1)
    packed = pack(me, next_info, tokens, half, capacity, "pack_own")
    weight_t, scales, rank, table = turned(me, weight, info, w_router.T, packed[0], half, capacity)
    saved, packed = lax.optimization_barrier((saved, packed))
    backs = back(me, saved, weight, half, capacity, turn)
    own = [route(packed[j], j, 1) for j in range(half)]
    backs, weight_t = lax.optimization_barrier((backs, weight_t))
    backs = spread(backs)
    own_product, *own_grads = own_expert(me, own, weight_t, saved, scales, half, capacity)
    far = pack(me, far_info, far_tokens, half, capacity, "pack_far", own_grads)
    far_grads = route(far_grad(far, backs, half, capacity), half + turn, 0)
    far = spread(far)
    d_hidden, grad_in = last(
        me, far, weight_t, own_product, info, far_grads, rank, table, saved, tokens, half, capacity, turn
    )
    return d_hidden.reshape(saved_hidden.shape), grad_in[None]


def from_behind(block, axis, distance):
    devices = range(lax.axis_size(axis))
    route = [((i - distance) % len(devices), i) for i in devices]
    return lax.ppermute(block, axis, route)


def route_slots(route_rows, peer_count, capacity):
    onehot = (route_rows[..., None] == jnp.arange(peer_count, dtype=jnp.int32)).astype(jnp.int32)
    rank_of = jnp.sum((jnp.cumsum(onehot, axis=1) - onehot) * onehot, axis=2)
    return route_rows * capacity + rank_of


def by_slots(grad_sent, routes, router_probs, saved_hidden, w_down, w_router):
    peer_count = lax.axis_size("expert")
    slot_count = saved_hidden.shape[1]
    capacity = slot_count // (MICRO * peer_count)
    send_width = peer_count * capacity
    model_width = grad_sent.shape[2]
    hidden_width = saved_hidden.shape[2]
    tokens = routes.shape[1]
    incoming = from_behind(grad_sent, "pipe", -1)[0]
    route_rows = routes[0].reshape(MICRO, MB_TOK * TOP)
    position = route_slots(route_rows, peer_count, capacity)
    chosen = jnp.take_along_axis(router_probs[0], routes[0], axis=1)
    weights = chosen / jnp.sum(chosen, axis=1, keepdims=True)
    rounded = weights.astype(jnp.bfloat16)
    micro_index = jnp.arange(MICRO, dtype=jnp.int32)[:, None]
    token_index = jnp.broadcast_to(
        jnp.arange(MB_TOK * TOP, dtype=jnp.int32)[None, :] // TOP, (MICRO, MB_TOK * TOP)
    )
    slot_token = (
        jnp.zeros((MICRO, send_width), jnp.int32).at[micro_index, position].set(token_index)
    )
    slot_used = jnp.zeros((MICRO, send_width), jnp.bool_).at[micro_index, position].set(True)
    send_scale = (
        jnp.zeros((MICRO, send_width), jnp.bfloat16)
        .at[micro_index, position]
        .set(rounded.reshape(MICRO, MB_TOK * TOP))
    )
    micro_grad = incoming.reshape(MICRO, MB_TOK, model_width)
    picked = jnp.take_along_axis(micro_grad, slot_token[..., None], axis=1)
    send_rows = jnp.where(slot_used[..., None], picked, jnp.zeros((), jnp.bfloat16))
    hidden = saved_hidden[0].reshape(MICRO, send_width, hidden_width)
    weight = w_down[0]
    arrived, arrived_scale = (
        lax.all_to_all(send_rows, "expert", split_axis=1, concat_axis=1, tiled=True),
        lax.all_to_all(send_scale, "expert", split_axis=1, concat_axis=1, tiled=True),
    )
    flat_rows = arrived.reshape(-1, model_width)
    flat_saved = hidden.reshape(flat_rows.shape[0], hidden_width)
    grad_hidden = lax.dot_general(
        flat_rows, weight, (((1,), (1,)), ((), ())), preferred_element_type=jnp.float32
    )
    route_grad = jnp.sum(grad_hidden * flat_saved.astype(jnp.float32), axis=1)
    scaled = (arrived_scale.reshape(-1, 1).astype(jnp.float32) * grad_hidden).astype(jnp.bfloat16)
    d_hidden, route_grad = (scaled, route_grad.reshape(arrived_scale.shape))
    returned = lax.all_to_all(route_grad, "expert", split_axis=1, concat_axis=1, tiled=True)
    slot_grad = jnp.take_along_axis(returned, position, axis=1).reshape(tokens, TOP)
    centred = slot_grad - jnp.sum(weights * slot_grad, axis=1, keepdims=True)
    logit_part = weights * centred
    onehot_tok = (routes[0][..., None] == jnp.arange(peer_count, dtype=jnp.int32)).astype(
        jnp.float32
    )
    logit_grad = jnp.sum(logit_part[..., None] * onehot_tok, axis=1)
    grad_in = jnp.dot(logit_grad, w_router.astype(jnp.float32).T, precision=lax.Precision.HIGHEST)
    return (d_hidden.reshape(1, slot_count, hidden_width), grad_in.astype(jnp.bfloat16)[None])


def on_device(*blocks):
    peers, slots = lax.axis_size("expert"), blocks[3].shape[1]
    capacity = slots // (MICRO * peers)
    if peers == 8 and capacity % 8 == 0 and capacity <= MB_TOK // 2:
        return by_halves(*blocks)
    return by_slots(*blocks)


def solution(mesh):
    placed = (
        P("pipe", "expert", None),
        P("pipe", "expert", None),
        P("pipe", "expert", None),
        P("pipe", "expert", None),
        P("expert", None, None),
        P(),
    )
    return jax.shard_map(
        on_device,
        mesh=mesh,
        in_specs=placed,
        out_specs=(P("pipe", "expert", None), P("pipe", "expert", None)),
        check_vma=False,
    )
```

```python
import functools

import jax
import jax.numpy as jnp
from jax import lax
from jax.experimental import pallas as pl
from jax.experimental.pallas import tpu as pltpu
from jax.sharding import PartitionSpec as P

TOP = 2
MICRO = 2
MB_TOK = 64
LANES = 128
F32, BF16 = jnp.float32, jnp.bfloat16
VMEM_LIMIT = 16 * 1024 * 1024
COLUMN = 256
SCALE = 4
OWN_ORDER, BACK_ORDER, FAR_ORDER = (0, 1, 2, 3), (0, 3, 2, 1), (0, 3, 2, 1)


def iota(shape, axis):
    return lax.broadcasted_iota(jnp.int32, shape, axis)


def info_kernel(routes_ref, probs_ref, info_ref):
    probs = probs_ref[...]
    expert = iota(probs.shape, 0)
    first, second = routes_ref[0:1, :], routes_ref[1:2, :]
    p_first = jnp.sum(jnp.where(expert == first, probs, 0.0), axis=0, keepdims=True)
    p_second = jnp.sum(jnp.where(expert == second, probs, 0.0), axis=0, keepdims=True)
    total = p_first + p_second
    info_ref[0:1, :] = first.astype(F32)
    info_ref[1:2, :] = second.astype(F32)
    info_ref[2:3, :] = p_first / total
    info_ref[3:4, :] = p_second / total
    info_ref[4:8, :] = jnp.zeros((4, LANES), F32)


def split(column):
    high = column.astype(BF16).astype(F32)
    middle = (column - high).astype(BF16).astype(F32)
    return high, middle, column - high - middle


def ranks(info, expert_rows):
    first, second = info[0:1, :].astype(jnp.int32), info[1:2, :].astype(jnp.int32)
    on_first, on_second = expert_rows == first, expert_rows == second
    named = on_first | on_second
    before = iota((LANES, LANES), 0)
    after = iota((LANES, LANES), 1)
    earlier = ((before < after) & (before // MB_TOK == after // MB_TOK)).astype(F32).astype(BF16)
    rank = jnp.dot(named.astype(F32).astype(BF16), earlier, preferred_element_type=F32)
    rank = jnp.where(named, rank.astype(jnp.int32), -1)
    weight = jnp.where(on_first, info[2:3, :], 0.0) + jnp.where(on_second, info[3:4, :], 0.0)
    return rank, weight.astype(BF16).astype(F32)


def pick(rank_row, weight_row, micro, capacity):
    slot = iota((capacity, LANES), 0)
    token = iota((capacity, LANES), 1)
    hit = (slot == rank_row) & (token // MB_TOK == micro)
    onehot = jnp.where(hit, 1.0, 0.0)
    scale = jnp.sum(jnp.where(hit, weight_row, 0.0), axis=1, keepdims=True)
    return onehot, jnp.broadcast_to(scale, (capacity, LANES))


def pack_kernel(half, capacity, me_ref, info_ref, token_ref, *refs):
    grads, outs = refs[:-half], refs[-half:]
    rows = jnp.bitwise_xor(me_ref[0], iota((8, LANES), 0))
    rank, weight = ranks(info_ref[...], rows)
    pieces, scales = [], []
    for j in range(half):
        for micro in range(MICRO):
            onehot, scale = pick(rank[j : j + 1, :], weight[j : j + 1, :], micro, capacity)
            pieces.append(onehot)
            scales.append(scale)
    width = token_ref.shape[1]
    chosen = jnp.concatenate(pieces, axis=0).astype(BF16)
    packed = jnp.dot(chosen, token_ref[...], preferred_element_type=F32).astype(BF16)
    size = MICRO * capacity
    lane = iota((size, LANES), 1)
    for j in range(half):
        outs[j][:, 0:width] = packed[j * size : (j + 1) * size]
        if grads:
            tail = jnp.concatenate(scales[j * MICRO : (j + 1) * MICRO], axis=0)
            outs[j][:, width:] = jnp.where(lane < SCALE, grads[j][...].astype(F32), tail).astype(BF16)


def pack(me, info, tokens, half, capacity, name, grads=()):
    block = jax.ShapeDtypeStruct((MICRO * capacity, tokens.shape[1] + LANES * bool(grads)), BF16)
    vmem = pl.BlockSpec(memory_space=pltpu.VMEM)
    return pl.pallas_call(
        functools.partial(pack_kernel, half, capacity),
        out_shape=[block] * half,
        in_specs=[pl.BlockSpec(memory_space=pltpu.SMEM)] + [vmem] * (2 + len(grads)),
        out_specs=[vmem] * half,
        compiler_params=pltpu.CompilerParams(vmem_limit_bytes=VMEM_LIMIT),
        name=name,
    )(me, info, tokens, *grads)


def chunks(width):
    step = COLUMN if width % COLUMN == 0 else width
    return [pl.ds(start, step) for start in range(0, width, step)]


def back_kernel(half, capacity, turn, me_ref, saved_ref, w_ref, *refs):
    outs, product = refs[:half], refs[half]
    run = half * capacity
    saved = jnp.concatenate([saved_ref[m, 0] for m in range(MICRO)], axis=0)
    here = jnp.bitwise_xor(lax.rem(me_ref[0], half), turn)
    for columns in chunks(w_ref.shape[1]):
        product[:, columns] = jnp.dot(saved, w_ref[:, columns], preferred_element_type=F32)
    for j in range(half):
        slots = [pl.multiple_of(m * run + jnp.bitwise_xor(here, j) * capacity, 8) for m in range(MICRO)]
        rows = jnp.concatenate([product[pl.ds(slot, capacity), :] for slot in slots], axis=0)
        outs[j][...] = rows.astype(BF16)


def back(me, saved, weight, half, capacity, turn):
    hidden_width, width = weight.shape
    run, rows = half * capacity, MICRO * capacity
    return pl.pallas_call(
        functools.partial(back_kernel, half, capacity, turn),
        grid_spec=pltpu.PrefetchScalarGridSpec(
            num_scalar_prefetch=1,
            grid=(1,),
            in_specs=[
                pl.BlockSpec((MICRO, 1, run, hidden_width), lambda i, me: (0, 1 - me[0] // half, 0, 0)),
                pl.BlockSpec(memory_space=pltpu.VMEM),
            ],
            out_specs=[pl.BlockSpec((rows, width), lambda i, me: (0, 0))] * half,
            scratch_shapes=[pltpu.VMEM((MICRO * run, width), F32)],
        ),
        out_shape=[jax.ShapeDtypeStruct((rows, width), BF16)] * half,
        compiler_params=pltpu.CompilerParams(vmem_limit_bytes=VMEM_LIMIT),
        name="back",
    )(me, saved, weight)


def turn_kernel(half, capacity, me_ref, w_ref, info_ref, router_ref, after_ref, out_ref, scale_ref, rank_ref, table_ref):
    del after_ref
    router = router_ref[...].astype(F32)
    router = jnp.concatenate([router, router, router, jnp.zeros((LANES - 24, router.shape[1]), F32)], axis=0)
    table_ref[...] = router.astype(BF16)
    for columns in chunks(w_ref.shape[1]):
        out_ref[columns, :] = w_ref[:, columns].T
    rank, weight = ranks(info_ref[...], jnp.bitwise_xor(me_ref[0], iota((8, LANES), 0)))
    rank_ref[...] = rank
    for j in range(half):
        for m in range(MICRO):
            _, scale = pick(rank[j : j + 1, :], weight[j : j + 1, :], m, capacity)
            scale_ref[j, m * capacity : (m + 1) * capacity, :] = scale


def turned(me, weight, info, router, after, half, capacity):
    vmem = pl.BlockSpec(memory_space=pltpu.VMEM)
    return pl.pallas_call(
        functools.partial(turn_kernel, half, capacity),
        out_shape=[
            jax.ShapeDtypeStruct(weight.shape[::-1], BF16),
            jax.ShapeDtypeStruct((half, MICRO * capacity, LANES), F32),
            jax.ShapeDtypeStruct((8, LANES), jnp.int32),
            jax.ShapeDtypeStruct((LANES, router.shape[1]), BF16),
        ],
        in_specs=[pl.BlockSpec(memory_space=pltpu.SMEM), vmem, vmem, vmem, pl.BlockSpec(memory_space=pl.ANY)],
        out_specs=[vmem] * 4,
        compiler_params=pltpu.CompilerParams(vmem_limit_bytes=VMEM_LIMIT),
        name="turned",
    )(me, weight, info, router, after)


def far_grad_kernel(half, capacity, *refs):
    blocks, (grad_ref,) = refs[:half], refs[2 * half :]
    backs = [refs[half + BACK_ORDER.index(j)] for j in range(half)]
    width = blocks[0].shape[1] - LANES
    rows = MICRO * capacity
    where = iota((rows, LANES), 1)
    table = jnp.zeros((rows, LANES), F32)
    for j in range(half):
        total = jnp.zeros((rows, LANES), F32)
        for lane in range(0, width, LANES):
            sent = blocks[j][:, lane : lane + LANES].astype(F32)
            total = total + sent * backs[j][:, lane : lane + LANES].astype(F32)
        for i, part in enumerate(split(jnp.sum(total, axis=1, keepdims=True))):
            table = jnp.where(where == 3 * j + i, part, table)
    grad_ref[...] = table.astype(BF16)


def far_grad(blocks, backs, half, capacity):
    vmem = pl.BlockSpec(memory_space=pltpu.VMEM)
    return pl.pallas_call(
        functools.partial(far_grad_kernel, half, capacity),
        out_shape=jax.ShapeDtypeStruct((MICRO * capacity, LANES), BF16),
        in_specs=[vmem] * (2 * half),
        out_specs=vmem,
        compiler_params=pltpu.CompilerParams(vmem_limit_bytes=VMEM_LIMIT),
        name="far_grad",
    )(*blocks, *[backs[j] for j in BACK_ORDER])


def own_kernel(half, capacity, me_ref, *refs):
    blocks, refs = [refs[OWN_ORDER.index(j)] for j in range(half)], refs[half:]
    w_ref, saved_ref, scale_ref, product, grads = refs[0], refs[1], refs[2], refs[3], refs[4 : 4 + half]
    lhs, partial = refs[4 + half :]
    hidden_width = w_ref.shape[1]
    run, size = half * capacity, MICRO * capacity
    me = me_ref[0]
    here, side = lax.rem(me, half), me // half
    places = []
    for j in range(half):
        lhs[j * size : (j + 1) * size, :] = blocks[j][...]
        for m in range(MICRO):
            slot = pl.multiple_of(m * run + jnp.bitwise_xor(here, j) * capacity, 8)
            places.append((j, m * capacity, slot))
    for columns in chunks(hidden_width):
        got = jnp.dot(lhs[...], w_ref[:, columns], preferred_element_type=F32)
        for j, row, slot in places:
            product[pl.ds(slot, capacity), columns] = got[j * size + row : j * size + row + capacity, :]
    for m in range(MICRO):
        total = jnp.zeros((run, LANES), F32)
        for lane in range(0, hidden_width, LANES):
            held = saved_ref[m, side, :, lane : lane + LANES].astype(F32)
            total = total + product[m * run : (m + 1) * run, lane : lane + LANES] * held
        partial[m * run : (m + 1) * run, :] = total
    lane = iota((size, LANES), 1)
    for j in range(half):
        slots = [slot for which, _, slot in places if which == j]
        sums = jnp.concatenate([partial[pl.ds(slot, capacity), :] for slot in slots], axis=0)
        table = scale_ref[j]
        for i, part in enumerate(split(jnp.sum(sums, axis=1, keepdims=True))):
            table = jnp.where(lane == i, part, table)
        grads[j][...] = table.astype(BF16)


def own_expert(me, blocks, weight, saved, scales, half, capacity):
    width, hidden_width = weight.shape
    rows = MICRO * capacity
    vmem = pl.BlockSpec(memory_space=pltpu.VMEM)
    return pl.pallas_call(
        functools.partial(own_kernel, half, capacity),
        out_shape=[jax.ShapeDtypeStruct((half * rows, hidden_width), F32)]
        + [jax.ShapeDtypeStruct((rows, LANES), BF16)] * half,
        in_specs=[pl.BlockSpec(memory_space=pltpu.SMEM)] + [vmem] * (half + 3),
        out_specs=[vmem] * (1 + half),
        scratch_shapes=[pltpu.VMEM((half * rows, width), BF16), pltpu.VMEM((half * rows, LANES), F32)],
        compiler_params=pltpu.CompilerParams(vmem_limit_bytes=VMEM_LIMIT),
        name="own_expert",
    )(me, *[blocks[j] for j in OWN_ORDER], weight, saved, scales)


def router_rows(half, capacity, turn, me, info_ref, own, far_ref, rank, table_ref):
    info = info_ref[...]
    relative = jnp.bitwise_xor(me, iota((8, LANES), 0))
    slot = iota((capacity, LANES), 0)
    token = iota((capacity, LANES), 1)
    far = far_ref[...].astype(F32)
    rows = []
    for j in range(2 * half):
        if j < half:
            table, lane = own[j], 0
        else:
            table, lane = far, 3 * ((j - half) ^ turn)
        column = table[:, lane : lane + 1] + table[:, lane + 1 : lane + 2] + table[:, lane + 2 : lane + 3]
        here = jnp.where(token // MB_TOK == 0, column[0:capacity], column[capacity : 2 * capacity])
        rows.append(jnp.sum(jnp.where(slot == rank[j : j + 1, :], here, 0.0), axis=0, keepdims=True))
    grads = jnp.concatenate(rows, axis=0)
    first, second = info[0:1, :].astype(jnp.int32), info[1:2, :].astype(jnp.int32)
    w_first, w_second = info[2:3, :], info[3:4, :]
    g_first = jnp.sum(jnp.where(relative == first, grads, 0.0), axis=0, keepdims=True)
    g_second = jnp.sum(jnp.where(relative == second, grads, 0.0), axis=0, keepdims=True)
    mean = w_first * g_first + w_second * g_second
    expert_rows = iota((8, LANES), 0)
    logit = jnp.where(expert_rows == first, w_first * (g_first - mean), 0.0)
    logit = logit + jnp.where(expert_rows == second, w_second * (g_second - mean), 0.0)
    parts = jnp.concatenate([*split(logit), jnp.zeros((LANES - 24, LANES), F32)], axis=0).T
    return jnp.dot(parts.astype(BF16), table_ref[...], preferred_element_type=F32).astype(BF16)


def last_kernel(half, capacity, turn, me_ref, *refs):
    blocks, refs = [refs[FAR_ORDER.index(j)] for j in range(half)], refs[half:]
    w_ref, own_ref, info_ref, far_ref, rank_ref, table_ref, d_ref, out_ref = refs[:8]
    lhs, product, scale, rows, hidden, row_sem, hidden_sem = refs[8:]
    width, hidden_width = w_ref.shape
    run, size = half * capacity, MICRO * capacity
    me = me_ref[0]
    side = me // half
    tails = [block[:, width:].astype(F32) for block in blocks]
    copies = []
    here = lax.rem(me, half)

    def spread_scale(lane_of, slots):
        for j in range(half):
            for m in range(MICRO):
                tail = tails[j][m * capacity : (m + 1) * capacity]
                column = jnp.broadcast_to(tail[:, lane_of : lane_of + 1], tail.shape)
                scale[pl.ds(slots[j][m], capacity), :] = column

    def scaled(far, source, columns):
        for m in range(MICRO):
            at = slice(m * run, (m + 1) * run)
            for lane in range(columns.start, columns.start + columns.size, LANES):
                lanes = slice(lane, lane + LANES)
                hidden[far, m, :, lanes] = (scale[at, :] * source[at, lanes]).astype(BF16)
            to = d_ref.at[m, 1 - side if far else side, :, columns]
            part = columns.start // columns.size
            copies.append(pltpu.make_async_copy(hidden.at[far, m, :, columns], to, hidden_sem.at[far, m, part]))
            copies[-1].start()

    def slots_of(first):
        return [
            [pl.multiple_of(m * run + jnp.bitwise_xor(first, j) * capacity, 8) for m in range(MICRO)] for j in range(half)
        ]

    spread_scale(SCALE - 1, slots_of(here))
    scaled(0, own_ref, pl.ds(0, hidden_width))
    rows[...] = router_rows(half, capacity, turn, me, info_ref, tails, far_ref, rank_ref[...], table_ref)
    cut = out_ref.shape[1] // 2
    for i in range(2):
        columns = pl.ds(i * cut, cut)
        copies.append(pltpu.make_async_copy(rows.at[:, columns], out_ref.at[:, columns], row_sem.at[i]))
        copies[-1].start()
    far_slots = slots_of(jnp.bitwise_xor(here, turn))
    spread_scale(SCALE, far_slots)
    for j in range(half):
        lhs[j * size : (j + 1) * size, :] = blocks[j][:, 0:width]
    for columns in chunks(hidden_width):
        got = jnp.dot(lhs[...], w_ref[:, columns], preferred_element_type=F32)
        for j in range(half):
            for m in range(MICRO):
                begin = j * size + m * capacity
                product[pl.ds(far_slots[j][m], capacity), columns] = got[begin : begin + capacity, :]
        scaled(1, product, columns)
    for copy in copies:
        copy.wait()


def last(me, blocks, weight, own, info, far, rank, table, saved, tokens, half, capacity, turn):
    width, hidden_width = weight.shape
    run = half * capacity
    vmem, anywhere = pl.BlockSpec(memory_space=pltpu.VMEM), pl.BlockSpec(memory_space=pl.ANY)
    return pl.pallas_call(
        functools.partial(last_kernel, half, capacity, turn),
        out_shape=[jax.ShapeDtypeStruct(saved.shape, BF16), jax.ShapeDtypeStruct(tokens.shape, BF16)],
        in_specs=[pl.BlockSpec(memory_space=pltpu.SMEM)] + [vmem] * (half + 6),
        out_specs=[anywhere, anywhere],
        scratch_shapes=[
            pltpu.VMEM((MICRO * run, width), BF16),
            pltpu.VMEM((MICRO * run, hidden_width), F32),
            pltpu.VMEM((MICRO * run, LANES), F32),
            pltpu.VMEM(tokens.shape, BF16),
            pltpu.VMEM((2, MICRO, run, hidden_width), BF16),
            pltpu.SemaphoreType.DMA((2,)),
            pltpu.SemaphoreType.DMA((2, MICRO, len(chunks(hidden_width)))),
        ],
        compiler_params=pltpu.CompilerParams(vmem_limit_bytes=VMEM_LIMIT),
        name="last",
    )(me, *[blocks[j] for j in FAR_ORDER], weight, own, info, far, rank, table)


def route(block, flip, back):
    sections, peers = lax.axis_size("pipe"), lax.axis_size("expert")
    pairs = [
        (p * peers + e, ((p - back) % sections) * peers + (e ^ flip)) for p in range(sections) for e in range(peers)
    ]
    return lax.ppermute(block, ("pipe", "expert"), pairs)


def by_halves(grad_sent, routes, router_probs, saved_hidden, w_down, w_router):
    peers = lax.axis_size("expert")
    half, turn = peers // 2, 2
    slots, hidden_width = saved_hidden.shape[1:]
    capacity = slots // (MICRO * peers)
    me = lax.axis_index("expert").astype(jnp.int32).reshape(1)
    tokens, weight = grad_sent[0], w_down[0]
    saved = saved_hidden.reshape(MICRO, 2, half * capacity, hidden_width)
    vmem = pl.BlockSpec(memory_space=pltpu.VMEM)

    def spread(blocks):
        return [blocks[0]] + [route(blocks[j], j, 0) for j in range(1, half)]

    info = pl.pallas_call(
        info_kernel,
        out_shape=jax.ShapeDtypeStruct((8, LANES), F32),
        in_specs=[vmem, vmem],
        out_specs=vmem,
        name="info",
    )(routes[0].T, router_probs[0].T)
    next_info = route(info, 0, -1)
    far_info = route(info, half + turn, 0)
    far_tokens = route(tokens, half + turn, 1)
    packed = pack(me, next_info, tokens, half, capacity, "pack_own")
    weight_t, scales, rank, table = turned(me, weight, info, w_router.T, packed[0], half, capacity)
    saved, packed = lax.optimization_barrier((saved, packed))
    backs = back(me, saved, weight, half, capacity, turn)
    own = [route(packed[j], j, 1) for j in range(half)]
    backs = spread(backs)
    own_product, *own_grads = own_expert(me, own, weight_t, saved, scales, half, capacity)
    far = pack(me, far_info, far_tokens, half, capacity, "pack_far", own_grads)
    far_grads = route(far_grad(far, backs, half, capacity), half + turn, 0)
    far = spread(far)
    d_hidden, grad_in = last(
        me, far, weight_t, own_product, info, far_grads, rank, table, saved, tokens, half, capacity, turn
    )
    return d_hidden.reshape(saved_hidden.shape), grad_in[None]


def from_behind(block, axis, distance):
    devices = range(lax.axis_size(axis))
    route = [((i - distance) % len(devices), i) for i in devices]
    return lax.ppermute(block, axis, route)


def route_slots(route_rows, peer_count, capacity):
    onehot = (route_rows[..., None] == jnp.arange(peer_count, dtype=jnp.int32)).astype(jnp.int32)
    rank_of = jnp.sum((jnp.cumsum(onehot, axis=1) - onehot) * onehot, axis=2)
    return route_rows * capacity + rank_of


def by_slots(grad_sent, routes, router_probs, saved_hidden, w_down, w_router):
    peer_count = lax.axis_size("expert")
    slot_count = saved_hidden.shape[1]
    capacity = slot_count // (MICRO * peer_count)
    send_width = peer_count * capacity
    model_width = grad_sent.shape[2]
    hidden_width = saved_hidden.shape[2]
    tokens = routes.shape[1]
    incoming = from_behind(grad_sent, "pipe", -1)[0]
    route_rows = routes[0].reshape(MICRO, MB_TOK * TOP)
    position = route_slots(route_rows, peer_count, capacity)
    chosen = jnp.take_along_axis(router_probs[0], routes[0], axis=1)
    weights = chosen / jnp.sum(chosen, axis=1, keepdims=True)
    rounded = weights.astype(jnp.bfloat16)
    micro_index = jnp.arange(MICRO, dtype=jnp.int32)[:, None]
    token_index = jnp.broadcast_to(
        jnp.arange(MB_TOK * TOP, dtype=jnp.int32)[None, :] // TOP, (MICRO, MB_TOK * TOP)
    )
    slot_token = (
        jnp.zeros((MICRO, send_width), jnp.int32).at[micro_index, position].set(token_index)
    )
    slot_used = jnp.zeros((MICRO, send_width), jnp.bool_).at[micro_index, position].set(True)
    send_scale = (
        jnp.zeros((MICRO, send_width), jnp.bfloat16)
        .at[micro_index, position]
        .set(rounded.reshape(MICRO, MB_TOK * TOP))
    )
    micro_grad = incoming.reshape(MICRO, MB_TOK, model_width)
    picked = jnp.take_along_axis(micro_grad, slot_token[..., None], axis=1)
    send_rows = jnp.where(slot_used[..., None], picked, jnp.zeros((), jnp.bfloat16))
    hidden = saved_hidden[0].reshape(MICRO, send_width, hidden_width)
    weight = w_down[0]
    arrived, arrived_scale = (
        lax.all_to_all(send_rows, "expert", split_axis=1, concat_axis=1, tiled=True),
        lax.all_to_all(send_scale, "expert", split_axis=1, concat_axis=1, tiled=True),
    )
    flat_rows = arrived.reshape(-1, model_width)
    flat_saved = hidden.reshape(flat_rows.shape[0], hidden_width)
    grad_hidden = lax.dot_general(
        flat_rows, weight, (((1,), (1,)), ((), ())), preferred_element_type=jnp.float32
    )
    route_grad = jnp.sum(grad_hidden * flat_saved.astype(jnp.float32), axis=1)
    scaled = (arrived_scale.reshape(-1, 1).astype(jnp.float32) * grad_hidden).astype(jnp.bfloat16)
    d_hidden, route_grad = (scaled, route_grad.reshape(arrived_scale.shape))
    returned = lax.all_to_all(route_grad, "expert", split_axis=1, concat_axis=1, tiled=True)
    slot_grad = jnp.take_along_axis(returned, position, axis=1).reshape(tokens, TOP)
    centred = slot_grad - jnp.sum(weights * slot_grad, axis=1, keepdims=True)
    logit_part = weights * centred
    onehot_tok = (routes[0][..., None] == jnp.arange(peer_count, dtype=jnp.int32)).astype(
        jnp.float32
    )
    logit_grad = jnp.sum(logit_part[..., None] * onehot_tok, axis=1)
    grad_in = jnp.dot(logit_grad, w_router.astype(jnp.float32).T, precision=lax.Precision.HIGHEST)
    return (d_hidden.reshape(1, slot_count, hidden_width), grad_in.astype(jnp.bfloat16)[None])


def on_device(*blocks):
    peers, slots = lax.axis_size("expert"), blocks[3].shape[1]
    capacity = slots // (MICRO * peers)
    if peers == 8 and capacity % 8 == 0 and capacity <= MB_TOK // 2:
        return by_halves(*blocks)
    return by_slots(*blocks)


def solution(mesh):
    placed = (
        P("pipe", "expert", None),
        P("pipe", "expert", None),
        P("pipe", "expert", None),
        P("pipe", "expert", None),
        P("expert", None, None),
        P(),
    )
    return jax.shard_map(
        on_device,
        mesh=mesh,
        in_specs=placed,
        out_specs=(P("pipe", "expert", None), P("pipe", "expert", None)),
        check_vma=False,
    )
```
